32 devices in a mesh: groups: 2 (over x), wide: 8 (over z, y), narrow: 2 (over core).
Axes of the slice: x: 2, y: 2, z: 4, core: 2. Of those that a mesh axis runs over, the one named last changes fastest.
Arguments:
- volume: bfloat16 [32, 128, 16, 32], P(None, ('groups', 'wide'), None, 'narrow'), parts along dimension 1, may hold values from -6 to 6
- cotangent: bfloat16 [32, 128, 16, 32], P(None, ('groups', 'wide'), None, 'narrow'), parts along dimension 1, may hold values from -6 to 6
- fine_weight: bfloat16 [27, 32, 32], replicated, may hold values from -0.21875 to 0.21875
- merge_weight: bfloat16 [16384, 1024], P('wide'), may hold values from -0.046875 to 0.046875
- hidden_weight: bfloat16 [27, 1024, 2048], P(None, None, 'wide'), may hold values from -0.0390625 to 0.0390625
- step_table: float32 [1000, 2048], P(None, 'wide'), may hold values from -6 to 6
- output_weight: bfloat16 [27, 2048, 1024], P(None, 'wide'), may hold values from -0.02734375 to 0.02734375
- expand_weight: bfloat16 [1024, 16384], P(None, 'wide'), may hold values from -0.1875 to 0.1875
- timestep: int32 [2], P('groups'), parts along dimension 0, may hold values from 0 to 999
Outputs:
- input_grad: bfloat16 [32, 128, 16, 32], P(None, ('groups', 'wide'), None, 'narrow'), parts along dimension 1
The draws below stay inside these ranges and needn't reach their ends.
There are 2 independent parts, one for each index of `groups`. The reference program is written for one: setup_inputs(seed, part) draws one part's arguments, and reference() takes and returns one part's arrays. A program takes and returns all parts, laid end to end along the dimension named above; an argument that names none is the same for every part. Nothing has to cross between parts.
All inputs are finite; a program needn't handle non-finite values.
Results may differ from the reference program's by a relative error of at most 0.012.
Values may be sent and summed in bfloat16 or wider, within the bound.
No kernel may reach another device: no remote copies, remote signals or barrier semaphores. Data moves between devices by JAX's collectives and lax.ppermute only.
A program may use at most 128 MiB of HBM per device.

```python
import jax
import jax.numpy as jnp

FINE_CH = 32
FEATURES = 1024
HIDDEN_SIZE = 2048
PATCH = 8
STEPS_ALL = 1000
SLAB_Y = 16
NX = 64
NZ = 32
MERGED = 16384


def block_levels(rng, dims, split, low, high):
    factor_of, own = 1.0, jax.random.fold_in(rng, 6)
    for dim, parts in split:
        heights = jnp.exp(jax.random.uniform(jax.random.fold_in(own, dim), (parts,), jnp.float32, low / len(split), high / len(split)))
        factor_of = factor_of * jnp.repeat(heights, dims[dim] // parts).reshape([-1 if axis == dim else 1 for axis in range(len(dims))])
    return factor_of


def normal_values(key, shape, deviation, reach, pieces=(), dtype=jnp.bfloat16):
    values = deviation * jax.random.normal(key, shape, jnp.float32)
    if pieces:
        values = values * block_levels(key, shape, pieces, -0.22, 0.18)
    return jnp.clip(values, -reach, reach).astype(dtype)


def setup_inputs(seed: int = 0, part: int = 0) -> dict:
    splits = jax.random.split(jax.random.key(seed), 10)
    part_keys = jax.random.split(jax.random.fold_in(splits[9], part), 10)
    volume = normal_values(part_keys[0], (FINE_CH, NX, SLAB_Y, NZ), 1.0, 6.0, ((1, 8), (3, 2)))
    cotangent = normal_values(part_keys[1], (FINE_CH, NX, SLAB_Y, NZ), 1.0, 6.0, ((1, 8), (3, 2)))
    fine_weight = normal_values(splits[2], (27, FINE_CH, FINE_CH), (27 * FINE_CH) ** -0.5, 0.21875)
    merge_weight = normal_values(splits[3], (MERGED, FEATURES), MERGED ** -0.5, 0.046875, ((0, 8),))
    hidden_weight = normal_values(splits[4], (27, FEATURES, HIDDEN_SIZE), (27 * FEATURES) ** -0.5, 0.0390625, ((2, 8),))
    step_table = normal_values(splits[5], (STEPS_ALL, HIDDEN_SIZE), 1.0, 6.0, ((1, 8),), jnp.float32)
    output_weight = normal_values(splits[6], (27, HIDDEN_SIZE, FEATURES), (27 * HIDDEN_SIZE) ** -0.5, 0.02734375, ((1, 8),))
    expand_weight = normal_values(splits[7], (FEATURES, MERGED), FEATURES ** -0.5, 0.1875, ((1, 8),))
    timestep = jax.random.randint(part_keys[8], (1,), 0, STEPS_ALL).astype(jnp.int32)
    return dict(volume=volume, cotangent=cotangent, fine_weight=fine_weight, merge_weight=merge_weight, hidden_weight=hidden_weight, step_table=step_table, output_weight=output_weight, expand_weight=expand_weight, timestep=timestep)


def tap_list(transposed):
    return [((2 - i, 2 - j, 2 - k) if transposed else (i, j, k)) for i in range(3) for j in range(3) for k in range(3)]


def conv_taps(volume, weight, transposed):
    padded = jnp.pad(volume, ((1, 1), (1, 1), (1, 1), (0, 0)))
    extent = volume.shape[:3]
    summed = jnp.zeros(extent + (weight.shape[2],), jnp.float32)
    for tap_index, (i, j, k) in enumerate(tap_list(transposed)):
        window = padded[i:i + extent[0], j:j + extent[1], k:k + extent[2]].astype(jnp.float32)
        summed = summed + jnp.einsum("xyzc,co->xyzo", window, weight[tap_index].astype(jnp.float32))
    return summed


def silu_slope(values):
    logistic = jax.nn.sigmoid(values)
    return logistic * (1.0 + values * (1.0 - logistic))


def to_cells(fine_field):
    shaped = fine_field.reshape(FINE_CH, NX // PATCH, PATCH, SLAB_Y // PATCH, PATCH, NZ // PATCH, PATCH)
    return shaped.transpose(1, 3, 5, 2, 4, 6, 0).reshape(-1, MERGED)


def from_cells(cell_rows):
    shaped = cell_rows.reshape(NX // PATCH, SLAB_Y // PATCH, NZ // PATCH, PATCH, PATCH, PATCH, FINE_CH)
    return shaped.transpose(6, 0, 3, 1, 4, 2, 5).reshape(FINE_CH, NX, SLAB_Y, NZ)


def reference(volume, cotangent, fine_weight, merge_weight, hidden_weight, step_table, output_weight, expand_weight, timestep):
    coarse_shape = (NX // PATCH, SLAB_Y // PATCH, NZ // PATCH)
    pre_act = conv_taps(volume.transpose(1, 2, 3, 0), fine_weight, False)
    activated = jax.nn.silu(pre_act).astype(jnp.bfloat16).transpose(3, 0, 1, 2)
    merged = jnp.dot(to_cells(activated), merge_weight, preferred_element_type=jnp.float32)
    coarse_in = merged.astype(jnp.bfloat16).reshape(coarse_shape + (FEATURES,))
    bias_row = step_table[timestep[0]]
    gate_pre = conv_taps(coarse_in, hidden_weight, False) + bias_row
    hidden_act = jax.nn.silu(gate_pre).astype(jnp.bfloat16)
    branch = conv_taps(hidden_act, output_weight, False).reshape(-1, FEATURES)
    residual_sum = (merged + branch).astype(jnp.bfloat16)
    expanded = jnp.dot(residual_sum, expand_weight, preferred_element_type=jnp.float32).astype(jnp.bfloat16)
    combined = activated.astype(jnp.float32) + from_cells(expanded).astype(jnp.float32)
    grad_comb = (cotangent.astype(jnp.float32) * silu_slope(combined)).astype(jnp.bfloat16)
    grad_res = jnp.dot(to_cells(grad_comb), expand_weight.T, preferred_element_type=jnp.float32)
    grad_res_b = grad_res.astype(jnp.bfloat16).reshape(coarse_shape + (FEATURES,))
    grad_hidden = conv_taps(grad_res_b, output_weight.transpose(0, 2, 1), True)
    grad_gate = (grad_hidden * silu_slope(gate_pre)).astype(jnp.bfloat16)
    grad_conv = conv_taps(grad_gate, hidden_weight.transpose(0, 2, 1), True).reshape(-1, FEATURES)
    grad_merged = (grad_res + grad_conv).astype(jnp.bfloat16)
    grad_cells = jnp.dot(grad_merged, merge_weight.T, preferred_element_type=jnp.float32).astype(jnp.bfloat16)
    grad_act = from_cells(grad_cells).astype(jnp.float32) + grad_comb.astype(jnp.float32)
    grad_pre = (grad_act * silu_slope(pre_act.transpose(3, 0, 1, 2))).astype(jnp.bfloat16)
    input_grad = conv_taps(grad_pre.transpose(1, 2, 3, 0), fine_weight.transpose(0, 2, 1), True)
    return input_grad.transpose(3, 0, 1, 2).astype(jnp.bfloat16)
```

```python
import functools

import jax
import jax.numpy as jnp
from jax import lax
from jax.experimental import pallas as pl
from jax.experimental.pallas import tpu as pltpu
from jax.sharding import PartitionSpec as P

PATCH = 8


def extended(cells, sides, width):
    for axis, dim in sides:
        count = lax.axis_size(axis)
        ends = count - 1
        head = lax.slice_in_dim(cells, 0, width, axis=dim)
        tail = lax.slice_in_dim(cells, cells.shape[dim] - width, cells.shape[dim], axis=dim)
        cells = jnp.concatenate(
            [
                lax.ppermute(tail, axis, [(i, (i + 1) % count) for i in range(ends)]),
                cells,
                lax.ppermute(head, axis, [((i + 1) % count, i) for i in range(ends)]),
            ],
            axis=dim,
        )
    return cells


def shifts(transposed):
    return [
        (2 - i, 2 - j, 2 - k) if transposed else (i, j, k)
        for i in range(3)
        for j in range(3)
        for k in range(3)
    ]


def silu_slope(values):
    logistic = jax.nn.sigmoid(values)
    return logistic * (1.0 + values * (1.0 - logistic))


def fine_conv(fine_field, weight, transposed):
    grown = extended(fine_field, (("wide", 1), ("narrow", 3)), 1)
    padded = jnp.pad(grown, ((0, 0), (0, 0), (1, 1), (0, 0)))
    kernel = weight.reshape(3, 3, 3, weight.shape[1], weight.shape[2])
    if transposed:
        kernel = kernel[::-1, ::-1, ::-1]
    result = lax.conv_general_dilated(
        padded[None],
        kernel,
        (1, 1, 1),
        "VALID",
        dimension_numbers=("NCDHW", "DHWIO", "NCDHW"),
        preferred_element_type=jnp.float32,
    )
    return result[0]


def to_patches(fine_field):
    channels = fine_field.shape[0]
    shaped = fine_field.reshape(
        channels, PATCH, fine_field.shape[2] // PATCH, PATCH, fine_field.shape[3] // PATCH, PATCH
    )
    return shaped.transpose(2, 4, 1, 3, 5, 0).reshape(-1, PATCH**3 * channels)


def send_patches(fine_field):
    return lax.all_to_all(to_patches(fine_field), "wide", split_axis=1, concat_axis=0, tiled=True)


def return_patches(patch_rows, fine_height, fine_depth, channels):
    returned = lax.all_to_all(patch_rows, "wide", split_axis=0, concat_axis=1, tiled=True)
    shaped = returned.reshape(
        fine_height // PATCH, fine_depth // PATCH, PATCH, PATCH, PATCH, channels
    )
    return shaped.transpose(5, 2, 0, 3, 1, 4).reshape(channels, PATCH, fine_height, fine_depth)


def coarse_faces(coarse_block):
    return extended(coarse_block, (("narrow", 2),), 1)


def wide_input_conv(coarse_block, weight_mat, out_count, transposed):
    grown = coarse_faces(coarse_block)
    products = jnp.einsum("xyzd,dk->xyzk", grown, weight_mat, preferred_element_type=jnp.float32)
    padded = jnp.pad(products, ((1, 1), (1, 1), (0, 0), (0, 0)))
    extent = coarse_block.shape[:3]
    summed = jnp.zeros(extent + (out_count,), jnp.float32)
    for tap_index, (a, b, c) in enumerate(shifts(transposed)):
        summed = (
            summed
            + padded[
                a : a + extent[0],
                b : b + extent[1],
                c : c + extent[2],
                tap_index * out_count : (tap_index + 1) * out_count,
            ]
        )
    return summed


def narrow_input_conv(coarse_block, weight_mat, transposed):
    grown = coarse_faces(coarse_block)
    padded = jnp.pad(grown, ((1, 1), (1, 1), (0, 0), (0, 0)))
    extent = coarse_block.shape[:3]
    columns = jnp.concatenate(
        [
            padded[a : a + extent[0], b : b + extent[1], c : c + extent[2]]
            for a, b, c in shifts(transposed)
        ],
        axis=3,
    )
    return jnp.einsum("xyzk,kd->xyzd", columns, weight_mat, preferred_element_type=jnp.float32)


BF = jnp.bfloat16
F32 = jnp.float32
LIMIT = 48 * 1024 * 1024


def nn_dot(lhs, rhs):
    return jnp.dot(lhs, rhs, preferred_element_type=F32)


def nt_dot(lhs, rhs):
    return lax.dot_general(lhs, rhs, (((1,), (1,)), ((), ())), preferred_element_type=F32)


def banded(weight):
    taps = weight.reshape(9, 3, 32, 32)
    band = jnp.concatenate([taps[:, 2], taps[:, 1], taps[:, 0]], axis=2)
    wide_band = jnp.pad(band, ((0, 0), (0, 0), (224, 224)))
    starts = [224 - 32 * (d - 1) for d in range(8)] + [288, 0]
    return jnp.concatenate([wide_band[:, :, s : s + 256] for s in starts], axis=1)


def fine_taps(planes_ref, band_ref):
    total = None
    for i in range(3):
        for j in range(3):
            lhs = planes_ref[i, j : j + 16].reshape(256, 320)
            part = nn_dot(lhs, band_ref[3 * i + j])
            total = part if total is None else total + part
    return total


def cell_rows(ref, b):
    low = ref[pl.ds(pl.multiple_of(b * 16, 16), 16), :]
    high = ref[pl.ds(pl.multiple_of(b * 16 + 128, 16), 16), :]
    return jnp.concatenate([low, high], axis=0)


def put_rows(ref, b, value):
    ref[pl.ds(pl.multiple_of(b * 16, 16), 16), :] = value[:16]
    ref[pl.ds(pl.multiple_of(b * 16 + 128, 16), 16), :] = value[16:]


def add_up(step, ref, value):
    @pl.when(step == 0)
    def _():
        ref[...] = value

    @pl.when(step > 0)
    def _():
        ref[...] += value


def merge_kernel(planes_ref, band_ref, merge_ref, pre_ref, act_ref, sum_ref, sum_b_ref):
    b = pl.program_id(0)

    @pl.when(b == 0)
    def _():
        pre = fine_taps(planes_ref, band_ref)
        pre_ref[...] = pre
        act_ref[...] = (pre * jax.nn.sigmoid(pre)).astype(BF)

    add_up(b, sum_ref, nn_dot(cell_rows(act_ref, b), merge_ref[...]))

    @pl.when(b == pl.num_programs(0) - 1)
    def _():
        sum_b_ref[...] = sum_ref[...].astype(BF)


def whole(shape):
    return pl.BlockSpec(shape, lambda *_: (0,) * len(shape))


def params():
    return pltpu.CompilerParams(vmem_limit_bytes=LIMIT)


def merge_call(planes, band, merge_weight):
    features = merge_weight.shape[1]
    return pl.pallas_call(
        merge_kernel,
        grid=(8,),
        in_specs=[
            whole(planes.shape),
            whole(band.shape),
            pl.BlockSpec((256, features), lambda b: (b, 0)),
        ],
        out_specs=[whole((256, 256)), whole((256, 256)), whole((32, features)), whole((32, features))],
        out_shape=[
            jax.ShapeDtypeStruct((256, 256), F32),
            jax.ShapeDtypeStruct((256, 256), BF),
            jax.ShapeDtypeStruct((32, features), F32),
            jax.ShapeDtypeStruct((32, features), BF),
        ],
        compiler_params=params(),
    )(planes, band, merge_weight)


def final_kernel(planes_ref, band_ref, out_ref):
    out_ref[...] = fine_taps(planes_ref, band_ref).astype(BF)


def final_call(planes, band):
    return pl.pallas_call(
        final_kernel,
        out_shape=jax.ShapeDtypeStruct((256, 256), BF),
        compiler_params=params(),
    )(planes, band)


def put_columns(cols_ref, cells):
    row = lax.broadcasted_iota(jnp.int32, (64, 1), 0)
    in_half, along_x, half = row & 1, (row >> 1) & 7, row >> 5
    zero = jnp.zeros_like(cells)
    below = jnp.where(
        in_half == 1,
        pltpu.roll(cells, 1, 0),
        jnp.where(half == 1, pltpu.roll(cells, 31, 0), zero),
    )
    above = jnp.where(
        in_half == 0,
        pltpu.roll(cells, 63, 0),
        jnp.where(half == 0, pltpu.roll(cells, 33, 0), zero),
    )
    none = jnp.zeros((16, cells.shape[1]), BF)
    for k, along_z in enumerate((below, cells, above)):
        before = jnp.where(along_x > 0, pltpu.roll(along_z, 2, 0), zero)
        after = jnp.where(along_x < 7, pltpu.roll(along_z, 62, 0), zero)
        for i, moved in enumerate((before, along_z, after)):
            rows = moved.astype(BF)
            blocks = [rows[16 * q : 16 * q + 16] for q in range(4)]
            cols_ref[9 * i + k] = jnp.concatenate([none, blocks[0], none, blocks[2]], axis=0)
            cols_ref[9 * i + 3 + k] = rows
            cols_ref[9 * i + 6 + k] = jnp.concatenate([blocks[1], none, blocks[3], none], axis=0)


def conv_steps(weight_ref, sum_ref, cols_ref, flipped, dot):
    step = pl.program_id(0)
    taps = weight_ref.shape[0]
    total = None
    for q in range(taps):
        t = step * taps + q
        part = dot(cols_ref[26 - t if flipped else t], weight_ref[q])
        total = part if total is None else total + part
    add_up(step, sum_ref, total)


def both_halves(n_ref, mine_ref, got_ref):
    mine, got = mine_ref[...].astype(F32), got_ref[...].astype(F32)
    first = n_ref[0] == 0
    return jnp.concatenate([jnp.where(first, mine, got), jnp.where(first, got, mine)], axis=0)


def outer_kernel(n_ref, mine_ref, got_ref, weight_ref, sum_ref, cols_ref, *, flipped, dot):
    @pl.when(pl.program_id(0) == 0)
    def _():
        put_columns(cols_ref, both_halves(n_ref, mine_ref, got_ref))

    conv_steps(weight_ref, sum_ref, cols_ref, flipped, dot)


def inner_forward_kernel(
    n_ref, mine_ref, got_ref, bias_ref, weight_ref, gate_ref, sum_ref, sum_b_ref, cols_ref
):
    @pl.when(pl.program_id(0) == 0)
    def _():
        gate = mine_ref[...] + got_ref[...] + bias_ref[...]
        gate_ref[...] = gate
        put_columns(cols_ref, gate * jax.nn.sigmoid(gate))

    conv_steps(weight_ref, sum_ref, cols_ref, False, nn_dot)

    @pl.when(pl.program_id(0) == pl.num_programs(0) - 1)
    def _():
        sum_b_ref[...] = sum_ref[...].astype(BF)


def inner_backward_kernel(
    n_ref, mine_ref, got_ref, gate_ref, weight_ref, sum_ref, sum_b_ref, cols_ref
):
    @pl.when(pl.program_id(0) == 0)
    def _():
        grad = (mine_ref[...] + got_ref[...]) * silu_slope(gate_ref[...])
        put_columns(cols_ref, grad)

    conv_steps(weight_ref, sum_ref, cols_ref, True, nt_dot)

    @pl.when(pl.program_id(0) == pl.num_programs(0) - 1)
    def _():
        sum_b_ref[...] = sum_ref[...].astype(BF)


def conv_call(kernel, n, small, weight, block, place, depth, outs):
    taps = block[0]
    return pl.pallas_call(
        kernel,
        grid_spec=pltpu.PrefetchScalarGridSpec(
            num_scalar_prefetch=1,
            grid=(27 // taps,),
            in_specs=[whole(a.shape) for a in small] + [pl.BlockSpec(block, place)],
            out_specs=[whole(o.shape) for o in outs],
            scratch_shapes=[pltpu.VMEM((27, 64, depth), BF)],
        ),
        out_shape=outs,
        compiler_params=params(),
    )(n, *small, weight)


def expand_kernel(
    n_ref, merged_ref, mine_ref, got_ref, act_ref, cot_ref, expand_ref, grad_ref, sum_ref, sum_b_ref, res_ref
):
    b = pl.program_id(0)

    @pl.when(b == 0)
    def _():
        mine, got = mine_ref[...].astype(F32), got_ref[...].astype(F32)
        first = n_ref[0] == 0
        branch = jnp.concatenate([jnp.where(first, mine, got), jnp.where(first, got, mine)], axis=1)
        res_ref[...] = (merged_ref[...] + branch).astype(BF)

    expanded = nn_dot(res_ref[...], expand_ref[...]).astype(BF)
    combined = cell_rows(act_ref, b).astype(F32) + expanded.astype(F32)
    grad = (cell_rows(cot_ref, b).astype(F32) * silu_slope(combined)).astype(BF)
    put_rows(grad_ref, b, grad)
    add_up(b, sum_ref, nt_dot(grad, expand_ref[...]))

    @pl.when(b == pl.num_programs(0) - 1)
    def _():
        sum_b_ref[...] = sum_ref[...].astype(BF)


def expand_call(n, merged, mine, got, act, cot, expand_weight):
    features = expand_weight.shape[0]
    small = (merged, mine, got, act, cot)
    outs = [
        jax.ShapeDtypeStruct((256, 256), BF),
        jax.ShapeDtypeStruct((32, features), F32),
        jax.ShapeDtypeStruct((32, features), BF),
    ]
    return pl.pallas_call(
        expand_kernel,
        grid_spec=pltpu.PrefetchScalarGridSpec(
            num_scalar_prefetch=1,
            grid=(8,),
            in_specs=[whole(a.shape) for a in small]
            + [pl.BlockSpec((features, 256), lambda b, n: (0, b))],
            out_specs=[whole(o.shape) for o in outs],
            scratch_shapes=[pltpu.VMEM((32, features), BF)],
        ),
        out_shape=outs,
        compiler_params=params(),
    )(n, *small, expand_weight)


def grad_kernel(n_ref, res_ref, mine_ref, got_ref, comb_ref, pre_ref, merge_ref, out_ref, sum_ref):
    b = pl.program_id(0)

    @pl.when(b == 0)
    def _():
        mine, got = mine_ref[...].astype(F32), got_ref[...].astype(F32)
        first = n_ref[0] == 0
        conv = jnp.concatenate([jnp.where(first, mine, got), jnp.where(first, got, mine)], axis=1)
        sum_ref[...] = (res_ref[...] + conv).astype(BF)

    cells = nt_dot(sum_ref[...], merge_ref[...]).astype(BF)
    grad = cells.astype(F32) + cell_rows(comb_ref, b).astype(F32)
    put_rows(out_ref, b, (grad * silu_slope(cell_rows(pre_ref, b))).astype(BF))


def grad_call(n, grad_res, mine, got, grad_comb, pre_act, merge_weight):
    features = merge_weight.shape[1]
    small = (grad_res, mine, got, grad_comb, pre_act)
    return pl.pallas_call(
        grad_kernel,
        grid_spec=pltpu.PrefetchScalarGridSpec(
            num_scalar_prefetch=1,
            grid=(8,),
            in_specs=[whole(a.shape) for a in small]
            + [pl.BlockSpec((256, features), lambda b, n: (b, 0))],
            out_specs=whole((256, 256)),
            scratch_shapes=[pltpu.VMEM((32, features), BF)],
        ),
        out_shape=jax.ShapeDtypeStruct((256, 256), BF),
        compiler_params=params(),
    )(n, *small, merge_weight)


def swap_narrow(value):
    return lax.ppermute(value, "narrow", [(0, 1), (1, 0)])


def summed_wide(part, part_b):
    def partner(value, mask):
        return lax.ppermute(value, "wide", [(i, i ^ mask) for i in range(8)])

    pair = part + partner(part_b, 1).astype(F32)
    pair_b = pair.astype(BF)
    others = [partner(pair_b, mask) for mask in (2, 4, 6)]
    return pair + others[0].astype(F32) + others[1].astype(F32) + others[2].astype(F32)


def to_feature_halves(n, cells):
    half = cells.shape[1] // 2
    low, high = cells[:, :half], cells[:, half:]
    return jnp.where(n == 0, low, high), swap_narrow(jnp.where(n == 0, high, low))


def to_cell_halves(n, rows):
    half = rows.shape[0] // 2
    low, high = rows[:half], rows[half:]
    return jnp.where(n == 0, low, high), swap_narrow(jnp.where(n == 0, high, low).astype(BF))


def with_edges(n, planes):
    low, high = planes[..., 0, :32], planes[..., 1, 224:]
    got = swap_narrow(jnp.where(n == 0, high, low))
    none = jnp.zeros_like(got)
    before = jnp.stack([jnp.where(n == 0, none, got), planes[..., 0, 224:]], axis=3)
    after = jnp.stack([planes[..., 1, :32], jnp.where(n == 0, got, none)], axis=3)
    rows = jnp.concatenate([planes, before, after], axis=4).reshape(3, 16, 16, 320)
    return jnp.pad(rows, ((0, 0), (1, 1), (0, 0), (0, 0)))


def along_x(planes, step):
    none = jnp.zeros_like(planes[:, :1])
    if step > 0:
        return jnp.concatenate([none, planes[:, :-1]], axis=1)
    return jnp.concatenate([planes[:, 1:], none], axis=1)


def eight_shards(
    volume,
    cotangent,
    fine_weight,
    merge_weight,
    hidden_weight,
    step_table,
    output_weight,
    expand_weight,
    timestep,
):
    features = merge_weight.shape[1]
    hidden = hidden_weight.shape[2]
    half = features // 2
    w, n = lax.axis_index("wide"), lax.axis_index("narrow")
    n_arr = n.astype(jnp.int32).reshape(1)

    def row_form(fine_field):
        return fine_field.transpose(1, 2, 3, 0).reshape(8, 16, 2, 256)

    field = row_form(volume)
    outgoing = jnp.stack(
        [jnp.roll(field, 1, 0), field, jnp.roll(field, -1, 0), row_form(cotangent)], axis=1
    )
    arrived = lax.all_to_all(
        outgoing.reshape(8, 128, 256), "wide", split_axis=0, concat_axis=0, tiled=True
    )
    planes = arrived.reshape(8, 4, 16, 2, 256).transpose(1, 2, 0, 3, 4)
    planes_in = jnp.stack(
        [
            jnp.where(w == 0, along_x(planes[0], 1), planes[0]),
            planes[1],
            jnp.where(w == 7, along_x(planes[2], -1), planes[2]),
        ]
    )
    cot = planes[3].reshape(256, 256)
    pre_act, act, merged_part, merged_part_b = merge_call(
        with_edges(n, planes_in), banded(fine_weight), merge_weight
    )
    merged = summed_wide(merged_part, merged_part_b)
    mine, got = to_feature_halves(n, merged.astype(BF))

    gate_shape = jax.ShapeDtypeStruct((64, hidden), F32)
    sum_shapes = [jax.ShapeDtypeStruct((64, half), F32), jax.ShapeDtypeStruct((64, half), BF)]
    hidden_block = ((3, half, hidden), lambda s, n: (s, n[0], 0))
    output_block = ((3, hidden, half), lambda s, n: (s, 0, n[0]))

    (gate_part,) = conv_call(
        functools.partial(outer_kernel, flipped=False, dot=nn_dot),
        n_arr, (mine, got), hidden_weight, *hidden_block, half, [gate_shape],
    )
    bias = lax.dynamic_slice_in_dim(step_table, timestep[0], 1, axis=0)
    gate_pre, branch_part, branch_part_b = conv_call(
        inner_forward_kernel,
        n_arr, (gate_part, swap_narrow(gate_part), bias), output_weight, *output_block, hidden,
        [gate_shape] + sum_shapes,
    )
    branch = summed_wide(branch_part, branch_part_b)
    mine, got = to_cell_halves(n, branch)
    grad_comb, res_part, res_part_b = expand_call(n_arr, merged, mine, got, act, cot, expand_weight)
    grad_res = summed_wide(res_part, res_part_b)
    mine, got = to_feature_halves(n, grad_res.astype(BF))
    (hidden_part,) = conv_call(
        functools.partial(outer_kernel, flipped=True, dot=nt_dot),
        n_arr, (mine, got), output_weight, *output_block, half, [gate_shape],
    )
    conv_part, conv_part_b = conv_call(
        inner_backward_kernel,
        n_arr, (hidden_part, swap_narrow(hidden_part), gate_pre), hidden_weight, *hidden_block, hidden,
        sum_shapes,
    )
    grad_conv = summed_wide(conv_part, conv_part_b)
    mine, got = to_cell_halves(n, grad_conv)
    grad_pre = grad_call(n_arr, grad_res, mine, got, grad_comb, pre_act, merge_weight)

    plane = grad_pre.reshape(16, 8, 2, 256)
    none = jnp.zeros_like(plane)
    beside = jnp.where(
        w == 0, along_x(plane, -1), jnp.where(w == 7, along_x(plane, 1), none)
    )
    leaving = jnp.stack([plane, beside]).transpose(2, 0, 1, 3, 4).reshape(8, 64, 256)
    returned = lax.all_to_all(leaving, "wide", split_axis=0, concat_axis=0, tiled=True)
    returned = returned.reshape(8, 2, 16, 2, 256)
    grown = jnp.concatenate([returned[7:, 1], returned[:, 0], returned[:1, 1]], axis=0)
    windows = jnp.stack([grown[i : i + 8].transpose(1, 0, 2, 3) for i in range(3)])
    back = fine_weight[::-1].transpose(0, 2, 1)
    result = final_call(with_edges(n, windows), banded(back))
    return result.reshape(16, 8, 2, 8, 32).transpose(4, 1, 0, 2, 3).reshape(32, 8, 16, 16)


def shards(
    volume,
    cotangent,
    fine_weight,
    merge_weight,
    hidden_weight,
    step_table,
    output_weight,
    expand_weight,
    timestep,
):
    channels = volume.shape[0]
    fine_height = volume.shape[2]
    fine_depth = volume.shape[3]
    wide_count = lax.axis_size("wide")
    features = merge_weight.shape[1]
    hidden_local = hidden_weight.shape[2]
    coarse_grid = (wide_count, fine_height // PATCH, fine_depth // PATCH)
    hidden_mat = hidden_weight.transpose(1, 0, 2).reshape(features, 27 * hidden_local)
    output_mat = output_weight.reshape(27 * hidden_local, features)
    output_back = output_weight.transpose(2, 0, 1).reshape(features, 27 * hidden_local)
    hidden_back = hidden_weight.transpose(0, 2, 1).reshape(27 * hidden_local, features)

    def total_rows(partial_value):
        return lax.psum(partial_value, "wide")

    pre_act = fine_conv(volume, fine_weight, False)
    activated = jax.nn.silu(pre_act).astype(jnp.bfloat16)
    received = send_patches(activated)
    merged = total_rows(jnp.dot(received, merge_weight, preferred_element_type=jnp.float32))
    coarse_in = merged.astype(jnp.bfloat16).reshape(coarse_grid + (features,))
    bias_row = step_table[timestep[0]]
    gate_pre = wide_input_conv(coarse_in, hidden_mat, hidden_local, False) + bias_row
    hidden_act = jax.nn.silu(gate_pre).astype(jnp.bfloat16)
    branch = total_rows(narrow_input_conv(hidden_act, output_mat, False).reshape(-1, features))
    residual_sum = (merged + branch).astype(jnp.bfloat16)
    expanded = jnp.dot(residual_sum, expand_weight, preferred_element_type=jnp.float32).astype(
        jnp.bfloat16
    )
    expanded_field = return_patches(expanded, fine_height, fine_depth, channels)
    combined = activated.astype(jnp.float32) + expanded_field.astype(jnp.float32)
    grad_comb = (cotangent.astype(jnp.float32) * silu_slope(combined)).astype(jnp.bfloat16)
    grad_res = total_rows(
        jnp.einsum(
            "nk,dk->nd", send_patches(grad_comb), expand_weight, preferred_element_type=jnp.float32
        )
    )
    grad_res_b = grad_res.astype(jnp.bfloat16).reshape(coarse_grid + (features,))
    grad_hidden = wide_input_conv(grad_res_b, output_back, hidden_local, True)
    grad_gate = (grad_hidden * silu_slope(gate_pre)).astype(jnp.bfloat16)
    grad_conv = total_rows(narrow_input_conv(grad_gate, hidden_back, True).reshape(-1, features))
    grad_merged = (grad_res + grad_conv).astype(jnp.bfloat16)
    grad_cells = jnp.einsum(
        "nd,kd->nk", grad_merged, merge_weight, preferred_element_type=jnp.float32
    ).astype(jnp.bfloat16)
    grad_act = return_patches(grad_cells, fine_height, fine_depth, channels).astype(
        jnp.float32
    ) + grad_comb.astype(jnp.float32)
    grad_pre = (grad_act * silu_slope(pre_act)).astype(jnp.bfloat16)
    return fine_conv(grad_pre, fine_weight.transpose(0, 2, 1), True).astype(jnp.bfloat16)


def solution(mesh):
    in_specs = (
        P(None, ("groups", "wide"), None, "narrow"),
        P(None, ("groups", "wide"), None, "narrow"),
        P(),
        P("wide", None),
        P(None, None, "wide"),
        P(None, "wide"),
        P(None, "wide", None),
        P(None, "wide"),
        P("groups"),
    )
    out_specs = P(None, ("groups", "wide"), None, "narrow")
    sizes = dict(mesh.shape)
    fits = sizes["wide"] == PATCH and sizes["narrow"] == 2
    body = eight_shards if fits else shards
    return jax.shard_map(body, mesh=mesh, in_specs=in_specs, out_specs=out_specs, check_vma=False)
```

```python
import functools

import jax
import jax.numpy as jnp
from jax import lax
from jax.experimental import pallas as pl
from jax.experimental.pallas import tpu as pltpu
from jax.sharding import PartitionSpec as P

PATCH = 8


def extended(cells, sides, width):
    for axis, dim in sides:
        count = lax.axis_size(axis)
        ends = count - 1
        head = lax.slice_in_dim(cells, 0, width, axis=dim)
        tail = lax.slice_in_dim(cells, cells.shape[dim] - width, cells.shape[dim], axis=dim)
        cells = jnp.concatenate(
            [
                lax.ppermute(tail, axis, [(i, (i + 1) % count) for i in range(ends)]),
                cells,
                lax.ppermute(head, axis, [((i + 1) % count, i) for i in range(ends)]),
            ],
            axis=dim,
        )
    return cells


def shifts(transposed):
    return [
        (2 - i, 2 - j, 2 - k) if transposed else (i, j, k)
        for i in range(3)
        for j in range(3)
        for k in range(3)
    ]


def silu_slope(values):
    logistic = jax.nn.sigmoid(values)
    return logistic * (1.0 + values * (1.0 - logistic))


def fine_conv(fine_field, weight, transposed):
    grown = extended(fine_field, (("wide", 1), ("narrow", 3)), 1)
    padded = jnp.pad(grown, ((0, 0), (0, 0), (1, 1), (0, 0)))
    kernel = weight.reshape(3, 3, 3, weight.shape[1], weight.shape[2])
    if transposed:
        kernel = kernel[::-1, ::-1, ::-1]
    result = lax.conv_general_dilated(
        padded[None],
        kernel,
        (1, 1, 1),
        "VALID",
        dimension_numbers=("NCDHW", "DHWIO", "NCDHW"),
        preferred_element_type=jnp.float32,
    )
    return result[0]


def to_patches(fine_field):
    channels = fine_field.shape[0]
    shaped = fine_field.reshape(
        channels, PATCH, fine_field.shape[2] // PATCH, PATCH, fine_field.shape[3] // PATCH, PATCH
    )
    return shaped.transpose(2, 4, 1, 3, 5, 0).reshape(-1, PATCH**3 * channels)


def send_patches(fine_field):
    return lax.all_to_all(to_patches(fine_field), "wide", split_axis=1, concat_axis=0, tiled=True)


def return_patches(patch_rows, fine_height, fine_depth, channels):
    returned = lax.all_to_all(patch_rows, "wide", split_axis=0, concat_axis=1, tiled=True)
    shaped = returned.reshape(
        fine_height // PATCH, fine_depth // PATCH, PATCH, PATCH, PATCH, channels
    )
    return shaped.transpose(5, 2, 0, 3, 1, 4).reshape(channels, PATCH, fine_height, fine_depth)


def coarse_faces(coarse_block):
    return extended(coarse_block, (("narrow", 2),), 1)


def wide_input_conv(coarse_block, weight_mat, out_count, transposed):
    grown = coarse_faces(coarse_block)
    products = jnp.einsum("xyzd,dk->xyzk", grown, weight_mat, preferred_element_type=jnp.float32)
    padded = jnp.pad(products, ((1, 1), (1, 1), (0, 0), (0, 0)))
    extent = coarse_block.shape[:3]
    summed = jnp.zeros(extent + (out_count,), jnp.float32)
    for tap_index, (a, b, c) in enumerate(shifts(transposed)):
        summed = (
            summed
            + padded[
                a : a + extent[0],
                b : b + extent[1],
                c : c + extent[2],
                tap_index * out_count : (tap_index + 1) * out_count,
            ]
        )
    return summed


def narrow_input_conv(coarse_block, weight_mat, transposed):
    grown = coarse_faces(coarse_block)
    padded = jnp.pad(grown, ((1, 1), (1, 1), (0, 0), (0, 0)))
    extent = coarse_block.shape[:3]
    columns = jnp.concatenate(
        [
            padded[a : a + extent[0], b : b + extent[1], c : c + extent[2]]
            for a, b, c in shifts(transposed)
        ],
        axis=3,
    )
    return jnp.einsum("xyzk,kd->xyzd", columns, weight_mat, preferred_element_type=jnp.float32)


BF = jnp.bfloat16
F32 = jnp.float32
LIMIT = 16 * 1024 * 1024
VMEM = pl.BlockSpec(memory_space=pltpu.VMEM)
SMEM = pl.BlockSpec(memory_space=pltpu.SMEM)


def nn_dot(lhs, rhs):
    return jnp.dot(lhs, rhs, preferred_element_type=F32)


def nt_dot(lhs, rhs):
    return lax.dot_general(lhs, rhs, (((1,), (1,)), ((), ())), preferred_element_type=F32)


def shape_of(dims, dtype):
    return jax.ShapeDtypeStruct(dims, dtype)


def kernel_call(kernel, places, arrays, outs, scratch=()):
    return pl.pallas_call(
        kernel,
        in_specs=[SMEM] * len(places) + [VMEM] * len(arrays),
        out_specs=[VMEM] * len(outs),
        out_shape=outs,
        scratch_shapes=list(scratch),
        compiler_params=pltpu.CompilerParams(vmem_limit_bytes=LIMIT),
    )(*places, *arrays)


def banded(weight):
    taps = weight.reshape(9, 3, 32, 32)
    band = jnp.concatenate([taps[:, 2], taps[:, 1], taps[:, 0]], axis=2)
    wide_band = jnp.pad(band, ((0, 0), (0, 0), (224, 224)))

    def placed(start):
        return wide_band[:, :, start : start + 256]

    planes = jnp.concatenate([placed(224 - 32 * (d - 1)) for d in range(8)], axis=1)
    sides = jnp.concatenate([placed(288), placed(0)], axis=1)
    planes = planes.reshape(3, 3, 256, 256)
    sides = sides.reshape(3, 3, 64, 256)
    columns = []
    for j in range(3):
        columns.append(
            jnp.concatenate(
                [planes[:, j].reshape(768, 256), sides[:, j].reshape(192, 256), jnp.zeros((64, 256), BF)],
                axis=0,
            )
        )
    return jnp.concatenate(columns, axis=1)


def pack_kernel(field_ref, cot_ref, out_ref):
    for a in range(8):
        out_ref[a, 0:32] = field_ref[(a + 7) % 8]
        out_ref[a, 32:64] = field_ref[a]
        out_ref[a, 64:96] = field_ref[(a + 1) % 8]
        out_ref[a, 96:128] = cot_ref[a]


def arrived_planes(w, arrived_ref):
    none = jnp.zeros((32, 256), BF)
    before, own, after = [
        arrived_ref[:, 32 * s : 32 * s + 32, :].reshape(256, 256) for s in range(3)
    ]
    before = jnp.where(w == 0, jnp.concatenate([none, before[:224]], axis=0), before)
    after = jnp.where(w == 7, jnp.concatenate([after[32:], none], axis=0), after)
    return before, own, after


def returned_planes(w, returned_ref):
    rows = [returned_ref[7, 32:64]] + [returned_ref[a, 0:32] for a in range(8)] + [returned_ref[0, 32:64]]
    grown = jnp.concatenate(rows, axis=0)
    return grown[0:256], grown[32:288], grown[64:320]


def side_kernel(w_ref, planes_ref, own_ref, send_ref, *, planes_of):
    planes = planes_of(w_ref[0], planes_ref)
    source = lax.broadcasted_iota(jnp.int32, (256, 256), 0)
    target = lax.broadcasted_iota(jnp.int32, (256, 256), 1)
    sides = None
    for i, plane in enumerate(planes):
        high = (source >= 224) & (target == source - 224 + 64 * i)
        low = (source < 32) & (target == source + 64 * i + 32)
        part = nn_dot(plane, (high | low).astype(BF))
        sides = part if sides is None else sides + part
    even = (source & 1) == 0
    sides = jnp.where(even, pltpu.roll(sides, 255, 0), pltpu.roll(sides, 1, 0))
    low_side = (target & 32) != 0
    own = even == low_side
    zero = jnp.zeros_like(sides)
    own_ref[...] = jnp.where(own, sides, zero).astype(BF)
    send_ref[...] = jnp.where(own, zero, sides).astype(BF)


def side_call(w, planes, planes_of):
    shape = shape_of((256, 256), BF)
    return kernel_call(
        functools.partial(side_kernel, planes_of=planes_of), (w,), (planes,), [shape, shape]
    )


def fine_sum(n, planes, own_ref, got_ref, band_ref):
    lane = lax.broadcasted_iota(jnp.int32, (256, 256), 1)
    keep = ((lane & 32) != 0) == (n == 0)
    got = jnp.where(keep, got_ref[...].astype(F32), jnp.zeros((256, 256), F32))
    sides = (own_ref[...].astype(F32) + got).astype(BF)
    lhs = jnp.concatenate([*planes, sides], axis=1)
    total = nn_dot(lhs, band_ref[:, 256:512])
    y = (lax.broadcasted_iota(jnp.int32, (256, 1), 0) >> 1) & 15
    zero = jnp.zeros_like(total)
    below = pltpu.roll(nn_dot(lhs, band_ref[:, 0:256]), 2, 0)
    above = pltpu.roll(nn_dot(lhs, band_ref[:, 512:768]), 254, 0)
    return total + jnp.where(y > 0, below, zero) + jnp.where(y < 15, above, zero)


def cell_rows(ref, b):
    return jnp.concatenate([ref[pl.ds(2 * b + z, 16, stride=16), :] for z in range(2)], axis=0)


def merge_kernel(
    n_ref, w_ref, planes_ref, own_ref, got_ref, band_ref, merge_ref, pre_ref, act_ref, sum_ref, sum_b_ref, rows_ref
):
    n = n_ref[0]
    planes = arrived_planes(w_ref[0], planes_ref)
    wide_rows = fine_sum(n, planes, own_ref, got_ref, band_ref)
    rows_ref[0] = wide_rows[:, :128]
    rows_ref[1] = wide_rows[:, 128:]
    total = None
    for b in range(8):
        pre = jnp.concatenate([cell_rows(rows_ref.at[h], b) for h in range(2)], axis=1)
        pre_ref[b] = pre
        act = (pre * jax.nn.sigmoid(pre)).astype(BF)
        act_ref[b] = act
        part = nn_dot(act, merge_ref[256 * b : 256 * b + 256])
        total = part if total is None else total + part
    sum_ref[...] = total
    sum_b_ref[...] = total.astype(BF)


def cot_kernel(planes_ref, cot_ref, rows_ref):
    rows = planes_ref[:, 96:128, :].reshape(256, 256).astype(F32)
    rows_ref[0] = rows[:, :128]
    rows_ref[1] = rows[:, 128:]
    for b in range(8):
        cot_ref[b] = jnp.concatenate([cell_rows(rows_ref.at[h], b) for h in range(2)], axis=1).astype(BF)


def final_kernel(n_ref, w_ref, planes_ref, own_ref, got_ref, band_ref, out_ref):
    planes = returned_planes(w_ref[0], planes_ref)
    out_ref[...] = fine_sum(n_ref[0], planes, own_ref, got_ref, band_ref).astype(BF)


def put_columns(cols_ref, cells):
    row = lax.broadcasted_iota(jnp.int32, (64, 1), 0)
    along_y, along_x = row & 1, (row >> 1) & 7
    zero = jnp.zeros_like(cells)
    none = jnp.zeros((16, cells.shape[1]), BF)
    below = jnp.where(along_y == 1, pltpu.roll(cells, 1, 0), zero)
    above = jnp.where(along_y == 0, pltpu.roll(cells, 63, 0), zero)
    for j, moved_y in enumerate((below, cells, above)):
        before = jnp.where(along_x > 0, pltpu.roll(moved_y, 2, 0), zero)
        after = jnp.where(along_x < 7, pltpu.roll(moved_y, 62, 0), zero)
        for i, moved in enumerate((before, moved_y, after)):
            rows = moved.astype(BF)
            cols_ref[9 * i + 3 * j] = jnp.concatenate([none, rows[:48]], axis=0)
            cols_ref[9 * i + 3 * j + 1] = rows
            cols_ref[9 * i + 3 * j + 2] = jnp.concatenate([rows[16:], none], axis=0)


def both_halves(n, mine, got, axis):
    first = n == 0
    return jnp.concatenate([jnp.where(first, mine, got), jnp.where(first, got, mine)], axis=axis)


def conv_sum(cols_ref, weight_of, flipped, dot):
    total = None
    for t in range(27):
        part = dot(cols_ref[26 - t if flipped else t], weight_of(t))
        total = part if total is None else total + part
    return total


def feature_rows(n, ref):
    half = ref.shape[1] // 2
    return lambda t: ref[t, pl.ds(pl.multiple_of(n * half, half), half), :]


def feature_columns(n, ref):
    half = ref.shape[2] // 2
    return lambda t: ref[t, :, pl.ds(pl.multiple_of(n * half, half), half)]


def outer_kernel(n_ref, mine_ref, got_ref, weight_ref, sum_ref, cols_ref, *, flipped, dot, part_of):
    n = n_ref[0]
    put_columns(cols_ref, both_halves(n, mine_ref[...].astype(F32), got_ref[...].astype(F32), 0))
    sum_ref[...] = conv_sum(cols_ref, part_of(n, weight_ref), flipped, dot)


def inner_forward_kernel(
    n_ref, mine_ref, got_ref, bias_ref, weight_ref, gate_ref, sum_ref, sum_b_ref, cols_ref
):
    gate = mine_ref[...] + got_ref[...] + bias_ref[...]
    gate_ref[...] = gate
    put_columns(cols_ref, gate * jax.nn.sigmoid(gate))
    total = conv_sum(cols_ref, feature_columns(n_ref[0], weight_ref), False, nn_dot)
    sum_ref[...] = total
    sum_b_ref[...] = total.astype(BF)


def inner_backward_kernel(
    n_ref, mine_ref, got_ref, gate_ref, weight_ref, sum_ref, sum_b_ref, cols_ref
):
    put_columns(cols_ref, (mine_ref[...] + got_ref[...]) * silu_slope(gate_ref[...]))
    total = conv_sum(cols_ref, feature_rows(n_ref[0], weight_ref), True, nt_dot)
    sum_ref[...] = total
    sum_b_ref[...] = total.astype(BF)


def expand_kernel(
    n_ref, merged_ref, mine_ref, got_ref, act_ref, cot_ref, expand_ref, grad_ref, sum_ref, sum_b_ref
):
    branch = both_halves(n_ref[0], mine_ref[...].astype(F32), got_ref[...].astype(F32), 1)
    residual = (merged_ref[...] + branch).astype(BF)
    total = None
    for b in range(8):
        part = expand_ref[:, 256 * b : 256 * b + 256]
        expanded = nn_dot(residual, part).astype(BF)
        combined = act_ref[b].astype(F32) + expanded.astype(F32)
        grad = (cot_ref[b].astype(F32) * silu_slope(combined)).astype(BF)
        grad_ref[b] = grad
        more = nt_dot(grad, part)
        total = more if total is None else total + more
    sum_ref[...] = total
    sum_b_ref[...] = total.astype(BF)


def grad_kernel(
    n_ref, w_ref, res_ref, mine_ref, got_ref, comb_ref, pre_ref, merge_ref, out_ref, rows_ref
):
    w = w_ref[0]
    conv = both_halves(n_ref[0], mine_ref[...].astype(F32), got_ref[...].astype(F32), 1)
    merged_grad = (res_ref[...] + conv).astype(BF)
    for b in range(8):
        cells = nt_dot(merged_grad, merge_ref[256 * b : 256 * b + 256]).astype(BF)
        grad = cells.astype(F32) + comb_ref[b].astype(F32)
        grad = grad * silu_slope(pre_ref[b])
        for z in range(2):
            for h in range(2):
                rows_ref[h, pl.ds(2 * b + z, 16, stride=16), :] = grad[
                    16 * z : 16 * z + 16, 128 * h : 128 * h + 128
                ]
    rows = jnp.concatenate([rows_ref[0], rows_ref[1]], axis=1).astype(BF)
    none = jnp.zeros((32, 256), BF)
    for x in range(8):
        ahead = rows[32 * x + 32 : 32 * x + 64] if x < 7 else none
        behind = rows[32 * x - 32 : 32 * x] if x > 0 else none
        out_ref[x, 0:32] = rows[32 * x : 32 * x + 32]
        out_ref[x, 32:64] = jnp.where(w == 0, ahead, behind)


def swap_narrow(value):
    return lax.ppermute(value, "narrow", [(0, 1), (1, 0)])


def summed_wide(part, part_b):
    def partner(value, mask):
        return lax.ppermute(value, "wide", [(i, i ^ mask) for i in range(8)])

    pair = part + partner(part_b, 1).astype(F32)
    pair_b = pair.astype(BF)
    others = [partner(pair_b, mask) for mask in (2, 4, 6)]
    return pair + others[0].astype(F32) + others[1].astype(F32) + others[2].astype(F32)


def to_feature_halves(n, cells):
    half = cells.shape[1] // 2
    low, high = cells[:, :half], cells[:, half:]
    return jnp.where(n == 0, low, high), swap_narrow(jnp.where(n == 0, high, low))


def to_cell_halves(n, rows):
    half = rows.shape[0] // 2
    low, high = rows[:half], rows[half:]
    return jnp.where(n == 0, low, high), swap_narrow(jnp.where(n == 0, high, low).astype(BF))


def across_wide(value):
    return lax.all_to_all(value, "wide", split_axis=0, concat_axis=0, tiled=True)


def eight_shards(
    volume,
    cotangent,
    fine_weight,
    merge_weight,
    hidden_weight,
    step_table,
    output_weight,
    expand_weight,
    timestep,
):
    features = merge_weight.shape[1]
    hidden = hidden_weight.shape[2]
    half = features // 2
    w = lax.axis_index("wide").astype(jnp.int32).reshape(1)
    n_index = lax.axis_index("narrow")
    n = n_index.astype(jnp.int32).reshape(1)

    def row_form(fine_field):
        return fine_field.transpose(1, 2, 3, 0).reshape(8, 32, 256)

    (outgoing,) = kernel_call(
        pack_kernel, (), (row_form(volume), row_form(cotangent)), [shape_of((8, 128, 256), BF)]
    )
    arrived = across_wide(outgoing)
    sides, sent = side_call(w, arrived, arrived_planes)
    fine_rows = pltpu.VMEM((2, 256, 128), F32)
    sum_shapes = [shape_of((32, features), F32), shape_of((32, features), BF)]
    pre_act, act, merged_part, merged_part_b = kernel_call(
        merge_kernel,
        (n, w),
        (arrived, sides, swap_narrow(sent), banded(fine_weight), merge_weight),
        [shape_of((8, 32, 256), F32), shape_of((8, 32, 256), BF)] + sum_shapes,
        [fine_rows],
    )
    (cot,) = kernel_call(cot_kernel, (), (arrived,), [shape_of((8, 32, 256), BF)], [fine_rows])
    merged = summed_wide(merged_part, merged_part_b)
    mine, got = to_feature_halves(n_index, merged.astype(BF))

    gate_shape = shape_of((64, hidden), F32)
    half_shapes = [shape_of((64, half), F32), shape_of((64, half), BF)]
    outer_columns = [pltpu.VMEM((27, 64, half), BF)]
    inner_columns = [pltpu.VMEM((27, 64, hidden), BF)]

    (gate_part,) = kernel_call(
        functools.partial(outer_kernel, flipped=False, dot=nn_dot, part_of=feature_rows),
        (n,), (mine, got, hidden_weight), [gate_shape], outer_columns,
    )
    bias = lax.dynamic_slice_in_dim(step_table, timestep[0], 1, axis=0)
    gate_pre, branch_part, branch_part_b = kernel_call(
        inner_forward_kernel,
        (n,), (gate_part, swap_narrow(gate_part), bias, output_weight),
        [gate_shape] + half_shapes, inner_columns,
    )
    mine, got = to_cell_halves(n_index, summed_wide(branch_part, branch_part_b))
    grad_comb, res_part, res_part_b = kernel_call(
        expand_kernel,
        (n,), (merged, mine, got, act, cot, expand_weight),
        [shape_of((8, 32, 256), BF)] + sum_shapes,
    )
    grad_res = summed_wide(res_part, res_part_b)
    mine, got = to_feature_halves(n_index, grad_res.astype(BF))
    (hidden_part,) = kernel_call(
        functools.partial(outer_kernel, flipped=True, dot=nt_dot, part_of=feature_columns),
        (n,), (mine, got, output_weight), [gate_shape], outer_columns,
    )
    conv_part, conv_part_b = kernel_call(
        inner_backward_kernel,
        (n,), (hidden_part, swap_narrow(hidden_part), gate_pre, hidden_weight),
        half_shapes, inner_columns,
    )
    mine, got = to_cell_halves(n_index, summed_wide(conv_part, conv_part_b))
    (leaving,) = kernel_call(
        grad_kernel,
        (n, w), (grad_res, mine, got, grad_comb, pre_act, merge_weight),
        [shape_of((8, 64, 256), BF)], [fine_rows],
    )
    returned = across_wide(leaving)
    sides, sent = side_call(w, returned, returned_planes)
    back = fine_weight[::-1].transpose(0, 2, 1)
    (result,) = kernel_call(
        final_kernel,
        (n, w), (returned, sides, swap_narrow(sent), banded(back)),
        [shape_of((256, 256), BF)],
    )
    return result.reshape(8, 16, 16, 32).transpose(3, 0, 1, 2)


def shards(
    volume,
    cotangent,
    fine_weight,
    merge_weight,
    hidden_weight,
    step_table,
    output_weight,
    expand_weight,
    timestep,
):
    channels = volume.shape[0]
    fine_height = volume.shape[2]
    fine_depth = volume.shape[3]
    wide_count = lax.axis_size("wide")
    features = merge_weight.shape[1]
    hidden_local = hidden_weight.shape[2]
    coarse_grid = (wide_count, fine_height // PATCH, fine_depth // PATCH)
    hidden_mat = hidden_weight.transpose(1, 0, 2).reshape(features, 27 * hidden_local)
    output_mat = output_weight.reshape(27 * hidden_local, features)
    output_back = output_weight.transpose(2, 0, 1).reshape(features, 27 * hidden_local)
    hidden_back = hidden_weight.transpose(0, 2, 1).reshape(27 * hidden_local, features)

    def total_rows(partial_value):
        return lax.psum(partial_value, "wide")

    pre_act = fine_conv(volume, fine_weight, False)
    activated = jax.nn.silu(pre_act).astype(jnp.bfloat16)
    received = send_patches(activated)
    merged = total_rows(jnp.dot(received, merge_weight, preferred_element_type=jnp.float32))
    coarse_in = merged.astype(jnp.bfloat16).reshape(coarse_grid + (features,))
    bias_row = step_table[timestep[0]]
    gate_pre = wide_input_conv(coarse_in, hidden_mat, hidden_local, False) + bias_row
    hidden_act = jax.nn.silu(gate_pre).astype(jnp.bfloat16)
    branch = total_rows(narrow_input_conv(hidden_act, output_mat, False).reshape(-1, features))
    residual_sum = (merged + branch).astype(jnp.bfloat16)
    expanded = jnp.dot(residual_sum, expand_weight, preferred_element_type=jnp.float32).astype(
        jnp.bfloat16
    )
    expanded_field = return_patches(expanded, fine_height, fine_depth, channels)
    combined = activated.astype(jnp.float32) + expanded_field.astype(jnp.float32)
    grad_comb = (cotangent.astype(jnp.float32) * silu_slope(combined)).astype(jnp.bfloat16)
    grad_res = total_rows(
        jnp.einsum(
            "nk,dk->nd", send_patches(grad_comb), expand_weight, preferred_element_type=jnp.float32
        )
    )
    grad_res_b = grad_res.astype(jnp.bfloat16).reshape(coarse_grid + (features,))
    grad_hidden = wide_input_conv(grad_res_b, output_back, hidden_local, True)
    grad_gate = (grad_hidden * silu_slope(gate_pre)).astype(jnp.bfloat16)
    grad_conv = total_rows(narrow_input_conv(grad_gate, hidden_back, True).reshape(-1, features))
    grad_merged = (grad_res + grad_conv).astype(jnp.bfloat16)
    grad_cells = jnp.einsum(
        "nd,kd->nk", grad_merged, merge_weight, preferred_element_type=jnp.float32
    ).astype(jnp.bfloat16)
    grad_act = return_patches(grad_cells, fine_height, fine_depth, channels).astype(
        jnp.float32
    ) + grad_comb.astype(jnp.float32)
    grad_pre = (grad_act * silu_slope(pre_act)).astype(jnp.bfloat16)
    return fine_conv(grad_pre, fine_weight.transpose(0, 2, 1), True).astype(jnp.bfloat16)


def solution(mesh):
    in_specs = (
        P(None, ("groups", "wide"), None, "narrow"),
        P(None, ("groups", "wide"), None, "narrow"),
        P(),
        P("wide", None),
        P(None, None, "wide"),
        P(None, "wide"),
        P(None, "wide", None),
        P(None, "wide"),
        P("groups"),
    )
    out_specs = P(None, ("groups", "wide"), None, "narrow")
    sizes = dict(mesh.shape)
    fits = sizes["wide"] == PATCH and sizes["narrow"] == 2
    body = eight_shards if fits else shards
    return jax.shard_map(body, mesh=mesh, in_specs=in_specs, out_specs=out_specs, check_vma=False)
```

```python
import functools

import jax
import jax.numpy as jnp
from jax import lax
from jax.experimental import pallas as pl
from jax.experimental.pallas import tpu as pltpu
from jax.sharding import PartitionSpec as P

PATCH = 8


def extended(cells, sides, width):
    for axis, dim in sides:
        count = lax.axis_size(axis)
        ends = count - 1
        head = lax.slice_in_dim(cells, 0, width, axis=dim)
        tail = lax.slice_in_dim(cells, cells.shape[dim] - width, cells.shape[dim], axis=dim)
        cells = jnp.concatenate(
            [
                lax.ppermute(tail, axis, [(i, (i + 1) % count) for i in range(ends)]),
                cells,
                lax.ppermute(head, axis, [((i + 1) % count, i) for i in range(ends)]),
            ],
            axis=dim,
        )
    return cells


def shifts(transposed):
    return [
        (2 - i, 2 - j, 2 - k) if transposed else (i, j, k)
        for i in range(3)
        for j in range(3)
        for k in range(3)
    ]


def silu_slope(values):
    logistic = jax.nn.sigmoid(values)
    return logistic * (1.0 + values * (1.0 - logistic))


def fine_conv(fine_field, weight, transposed):
    grown = extended(fine_field, (("wide", 1), ("narrow", 3)), 1)
    padded = jnp.pad(grown, ((0, 0), (0, 0), (1, 1), (0, 0)))
    kernel = weight.reshape(3, 3, 3, weight.shape[1], weight.shape[2])
    if transposed:
        kernel = kernel[::-1, ::-1, ::-1]
    result = lax.conv_general_dilated(
        padded[None],
        kernel,
        (1, 1, 1),
        "VALID",
        dimension_numbers=("NCDHW", "DHWIO", "NCDHW"),
        preferred_element_type=jnp.float32,
    )
    return result[0]


def to_patches(fine_field):
    channels = fine_field.shape[0]
    shaped = fine_field.reshape(
        channels, PATCH, fine_field.shape[2] // PATCH, PATCH, fine_field.shape[3] // PATCH, PATCH
    )
    return shaped.transpose(2, 4, 1, 3, 5, 0).reshape(-1, PATCH**3 * channels)


def send_patches(fine_field):
    return lax.all_to_all(to_patches(fine_field), "wide", split_axis=1, concat_axis=0, tiled=True)


def return_patches(patch_rows, fine_height, fine_depth, channels):
    returned = lax.all_to_all(patch_rows, "wide", split_axis=0, concat_axis=1, tiled=True)
    shaped = returned.reshape(
        fine_height // PATCH, fine_depth // PATCH, PATCH, PATCH, PATCH, channels
    )
    return shaped.transpose(5, 2, 0, 3, 1, 4).reshape(channels, PATCH, fine_height, fine_depth)


def coarse_faces(coarse_block):
    return extended(coarse_block, (("narrow", 2),), 1)


def wide_input_conv(coarse_block, weight_mat, out_count, transposed):
    grown = coarse_faces(coarse_block)
    products = jnp.einsum("xyzd,dk->xyzk", grown, weight_mat, preferred_element_type=jnp.float32)
    padded = jnp.pad(products, ((1, 1), (1, 1), (0, 0), (0, 0)))
    extent = coarse_block.shape[:3]
    summed = jnp.zeros(extent + (out_count,), jnp.float32)
    for tap_index, (a, b, c) in enumerate(shifts(transposed)):
        summed = (
            summed
            + padded[
                a : a + extent[0],
                b : b + extent[1],
                c : c + extent[2],
                tap_index * out_count : (tap_index + 1) * out_count,
            ]
        )
    return summed


def narrow_input_conv(coarse_block, weight_mat, transposed):
    grown = coarse_faces(coarse_block)
    padded = jnp.pad(grown, ((1, 1), (1, 1), (0, 0), (0, 0)))
    extent = coarse_block.shape[:3]
    columns = jnp.concatenate(
        [
            padded[a : a + extent[0], b : b + extent[1], c : c + extent[2]]
            for a, b, c in shifts(transposed)
        ],
        axis=3,
    )
    return jnp.einsum("xyzk,kd->xyzd", columns, weight_mat, preferred_element_type=jnp.float32)


BF = jnp.bfloat16
F32 = jnp.float32
LIMIT = 10 * 1024 * 1024
BESIDE = 32 * 1024 * 1024
VMEM = pl.BlockSpec(memory_space=pltpu.VMEM)
SMEM = pl.BlockSpec(memory_space=pltpu.SMEM)


def nn_dot(lhs, rhs):
    return jnp.dot(lhs, rhs, preferred_element_type=F32)


def nt_dot(lhs, rhs):
    return lax.dot_general(lhs, rhs, (((1,), (1,)), ((), ())), preferred_element_type=F32)


def shape_of(dims, dtype):
    return jax.ShapeDtypeStruct(dims, dtype)


def kernel_call(kernel, places, arrays, outs, scratch=(), cost=None, rest=()):
    return pl.pallas_call(
        kernel,
        in_specs=[SMEM] * len(places) + [VMEM] * len(arrays) + [pl.BlockSpec(memory_space=pl.ANY)] * len(rest),
        out_specs=[VMEM] * len(outs),
        out_shape=outs,
        scratch_shapes=list(scratch),
        cost_estimate=cost and pl.CostEstimate(flops=0, bytes_accessed=cost, transcendentals=0),
        compiler_params=pltpu.CompilerParams(vmem_limit_bytes=LIMIT),
    )(*places, *arrays, *rest)


def band_kernel(weight_ref, out_ref, *, back):
    row = lax.broadcasted_iota(jnp.int32, (32, 256), 0)
    lane = lax.broadcasted_iota(jnp.int32, (32, 256), 1)
    places = [(lane == row + 32 * (2 - k)).astype(BF) for k in range(3)]
    same = (
        lax.broadcasted_iota(jnp.int32, (32, 32), 0) == lax.broadcasted_iota(jnp.int32, (32, 32), 1)
    ).astype(BF)
    for i in range(3):
        for j in range(3):
            taps = None
            for k in range(3):
                t = 9 * i + 3 * j + k
                tap = nt_dot(same, weight_ref[26 - t]).astype(BF) if back else weight_ref[t]
                part = nn_dot(tap, places[k])
                taps = part if taps is None else taps + part
            columns = slice(256 * j, 256 * j + 256)

            def placed(start):
                moved = pltpu.roll(taps, start % 256, 1)
                return jnp.where((lane >= start) & (lane < start + 96), moved, 0.0).astype(BF)

            for d in range(8):
                out_ref[256 * i + 32 * d : 256 * i + 32 * d + 32, columns] = placed(32 * (d - 1))
            out_ref[768 + 64 * i : 800 + 64 * i, columns] = placed(-64)
            out_ref[800 + 64 * i : 832 + 64 * i, columns] = placed(224)
    out_ref[960:1024, :] = jnp.zeros((64, 768), BF)


def banded(weight, back):
    (out,) = kernel_call(
        functools.partial(band_kernel, back=back), (), (weight,), [shape_of((1024, 768), BF)], cost=BESIDE
    )
    return out


def pack_kernel(field_ref, cot_ref, out_ref):
    for a in range(8):
        out_ref[a, 0:32] = field_ref[(a + 7) % 8]
        out_ref[a, 32:64] = field_ref[a]
        out_ref[a, 64:96] = field_ref[(a + 1) % 8]
        out_ref[a, 96:128] = cot_ref[a]


def arrived_planes(w, arrived_ref):
    none = jnp.zeros((32, 256), BF)
    before, own, after = [
        arrived_ref[:, 32 * s : 32 * s + 32, :].reshape(256, 256) for s in range(3)
    ]
    before = jnp.where(w == 0, jnp.concatenate([none, before[:224]], axis=0), before)
    after = jnp.where(w == 7, jnp.concatenate([after[32:], none], axis=0), after)
    return before, own, after


def returned_planes(w, returned_ref):
    rows = [returned_ref[7, 32:64]] + [returned_ref[a, 0:32] for a in range(8)] + [returned_ref[0, 32:64]]
    grown = jnp.concatenate(rows, axis=0)
    return grown[0:256], grown[32:288], grown[64:320]


def side_kernel(w_ref, planes_ref, band_ref, own_ref, send_ref, *, planes_of):
    del band_ref
    planes = planes_of(w_ref[0], planes_ref)
    source = lax.broadcasted_iota(jnp.int32, (256, 256), 0)
    target = lax.broadcasted_iota(jnp.int32, (256, 256), 1)
    sides = None
    for i, plane in enumerate(planes):
        high = (source >= 224) & (target == source - 224 + 64 * i)
        low = (source < 32) & (target == source + 64 * i + 32)
        part = nn_dot(plane, (high | low).astype(BF))
        sides = part if sides is None else sides + part
    even = (source & 1) == 0
    sides = jnp.where(even, pltpu.roll(sides, 255, 0), pltpu.roll(sides, 1, 0))
    low_side = (target & 32) != 0
    own = even == low_side
    zero = jnp.zeros_like(sides)
    own_ref[...] = jnp.where(own, sides, zero).astype(BF)
    send_ref[...] = jnp.where(own, zero, sides).astype(BF)


def side_call(w, planes, band, planes_of):
    shape = shape_of((256, 256), BF)
    return kernel_call(
        functools.partial(side_kernel, planes_of=planes_of), (w,), (planes, band), [shape, shape]
    )


def fine_sum(n, planes, own_ref, got_ref, band_ref):
    lane = lax.broadcasted_iota(jnp.int32, (256, 256), 1)
    keep = ((lane & 32) != 0) == (n == 0)
    got = jnp.where(keep, got_ref[...].astype(F32), jnp.zeros((256, 256), F32))
    sides = (own_ref[...].astype(F32) + got).astype(BF)
    lhs = jnp.concatenate([*planes, sides], axis=1)
    total = nn_dot(lhs, band_ref[:, 256:512])
    y = (lax.broadcasted_iota(jnp.int32, (256, 1), 0) >> 1) & 15
    zero = jnp.zeros_like(total)
    below = pltpu.roll(nn_dot(lhs, band_ref[:, 0:256]), 2, 0)
    above = pltpu.roll(nn_dot(lhs, band_ref[:, 512:768]), 254, 0)
    return total + jnp.where(y > 0, below, zero) + jnp.where(y < 15, above, zero)


def cell_rows(ref, b):
    return jnp.concatenate([ref[pl.ds(2 * b + z, 16, stride=16), :] for z in range(2)], axis=0)


def merge_kernel(
    n_ref, w_ref, planes_ref, own_ref, got_ref, band_ref, merge_ref, pre_ref, act_ref, sum_ref, sum_b_ref, rows_ref
):
    n = n_ref[0]
    planes = arrived_planes(w_ref[0], planes_ref)
    wide_rows = fine_sum(n, planes, own_ref, got_ref, band_ref)
    rows_ref[0] = wide_rows[:, :128]
    rows_ref[1] = wide_rows[:, 128:]
    total = None
    for b in range(8):
        pre = jnp.concatenate([cell_rows(rows_ref.at[h], b) for h in range(2)], axis=1)
        pre_ref[b] = pre
        act = (pre * jax.nn.sigmoid(pre)).astype(BF)
        act_ref[b] = act
        part = nn_dot(act, merge_ref[256 * b : 256 * b + 256])
        total = part if total is None else total + part
    sum_ref[...] = total
    sum_b_ref[...] = total.astype(BF)


def cot_kernel(planes_ref, cot_ref, rows_ref):
    rows = planes_ref[:, 96:128, :].reshape(256, 256).astype(F32)
    rows_ref[0] = rows[:, :128]
    rows_ref[1] = rows[:, 128:]
    for b in range(8):
        cot_ref[b] = jnp.concatenate([cell_rows(rows_ref.at[h], b) for h in range(2)], axis=1).astype(BF)


def final_kernel(n_ref, w_ref, planes_ref, own_ref, got_ref, band_ref, out_ref):
    planes = returned_planes(w_ref[0], planes_ref)
    out_ref[...] = fine_sum(n_ref[0], planes, own_ref, got_ref, band_ref).astype(BF)


def put_columns(cols_ref, cells):
    row = lax.broadcasted_iota(jnp.int32, (64, 1), 0)
    along_y, along_x = row & 1, (row >> 1) & 7
    zero = jnp.zeros_like(cells)
    none = jnp.zeros((16, cells.shape[1]), BF)
    below = jnp.where(along_y == 1, pltpu.roll(cells, 1, 0), zero)
    above = jnp.where(along_y == 0, pltpu.roll(cells, 63, 0), zero)
    for j, moved_y in enumerate((below, cells, above)):
        before = jnp.where(along_x > 0, pltpu.roll(moved_y, 2, 0), zero)
        after = jnp.where(along_x < 7, pltpu.roll(moved_y, 62, 0), zero)
        for i, moved in enumerate((before, moved_y, after)):
            rows = moved.astype(BF)
            cols_ref[9 * i + 3 * j] = jnp.concatenate([none, rows[:48]], axis=0)
            cols_ref[9 * i + 3 * j + 1] = rows
            cols_ref[9 * i + 3 * j + 2] = jnp.concatenate([rows[16:], none], axis=0)


def both_halves(n, mine, got, axis):
    first = n == 0
    return jnp.concatenate([jnp.where(first, mine, got), jnp.where(first, got, mine)], axis=axis)


def conv_sum(cols_ref, weight_of, flipped, dot):
    total = None
    for t in range(27):
        part = dot(cols_ref[26 - t if flipped else t], weight_of(t))
        total = part if total is None else total + part
    return total


def feature_rows(n, ref):
    half = ref.shape[1] // 2
    return lambda t: ref[t, pl.ds(pl.multiple_of(n * half, half), half), :]


def feature_columns(n, ref):
    half = ref.shape[2] // 2
    return lambda t: ref[t, :, pl.ds(pl.multiple_of(n * half, half), half)]


def outer_kernel(n_ref, mine_ref, got_ref, weight_ref, sum_ref, cols_ref, *, flipped, dot, part_of):
    n = n_ref[0]
    put_columns(cols_ref, both_halves(n, mine_ref[...].astype(F32), got_ref[...].astype(F32), 0))
    sum_ref[...] = conv_sum(cols_ref, part_of(n, weight_ref), flipped, dot)


def inner_forward_kernel(
    n_ref, step_ref, mine_ref, got_ref, weight_ref, table_ref, gate_ref, sum_ref, sum_b_ref, cols_ref, bias_ref, sem
):
    step = step_ref[0]
    group = pl.ds(pl.multiple_of(step // 8 * 8, 8), 8)
    fetch = pltpu.make_async_copy(table_ref.at[group], bias_ref, sem)
    fetch.start()
    fetch.wait()
    rows = bias_ref[...]
    chosen = lax.broadcasted_iota(jnp.int32, rows.shape, 0) == step % 8
    bias = jnp.sum(jnp.where(chosen, rows, jnp.zeros_like(rows)), axis=0, keepdims=True)
    gate = mine_ref[...] + got_ref[...] + bias
    gate_ref[...] = gate
    put_columns(cols_ref, gate * jax.nn.sigmoid(gate))
    total = conv_sum(cols_ref, feature_columns(n_ref[0], weight_ref), False, nn_dot)
    sum_ref[...] = total
    sum_b_ref[...] = total.astype(BF)


def inner_backward_kernel(
    n_ref, mine_ref, got_ref, gate_ref, weight_ref, sum_ref, sum_b_ref, cols_ref
):
    put_columns(cols_ref, (mine_ref[...] + got_ref[...]) * silu_slope(gate_ref[...]))
    total = conv_sum(cols_ref, feature_rows(n_ref[0], weight_ref), True, nt_dot)
    sum_ref[...] = total
    sum_b_ref[...] = total.astype(BF)


def expand_kernel(
    n_ref, merged_ref, mine_ref, got_ref, act_ref, cot_ref, expand_ref, grad_ref, sum_ref, sum_b_ref
):
    branch = both_halves(n_ref[0], mine_ref[...].astype(F32), got_ref[...].astype(F32), 1)
    residual = (merged_ref[...] + branch).astype(BF)
    total = None
    for b in range(8):
        part = expand_ref[:, 256 * b : 256 * b + 256]
        expanded = nn_dot(residual, part).astype(BF)
        combined = act_ref[b].astype(F32) + expanded.astype(F32)
        grad = (cot_ref[b].astype(F32) * silu_slope(combined)).astype(BF)
        grad_ref[b] = grad
        more = nt_dot(grad, part)
        total = more if total is None else total + more
    sum_ref[...] = total
    sum_b_ref[...] = total.astype(BF)


def grad_kernel(
    n_ref, w_ref, res_ref, mine_ref, got_ref, comb_ref, pre_ref, merge_ref, out_ref, rows_ref
):
    w = w_ref[0]
    conv = both_halves(n_ref[0], mine_ref[...].astype(F32), got_ref[...].astype(F32), 1)
    merged_grad = (res_ref[...] + conv).astype(BF)
    for b in range(8):
        cells = nt_dot(merged_grad, merge_ref[256 * b : 256 * b + 256]).astype(BF)
        grad = cells.astype(F32) + comb_ref[b].astype(F32)
        grad = grad * silu_slope(pre_ref[b])
        for z in range(2):
            for h in range(2):
                rows_ref[h, pl.ds(2 * b + z, 16, stride=16), :] = grad[
                    16 * z : 16 * z + 16, 128 * h : 128 * h + 128
                ]
    rows = jnp.concatenate([rows_ref[0], rows_ref[1]], axis=1).astype(BF)
    none = jnp.zeros((32, 256), BF)
    for x in range(8):
        ahead = rows[32 * x + 32 : 32 * x + 64] if x < 7 else none
        behind = rows[32 * x - 32 : 32 * x] if x > 0 else none
        out_ref[x, 0:32] = rows[32 * x : 32 * x + 32]
        out_ref[x, 32:64] = jnp.where(w == 0, ahead, behind)


def swap_narrow(value):
    return lax.ppermute(value, "narrow", [(0, 1), (1, 0)])


def pair_kernel(part_ref, got_ref, pair_ref, pair_b_ref):
    pair = part_ref[...] + got_ref[...].astype(F32)
    pair_ref[...] = pair
    pair_b_ref[...] = pair.astype(BF)


def summed_wide(part, part_b):
    def partner(value, mask):
        return lax.ppermute(value, "wide", [(i, i ^ mask) for i in range(8)])

    shape = part.shape
    pair, pair_b = kernel_call(
        pair_kernel, (), (part, partner(part_b, 1)), [shape_of(shape, F32), shape_of(shape, BF)], cost=BESIDE
    )
    others = [partner(pair_b, mask) for mask in (2, 4, 6)]
    return pair + others[0].astype(F32) + others[1].astype(F32) + others[2].astype(F32)


def to_feature_halves(n, cells):
    half = cells.shape[1] // 2
    low, high = cells[:, :half], cells[:, half:]
    return jnp.where(n == 0, low, high), swap_narrow(jnp.where(n == 0, high, low))


def to_cell_halves(n, rows):
    half = rows.shape[0] // 2
    low, high = rows[:half], rows[half:]
    return jnp.where(n == 0, low, high), swap_narrow(jnp.where(n == 0, high, low).astype(BF))


def across_wide(value):
    return lax.all_to_all(value, "wide", split_axis=0, concat_axis=0, tiled=True)


def eight_shards(
    volume,
    cotangent,
    fine_weight,
    merge_weight,
    hidden_weight,
    step_table,
    output_weight,
    expand_weight,
    timestep,
):
    features = merge_weight.shape[1]
    hidden = hidden_weight.shape[2]
    half = features // 2
    w = lax.axis_index("wide").astype(jnp.int32).reshape(1)
    n_index = lax.axis_index("narrow")
    n = n_index.astype(jnp.int32).reshape(1)

    def row_form(fine_field):
        return fine_field.transpose(1, 2, 3, 0).reshape(8, 32, 256)

    (outgoing,) = kernel_call(
        pack_kernel, (), (row_form(volume), row_form(cotangent)), [shape_of((8, 128, 256), BF)]
    )
    arrived = across_wide(outgoing)
    band = banded(fine_weight, False)
    sides, sent = side_call(w, arrived, band, arrived_planes)
    fine_rows = pltpu.VMEM((2, 256, 128), F32)
    sum_shapes = [shape_of((32, features), F32), shape_of((32, features), BF)]
    pre_act, act, merged_part, merged_part_b = kernel_call(
        merge_kernel,
        (n, w),
        (arrived, sides, swap_narrow(sent), band, merge_weight),
        [shape_of((8, 32, 256), F32), shape_of((8, 32, 256), BF)] + sum_shapes,
        [fine_rows],
    )
    (cot,) = kernel_call(cot_kernel, (), (arrived,), [shape_of((8, 32, 256), BF)], [fine_rows])
    merged = summed_wide(merged_part, merged_part_b)
    mine, got = to_feature_halves(n_index, merged.astype(BF))

    gate_shape = shape_of((64, hidden), F32)
    half_shapes = [shape_of((64, half), F32), shape_of((64, half), BF)]
    outer_columns = [pltpu.VMEM((27, 64, half), BF)]
    inner_columns = [pltpu.VMEM((27, 64, hidden), BF)]

    (gate_part,) = kernel_call(
        functools.partial(outer_kernel, flipped=False, dot=nn_dot, part_of=feature_rows),
        (n,), (mine, got, hidden_weight), [gate_shape], outer_columns,
    )
    gate_pre, branch_part, branch_part_b = kernel_call(
        inner_forward_kernel,
        (n, timestep), (gate_part, swap_narrow(gate_part), output_weight), [gate_shape] + half_shapes,
        inner_columns + [pltpu.VMEM((8, hidden), F32), pltpu.SemaphoreType.DMA], rest=(step_table,),
    )
    mine, got = to_cell_halves(n_index, summed_wide(branch_part, branch_part_b))
    grad_comb, res_part, res_part_b = kernel_call(
        expand_kernel,
        (n,), (merged, mine, got, act, cot, expand_weight),
        [shape_of((8, 32, 256), BF)] + sum_shapes,
    )
    grad_res = summed_wide(res_part, res_part_b)
    mine, got = to_feature_halves(n_index, grad_res.astype(BF))
    (hidden_part,) = kernel_call(
        functools.partial(outer_kernel, flipped=True, dot=nt_dot, part_of=feature_columns),
        (n,), (mine, got, output_weight), [gate_shape], outer_columns,
    )
    conv_part, conv_part_b = kernel_call(
        inner_backward_kernel,
        (n,), (hidden_part, swap_narrow(hidden_part), gate_pre, hidden_weight),
        half_shapes, inner_columns,
    )
    mine, got = to_cell_halves(n_index, summed_wide(conv_part, conv_part_b))
    (leaving,) = kernel_call(
        grad_kernel,
        (n, w), (grad_res, mine, got, grad_comb, pre_act, merge_weight),
        [shape_of((8, 64, 256), BF)], [fine_rows],
    )
    returned = across_wide(leaving)
    band = banded(fine_weight, True)
    sides, sent = side_call(w, returned, band, returned_planes)
    (result,) = kernel_call(
        final_kernel,
        (n, w), (returned, sides, swap_narrow(sent), band),
        [shape_of((256, 256), BF)],
    )
    return result.reshape(8, 16, 16, 32).transpose(3, 0, 1, 2)


def shards(
    volume,
    cotangent,
    fine_weight,
    merge_weight,
    hidden_weight,
    step_table,
    output_weight,
    expand_weight,
    timestep,
):
    channels = volume.shape[0]
    fine_height = volume.shape[2]
    fine_depth = volume.shape[3]
    wide_count = lax.axis_size("wide")
    features = merge_weight.shape[1]
    hidden_local = hidden_weight.shape[2]
    coarse_grid = (wide_count, fine_height // PATCH, fine_depth // PATCH)
    hidden_mat = hidden_weight.transpose(1, 0, 2).reshape(features, 27 * hidden_local)
    output_mat = output_weight.reshape(27 * hidden_local, features)
    output_back = output_weight.transpose(2, 0, 1).reshape(features, 27 * hidden_local)
    hidden_back = hidden_weight.transpose(0, 2, 1).reshape(27 * hidden_local, features)

    def total_rows(partial_value):
        return lax.psum(partial_value, "wide")

    pre_act = fine_conv(volume, fine_weight, False)
    activated = jax.nn.silu(pre_act).astype(jnp.bfloat16)
    received = send_patches(activated)
    merged = total_rows(jnp.dot(received, merge_weight, preferred_element_type=jnp.float32))
    coarse_in = merged.astype(jnp.bfloat16).reshape(coarse_grid + (features,))
    bias_row = step_table[timestep[0]]
    gate_pre = wide_input_conv(coarse_in, hidden_mat, hidden_local, False) + bias_row
    hidden_act = jax.nn.silu(gate_pre).astype(jnp.bfloat16)
    branch = total_rows(narrow_input_conv(hidden_act, output_mat, False).reshape(-1, features))
    residual_sum = (merged + branch).astype(jnp.bfloat16)
    expanded = jnp.dot(residual_sum, expand_weight, preferred_element_type=jnp.float32).astype(
        jnp.bfloat16
    )
    expanded_field = return_patches(expanded, fine_height, fine_depth, channels)
    combined = activated.astype(jnp.float32) + expanded_field.astype(jnp.float32)
    grad_comb = (cotangent.astype(jnp.float32) * silu_slope(combined)).astype(jnp.bfloat16)
    grad_res = total_rows(
        jnp.einsum(
            "nk,dk->nd", send_patches(grad_comb), expand_weight, preferred_element_type=jnp.float32
        )
    )
    grad_res_b = grad_res.astype(jnp.bfloat16).reshape(coarse_grid + (features,))
    grad_hidden = wide_input_conv(grad_res_b, output_back, hidden_local, True)
    grad_gate = (grad_hidden * silu_slope(gate_pre)).astype(jnp.bfloat16)
    grad_conv = total_rows(narrow_input_conv(grad_gate, hidden_back, True).reshape(-1, features))
    grad_merged = (grad_res + grad_conv).astype(jnp.bfloat16)
    grad_cells = jnp.einsum(
        "nd,kd->nk", grad_merged, merge_weight, preferred_element_type=jnp.float32
    ).astype(jnp.bfloat16)
    grad_act = return_patches(grad_cells, fine_height, fine_depth, channels).astype(
        jnp.float32
    ) + grad_comb.astype(jnp.float32)
    grad_pre = (grad_act * silu_slope(pre_act)).astype(jnp.bfloat16)
    return fine_conv(grad_pre, fine_weight.transpose(0, 2, 1), True).astype(jnp.bfloat16)


def solution(mesh):
    in_specs = (
        P(None, ("groups", "wide"), None, "narrow"),
        P(None, ("groups", "wide"), None, "narrow"),
        P(),
        P("wide", None),
        P(None, None, "wide"),
        P(None, "wide"),
        P(None, "wide", None),
        P(None, "wide"),
        P("groups"),
    )
    out_specs = P(None, ("groups", "wide"), None, "narrow")
    sizes = dict(mesh.shape)
    fits = sizes["wide"] == PATCH and sizes["narrow"] == 2
    body = eight_shards if fits else shards
    return jax.shard_map(body, mesh=mesh, in_specs=in_specs, out_specs=out_specs, check_vma=False)
```

```python
import functools

import jax
import jax.numpy as jnp
from jax import lax
from jax.experimental import pallas as pl
from jax.experimental.pallas import tpu as pltpu
from jax.sharding import PartitionSpec as P

PATCH = 8


def extended(cells, sides, width):
    for axis, dim in sides:
        count = lax.axis_size(axis)
        ends = count - 1
        head = lax.slice_in_dim(cells, 0, width, axis=dim)
        tail = lax.slice_in_dim(cells, cells.shape[dim] - width, cells.shape[dim], axis=dim)
        cells = jnp.concatenate(
            [
                lax.ppermute(tail, axis, [(i, (i + 1) % count) for i in range(ends)]),
                cells,
                lax.ppermute(head, axis, [((i + 1) % count, i) for i in range(ends)]),
            ],
            axis=dim,
        )
    return cells


def shifts(transposed):
    return [
        (2 - i, 2 - j, 2 - k) if transposed else (i, j, k)
        for i in range(3)
        for j in range(3)
        for k in range(3)
    ]


def silu_slope(values):
    logistic = jax.nn.sigmoid(values)
    return logistic * (1.0 + values * (1.0 - logistic))


def fine_conv(fine_field, weight, transposed):
    grown = extended(fine_field, (("wide", 1), ("narrow", 3)), 1)
    padded = jnp.pad(grown, ((0, 0), (0, 0), (1, 1), (0, 0)))
    kernel = weight.reshape(3, 3, 3, weight.shape[1], weight.shape[2])
    if transposed:
        kernel = kernel[::-1, ::-1, ::-1]
    result = lax.conv_general_dilated(
        padded[None],
        kernel,
        (1, 1, 1),
        "VALID",
        dimension_numbers=("NCDHW", "DHWIO", "NCDHW"),
        preferred_element_type=jnp.float32,
    )
    return result[0]


def to_patches(fine_field):
    channels = fine_field.shape[0]
    shaped = fine_field.reshape(
        channels, PATCH, fine_field.shape[2] // PATCH, PATCH, fine_field.shape[3] // PATCH, PATCH
    )
    return shaped.transpose(2, 4, 1, 3, 5, 0).reshape(-1, PATCH**3 * channels)


def send_patches(fine_field):
    return lax.all_to_all(to_patches(fine_field), "wide", split_axis=1, concat_axis=0, tiled=True)


def return_patches(patch_rows, fine_height, fine_depth, channels):
    returned = lax.all_to_all(patch_rows, "wide", split_axis=0, concat_axis=1, tiled=True)
    shaped = returned.reshape(
        fine_height // PATCH, fine_depth // PATCH, PATCH, PATCH, PATCH, channels
    )
    return shaped.transpose(5, 2, 0, 3, 1, 4).reshape(channels, PATCH, fine_height, fine_depth)


def coarse_faces(coarse_block):
    return extended(coarse_block, (("narrow", 2),), 1)


def wide_input_conv(coarse_block, weight_mat, out_count, transposed):
    grown = coarse_faces(coarse_block)
    products = jnp.einsum("xyzd,dk->xyzk", grown, weight_mat, preferred_element_type=jnp.float32)
    padded = jnp.pad(products, ((1, 1), (1, 1), (0, 0), (0, 0)))
    extent = coarse_block.shape[:3]
    summed = jnp.zeros(extent + (out_count,), jnp.float32)
    for tap_index, (a, b, c) in enumerate(shifts(transposed)):
        summed = (
            summed
            + padded[
                a : a + extent[0],
                b : b + extent[1],
                c : c + extent[2],
                tap_index * out_count : (tap_index + 1) * out_count,
            ]
        )
    return summed


def narrow_input_conv(coarse_block, weight_mat, transposed):
    grown = coarse_faces(coarse_block)
    padded = jnp.pad(grown, ((1, 1), (1, 1), (0, 0), (0, 0)))
    extent = coarse_block.shape[:3]
    columns = jnp.concatenate(
        [
            padded[a : a + extent[0], b : b + extent[1], c : c + extent[2]]
            for a, b, c in shifts(transposed)
        ],
        axis=3,
    )
    return jnp.einsum("xyzk,kd->xyzd", columns, weight_mat, preferred_element_type=jnp.float32)


BF = jnp.bfloat16
F32 = jnp.float32
LIMIT = 10 * 1024 * 1024
BESIDE = 32 * 1024 * 1024
VMEM = pl.BlockSpec(memory_space=pltpu.VMEM)
SMEM = pl.BlockSpec(memory_space=pltpu.SMEM)


def nn_dot(lhs, rhs):
    return jnp.dot(lhs, rhs, preferred_element_type=F32)


def nt_dot(lhs, rhs):
    return lax.dot_general(lhs, rhs, (((1,), (1,)), ((), ())), preferred_element_type=F32)


def shape_of(dims, dtype):
    return jax.ShapeDtypeStruct(dims, dtype)


def kernel_call(kernel, places, arrays, outs, scratch=(), cost=None, rest=()):
    return pl.pallas_call(
        kernel,
        in_specs=[SMEM] * len(places) + [VMEM] * len(arrays) + [pl.BlockSpec(memory_space=pl.ANY)] * len(rest),
        out_specs=[VMEM] * len(outs),
        out_shape=outs,
        scratch_shapes=list(scratch),
        cost_estimate=cost and pl.CostEstimate(flops=0, bytes_accessed=cost, transcendentals=0),
        compiler_params=pltpu.CompilerParams(vmem_limit_bytes=LIMIT),
    )(*places, *arrays, *[pltpu.with_memory_space_constraint(a, pltpu.HBM) for a in rest])


def band_kernel(weight_ref, out_ref, *, back):
    row = lax.broadcasted_iota(jnp.int32, (32, 256), 0)
    lane = lax.broadcasted_iota(jnp.int32, (32, 256), 1)
    places = [(lane == row + 32 * (2 - k)).astype(BF) for k in range(3)]
    same = (
        lax.broadcasted_iota(jnp.int32, (32, 32), 0) == lax.broadcasted_iota(jnp.int32, (32, 32), 1)
    ).astype(BF)
    for i in range(3):
        for j in range(3):
            taps = None
            for k in range(3):
                t = 9 * i + 3 * j + k
                tap = nt_dot(same, weight_ref[26 - t]).astype(BF) if back else weight_ref[t]
                part = nn_dot(tap, places[k])
                taps = part if taps is None else taps + part
            columns = slice(256 * j, 256 * j + 256)

            def placed(start):
                moved = pltpu.roll(taps, start % 256, 1)
                return jnp.where((lane >= start) & (lane < start + 96), moved, 0.0).astype(BF)

            for d in range(8):
                out_ref[256 * i + 32 * d : 256 * i + 32 * d + 32, columns] = placed(32 * (d - 1))
            out_ref[768 + 64 * i : 800 + 64 * i, columns] = placed(-64)
            out_ref[800 + 64 * i : 832 + 64 * i, columns] = placed(224)
    out_ref[960:1024, :] = jnp.zeros((64, 768), BF)


def banded(weight, back):
    (out,) = kernel_call(
        functools.partial(band_kernel, back=back), (), (weight,), [shape_of((1024, 768), BF)], cost=BESIDE
    )
    return out


def pack_kernel(n_ref, w_ref, step_ref, field_ref, cot_ref, out_ref):
    del n_ref, w_ref, step_ref
    for a in range(8):
        out_ref[a, 0:32] = field_ref[(a + 7) % 8]
        out_ref[a, 32:64] = field_ref[a]
        out_ref[a, 64:96] = field_ref[(a + 1) % 8]
        out_ref[a, 96:128] = cot_ref[a]


def arrived_planes(w, arrived_ref):
    none = jnp.zeros((32, 256), BF)
    before, own, after = [
        arrived_ref[:, 32 * s : 32 * s + 32, :].reshape(256, 256) for s in range(3)
    ]
    before = jnp.where(w == 0, jnp.concatenate([none, before[:224]], axis=0), before)
    after = jnp.where(w == 7, jnp.concatenate([after[32:], none], axis=0), after)
    return before, own, after


def returned_planes(w, returned_ref):
    rows = [returned_ref[7, 32:64]] + [returned_ref[a, 0:32] for a in range(8)] + [returned_ref[0, 32:64]]
    grown = jnp.concatenate(rows, axis=0)
    return grown[0:256], grown[32:288], grown[64:320]


def side_kernel(w_ref, planes_ref, band_ref, own_ref, send_ref, *, planes_of):
    del band_ref
    planes = planes_of(w_ref[0], planes_ref)
    source = lax.broadcasted_iota(jnp.int32, (256, 256), 0)
    target = lax.broadcasted_iota(jnp.int32, (256, 256), 1)
    sides = None
    for i, plane in enumerate(planes):
        high = (source >= 224) & (target == source - 224 + 64 * i)
        low = (source < 32) & (target == source + 64 * i + 32)
        part = nn_dot(plane, (high | low).astype(BF))
        sides = part if sides is None else sides + part
    even = (source & 1) == 0
    sides = jnp.where(even, pltpu.roll(sides, 255, 0), pltpu.roll(sides, 1, 0))
    low_side = (target & 32) != 0
    own = even == low_side
    zero = jnp.zeros_like(sides)
    own_ref[...] = jnp.where(own, sides, zero).astype(BF)
    send_ref[...] = jnp.where(own, zero, sides).astype(BF)


def side_call(w, planes, band, planes_of):
    shape = shape_of((256, 256), BF)
    return kernel_call(
        functools.partial(side_kernel, planes_of=planes_of), (w,), (planes, band), [shape, shape]
    )


def fine_sum(n, planes, own_ref, got_ref, band_ref):
    lane = lax.broadcasted_iota(jnp.int32, (256, 256), 1)
    keep = ((lane & 32) != 0) == (n == 0)
    got = jnp.where(keep, got_ref[...].astype(F32), jnp.zeros((256, 256), F32))
    sides = (own_ref[...].astype(F32) + got).astype(BF)
    lhs = jnp.concatenate([*planes, sides], axis=1)
    total = nn_dot(lhs, band_ref[:, 256:512])
    y = (lax.broadcasted_iota(jnp.int32, (256, 1), 0) >> 1) & 15
    zero = jnp.zeros_like(total)
    below = pltpu.roll(nn_dot(lhs, band_ref[:, 0:256]), 2, 0)
    above = pltpu.roll(nn_dot(lhs, band_ref[:, 512:768]), 254, 0)
    return total + jnp.where(y > 0, below, zero) + jnp.where(y < 15, above, zero)


def cell_rows(ref, b):
    return jnp.concatenate([ref[pl.ds(2 * b + z, 16, stride=16), :] for z in range(2)], axis=0)


def merge_kernel(
    n_ref, w_ref, planes_ref, own_ref, got_ref, band_ref, merge_ref, pre_ref, act_ref, sum_ref, sum_b_ref,
    rows_ref, weight_ref, sems
):
    n = n_ref[0]
    copies = []
    for b in range(8):
        place = pl.ds(256 * b, 256)
        copies.append(pltpu.make_async_copy(merge_ref.at[place], weight_ref.at[place], sems.at[b]))
        copies[b].start()
    planes = arrived_planes(w_ref[0], planes_ref)
    wide_rows = fine_sum(n, planes, own_ref, got_ref, band_ref)
    rows_ref[0] = wide_rows[:, :128]
    rows_ref[1] = wide_rows[:, 128:]
    total = None
    for b in range(8):
        pre = jnp.concatenate([cell_rows(rows_ref.at[h], b) for h in range(2)], axis=1)
        pre_ref[b] = pre
        act = (pre * jax.nn.sigmoid(pre)).astype(BF)
        act_ref[b] = act
        copies[b].wait()
        part = nn_dot(act, weight_ref[256 * b : 256 * b + 256])
        total = part if total is None else total + part
    sum_ref[...] = total
    sum_b_ref[...] = total.astype(BF)


def cot_kernel(planes_ref, cot_ref, rows_ref):
    rows = planes_ref[:, 96:128, :].reshape(256, 256).astype(F32)
    rows_ref[0] = rows[:, :128]
    rows_ref[1] = rows[:, 128:]
    for b in range(8):
        cot_ref[b] = jnp.concatenate([cell_rows(rows_ref.at[h], b) for h in range(2)], axis=1).astype(BF)


def final_kernel(n_ref, w_ref, planes_ref, own_ref, got_ref, band_ref, out_ref):
    planes = returned_planes(w_ref[0], planes_ref)
    out_ref[...] = fine_sum(n_ref[0], planes, own_ref, got_ref, band_ref).astype(BF)


def put_columns(cols_ref, cells):
    row = lax.broadcasted_iota(jnp.int32, (64, 1), 0)
    along_y, along_x = row & 1, (row >> 1) & 7
    zero = jnp.zeros_like(cells)
    none = jnp.zeros((16, cells.shape[1]), BF)
    below = jnp.where(along_y == 1, pltpu.roll(cells, 1, 0), zero)
    above = jnp.where(along_y == 0, pltpu.roll(cells, 63, 0), zero)
    for j, moved_y in enumerate((below, cells, above)):
        before = jnp.where(along_x > 0, pltpu.roll(moved_y, 2, 0), zero)
        after = jnp.where(along_x < 7, pltpu.roll(moved_y, 62, 0), zero)
        for i, moved in enumerate((before, moved_y, after)):
            rows = moved.astype(BF)
            cols_ref[9 * i + 3 * j] = jnp.concatenate([none, rows[:48]], axis=0)
            cols_ref[9 * i + 3 * j + 1] = rows
            cols_ref[9 * i + 3 * j + 2] = jnp.concatenate([rows[16:], none], axis=0)


def both_halves(n, mine, got, axis):
    first = n == 0
    return jnp.concatenate([jnp.where(first, mine, got), jnp.where(first, got, mine)], axis=axis)


def conv_sum(cols_ref, weight_of, flipped, dot):
    total = None
    for t in range(27):
        part = dot(cols_ref[26 - t if flipped else t], weight_of(t))
        total = part if total is None else total + part
    return total


def feature_rows(n, ref):
    half = ref.shape[1] // 2
    return lambda t: ref[t, pl.ds(pl.multiple_of(n * half, half), half), :]


def feature_columns(n, ref):
    half = ref.shape[2] // 2
    return lambda t: ref[t, :, pl.ds(pl.multiple_of(n * half, half), half)]


def outer_kernel(n_ref, mine_ref, got_ref, weight_ref, sum_ref, cols_ref, *, flipped, dot, part_of):
    n = n_ref[0]
    put_columns(cols_ref, both_halves(n, mine_ref[...].astype(F32), got_ref[...].astype(F32), 0))
    sum_ref[...] = conv_sum(cols_ref, part_of(n, weight_ref), flipped, dot)


def inner_forward_kernel(
    n_ref, step_ref, mine_ref, got_ref, weight_ref, table_ref, gate_ref, sum_ref, sum_b_ref, cols_ref, bias_ref, sem
):
    step = step_ref[0]
    group = pl.ds(pl.multiple_of(step // 8 * 8, 8), 8)
    fetch = pltpu.make_async_copy(table_ref.at[group], bias_ref, sem)
    fetch.start()
    fetch.wait()
    rows = bias_ref[...]
    chosen = lax.broadcasted_iota(jnp.int32, rows.shape, 0) == step % 8
    bias = jnp.sum(jnp.where(chosen, rows, jnp.zeros_like(rows)), axis=0, keepdims=True)
    gate = mine_ref[...] + got_ref[...] + bias
    gate_ref[...] = gate
    put_columns(cols_ref, gate * jax.nn.sigmoid(gate))
    total = conv_sum(cols_ref, feature_columns(n_ref[0], weight_ref), False, nn_dot)
    sum_ref[...] = total
    sum_b_ref[...] = total.astype(BF)


def inner_backward_kernel(
    n_ref, mine_ref, got_ref, gate_ref, weight_ref, sum_ref, sum_b_ref, cols_ref
):
    put_columns(cols_ref, (mine_ref[...] + got_ref[...]) * silu_slope(gate_ref[...]))
    total = conv_sum(cols_ref, feature_rows(n_ref[0], weight_ref), True, nt_dot)
    sum_ref[...] = total
    sum_b_ref[...] = total.astype(BF)


def expand_kernel(
    n_ref, merged_ref, mine_ref, got_ref, act_ref, cot_ref, expand_ref, grad_ref, sum_ref, sum_b_ref
):
    branch = both_halves(n_ref[0], mine_ref[...].astype(F32), got_ref[...].astype(F32), 1)
    residual = (merged_ref[...] + branch).astype(BF)
    total = None
    for b in range(8):
        part = expand_ref[:, 256 * b : 256 * b + 256]
        expanded = nn_dot(residual, part).astype(BF)
        combined = act_ref[b].astype(F32) + expanded.astype(F32)
        grad = (cot_ref[b].astype(F32) * silu_slope(combined)).astype(BF)
        grad_ref[b] = grad
        more = nt_dot(grad, part)
        total = more if total is None else total + more
    sum_ref[...] = total
    sum_b_ref[...] = total.astype(BF)


def grad_kernel(
    n_ref, w_ref, res_ref, mine_ref, got_ref, comb_ref, pre_ref, merge_ref, out_ref, rows_ref
):
    w = w_ref[0]
    conv = both_halves(n_ref[0], mine_ref[...].astype(F32), got_ref[...].astype(F32), 1)
    merged_grad = (res_ref[...] + conv).astype(BF)
    for b in range(8):
        cells = nt_dot(merged_grad, merge_ref[256 * b : 256 * b + 256]).astype(BF)
        grad = cells.astype(F32) + comb_ref[b].astype(F32)
        grad = grad * silu_slope(pre_ref[b])
        for z in range(2):
            for h in range(2):
                rows_ref[h, pl.ds(2 * b + z, 16, stride=16), :] = grad[
                    16 * z : 16 * z + 16, 128 * h : 128 * h + 128
                ]
    rows = jnp.concatenate([rows_ref[0], rows_ref[1]], axis=1).astype(BF)
    none = jnp.zeros((32, 256), BF)
    for x in range(8):
        ahead = rows[32 * x + 32 : 32 * x + 64] if x < 7 else none
        behind = rows[32 * x - 32 : 32 * x] if x > 0 else none
        out_ref[x, 0:32] = rows[32 * x : 32 * x + 32]
        out_ref[x, 32:64] = jnp.where(w == 0, ahead, behind)


def swap_narrow(value):
    return lax.ppermute(value, "narrow", [(0, 1), (1, 0)])


def pair_kernel(part_ref, got_ref, *refs):
    pair_ref, pair_b_ref = refs[-2:]
    pair = part_ref[...] + got_ref[...].astype(F32)
    pair_ref[...] = pair
    pair_b_ref[...] = pair.astype(BF)


def features_kernel(n_ref, pair_ref, one_ref, two_ref, three_ref, *refs):
    sum_ref, mine_ref, send_ref = refs[-3:]
    total = pair_ref[...] + one_ref[...].astype(F32) + two_ref[...].astype(F32) + three_ref[...].astype(F32)
    sum_ref[...] = total
    half = total.shape[1] // 2
    low, high = total[:, :half], total[:, half:]
    first = n_ref[0] == 0
    mine_ref[...] = jnp.where(first, low, high).astype(BF)
    send_ref[...] = jnp.where(first, high, low).astype(BF)


def cells_kernel(n_ref, pair_ref, one_ref, two_ref, three_ref, mine_ref, send_ref):
    total = pair_ref[...] + one_ref[...].astype(F32) + two_ref[...].astype(F32) + three_ref[...].astype(F32)
    half = total.shape[0] // 2
    low, high = total[:half], total[half:]
    first = n_ref[0] == 0
    mine_ref[...] = jnp.where(first, low, high)
    send_ref[...] = jnp.where(first, high, low).astype(BF)


def wide_terms(part, part_b, rest=()):
    def partner(value, mask):
        return lax.ppermute(value, "wide", [(i, i ^ mask) for i in range(8)])

    shape = part.shape
    pair, pair_b = kernel_call(
        pair_kernel, (), (part, partner(part_b, 1)), [shape_of(shape, F32), shape_of(shape, BF)], rest=rest
    )
    return (pair, *[partner(pair_b, mask) for mask in (2, 4, 6)])


def to_feature_halves(n, part, part_b, rest=()):
    terms = wide_terms(part, part_b, rest)
    cells, features = part.shape
    half_shape = shape_of((cells, features // 2), BF)
    total, mine, send = kernel_call(
        features_kernel, (n,), terms, [shape_of(part.shape, F32), half_shape, half_shape], rest=rest
    )
    return total, mine, swap_narrow(send)


def to_cell_halves(n, part, part_b):
    terms = wide_terms(part, part_b)
    cells, features = part.shape
    half = (cells // 2, features)
    mine, send = kernel_call(cells_kernel, (n,), terms, [shape_of(half, F32), shape_of(half, BF)])
    return mine, swap_narrow(send)


def across_wide(value):
    return lax.all_to_all(value, "wide", split_axis=0, concat_axis=0, tiled=True)


def eight_shards(
    volume,
    cotangent,
    fine_weight,
    merge_weight,
    hidden_weight,
    step_table,
    output_weight,
    expand_weight,
    timestep,
):
    features = merge_weight.shape[1]
    hidden = hidden_weight.shape[2]
    half = features // 2
    w = lax.axis_index("wide").astype(jnp.int32).reshape(1)
    n = lax.axis_index("narrow").astype(jnp.int32).reshape(1)

    def row_form(fine_field):
        return fine_field.transpose(1, 2, 3, 0).reshape(8, 32, 256)

    (outgoing,) = kernel_call(
        pack_kernel, (n, w, timestep), (row_form(volume), row_form(cotangent)), [shape_of((8, 128, 256), BF)]
    )
    arrived = across_wide(outgoing)
    band = banded(fine_weight, False)
    sides, sent = side_call(w, arrived, band, arrived_planes)
    fine_rows = pltpu.VMEM((2, 256, 128), F32)
    sum_shapes = [shape_of((32, features), F32), shape_of((32, features), BF)]
    pre_act, act, merged_part, merged_part_b = kernel_call(
        merge_kernel,
        (n, w),
        (arrived, sides, swap_narrow(sent), band),
        [shape_of((8, 32, 256), F32), shape_of((8, 32, 256), BF)] + sum_shapes,
        [fine_rows, pltpu.VMEM(merge_weight.shape, BF), pltpu.SemaphoreType.DMA((8,))],
        rest=(merge_weight,),
    )
    (cot,) = kernel_call(cot_kernel, (), (arrived,), [shape_of((8, 32, 256), BF)], [fine_rows])
    merged, mine, got = to_feature_halves(n, merged_part, merged_part_b, (hidden_weight,))

    gate_shape = shape_of((64, hidden), F32)
    half_shapes = [shape_of((64, half), F32), shape_of((64, half), BF)]
    outer_columns = [pltpu.VMEM((27, 64, half), BF)]
    inner_columns = [pltpu.VMEM((27, 64, hidden), BF)]

    (gate_part,) = kernel_call(
        functools.partial(outer_kernel, flipped=False, dot=nn_dot, part_of=feature_rows),
        (n,), (mine, got, hidden_weight), [gate_shape], outer_columns,
    )
    gate_pre, branch_part, branch_part_b = kernel_call(
        inner_forward_kernel,
        (n, timestep), (gate_part, swap_narrow(gate_part), output_weight), [gate_shape] + half_shapes,
        inner_columns + [pltpu.VMEM((8, hidden), F32), pltpu.SemaphoreType.DMA], rest=(step_table,),
    )
    mine, got = to_cell_halves(n, branch_part, branch_part_b)
    grad_comb, res_part, res_part_b = kernel_call(
        expand_kernel,
        (n,), (merged, mine, got, act, cot, expand_weight),
        [shape_of((8, 32, 256), BF)] + sum_shapes,
    )
    grad_res, mine, got = to_feature_halves(n, res_part, res_part_b)
    (hidden_part,) = kernel_call(
        functools.partial(outer_kernel, flipped=True, dot=nt_dot, part_of=feature_columns),
        (n,), (mine, got, output_weight), [gate_shape], outer_columns,
    )
    conv_part, conv_part_b = kernel_call(
        inner_backward_kernel,
        (n,), (hidden_part, swap_narrow(hidden_part), gate_pre, hidden_weight),
        half_shapes, inner_columns,
    )
    mine, got = to_cell_halves(n, conv_part, conv_part_b)
    (leaving,) = kernel_call(
        grad_kernel,
        (n, w), (grad_res, mine, got, grad_comb, pre_act, merge_weight),
        [shape_of((8, 64, 256), BF)], [fine_rows],
    )
    returned = across_wide(leaving)
    band = banded(fine_weight, True)
    sides, sent = side_call(w, returned, band, returned_planes)
    (result,) = kernel_call(
        final_kernel,
        (n, w), (returned, sides, swap_narrow(sent), band),
        [shape_of((256, 256), BF)],
    )
    return result.reshape(8, 16, 16, 32).transpose(3, 0, 1, 2)


def shards(
    volume,
    cotangent,
    fine_weight,
    merge_weight,
    hidden_weight,
    step_table,
    output_weight,
    expand_weight,
    timestep,
):
    channels = volume.shape[0]
    fine_height = volume.shape[2]
    fine_depth = volume.shape[3]
    wide_count = lax.axis_size("wide")
    features = merge_weight.shape[1]
    hidden_local = hidden_weight.shape[2]
    coarse_grid = (wide_count, fine_height // PATCH, fine_depth // PATCH)
    hidden_mat = hidden_weight.transpose(1, 0, 2).reshape(features, 27 * hidden_local)
    output_mat = output_weight.reshape(27 * hidden_local, features)
    output_back = output_weight.transpose(2, 0, 1).reshape(features, 27 * hidden_local)
    hidden_back = hidden_weight.transpose(0, 2, 1).reshape(27 * hidden_local, features)

    def total_rows(partial_value):
        return lax.psum(partial_value, "wide")

    pre_act = fine_conv(volume, fine_weight, False)
    activated = jax.nn.silu(pre_act).astype(jnp.bfloat16)
    received = send_patches(activated)
    merged = total_rows(jnp.dot(received, merge_weight, preferred_element_type=jnp.float32))
    coarse_in = merged.astype(jnp.bfloat16).reshape(coarse_grid + (features,))
    bias_row = step_table[timestep[0]]
    gate_pre = wide_input_conv(coarse_in, hidden_mat, hidden_local, False) + bias_row
    hidden_act = jax.nn.silu(gate_pre).astype(jnp.bfloat16)
    branch = total_rows(narrow_input_conv(hidden_act, output_mat, False).reshape(-1, features))
    residual_sum = (merged + branch).astype(jnp.bfloat16)
    expanded = jnp.dot(residual_sum, expand_weight, preferred_element_type=jnp.float32).astype(
        jnp.bfloat16
    )
    expanded_field = return_patches(expanded, fine_height, fine_depth, channels)
    combined = activated.astype(jnp.float32) + expanded_field.astype(jnp.float32)
    grad_comb = (cotangent.astype(jnp.float32) * silu_slope(combined)).astype(jnp.bfloat16)
    grad_res = total_rows(
        jnp.einsum(
            "nk,dk->nd", send_patches(grad_comb), expand_weight, preferred_element_type=jnp.float32
        )
    )
    grad_res_b = grad_res.astype(jnp.bfloat16).reshape(coarse_grid + (features,))
    grad_hidden = wide_input_conv(grad_res_b, output_back, hidden_local, True)
    grad_gate = (grad_hidden * silu_slope(gate_pre)).astype(jnp.bfloat16)
    grad_conv = total_rows(narrow_input_conv(grad_gate, hidden_back, True).reshape(-1, features))
    grad_merged = (grad_res + grad_conv).astype(jnp.bfloat16)
    grad_cells = jnp.einsum(
        "nd,kd->nk", grad_merged, merge_weight, preferred_element_type=jnp.float32
    ).astype(jnp.bfloat16)
    grad_act = return_patches(grad_cells, fine_height, fine_depth, channels).astype(
        jnp.float32
    ) + grad_comb.astype(jnp.float32)
    grad_pre = (grad_act * silu_slope(pre_act)).astype(jnp.bfloat16)
    return fine_conv(grad_pre, fine_weight.transpose(0, 2, 1), True).astype(jnp.bfloat16)


def solution(mesh):
    in_specs = (
        P(None, ("groups", "wide"), None, "narrow"),
        P(None, ("groups", "wide"), None, "narrow"),
        P(),
        P("wide", None),
        P(None, None, "wide"),
        P(None, "wide"),
        P(None, "wide", None),
        P(None, "wide"),
        P("groups"),
    )
    out_specs = P(None, ("groups", "wide"), None, "narrow")
    sizes = dict(mesh.shape)
    fits = sizes["wide"] == PATCH and sizes["narrow"] == 2
    body = eight_shards if fits else shards
    return jax.shard_map(body, mesh=mesh, in_specs=in_specs, out_specs=out_specs, check_vma=False)
```

```python
import functools

import jax
import jax.numpy as jnp
from jax import lax
from jax.experimental import pallas as pl
from jax.experimental.pallas import tpu as pltpu
from jax.sharding import PartitionSpec as P

PATCH = 8


def extended(cells, sides, width):
    for axis, dim in sides:
        count = lax.axis_size(axis)
        ends = count - 1
        head = lax.slice_in_dim(cells, 0, width, axis=dim)
        tail = lax.slice_in_dim(cells, cells.shape[dim] - width, cells.shape[dim], axis=dim)
        cells = jnp.concatenate(
            [
                lax.ppermute(tail, axis, [(i, (i + 1) % count) for i in range(ends)]),
                cells,
                lax.ppermute(head, axis, [((i + 1) % count, i) for i in range(ends)]),
            ],
            axis=dim,
        )
    return cells


def shifts(transposed):
    return [
        (2 - i, 2 - j, 2 - k) if transposed else (i, j, k)
        for i in range(3)
        for j in range(3)
        for k in range(3)
    ]


def silu_slope(values):
    logistic = jax.nn.sigmoid(values)
    return logistic * (1.0 + values * (1.0 - logistic))


def fine_conv(fine_field, weight, transposed):
    grown = extended(fine_field, (("wide", 1), ("narrow", 3)), 1)
    padded = jnp.pad(grown, ((0, 0), (0, 0), (1, 1), (0, 0)))
    kernel = weight.reshape(3, 3, 3, weight.shape[1], weight.shape[2])
    if transposed:
        kernel = kernel[::-1, ::-1, ::-1]
    result = lax.conv_general_dilated(
        padded[None],
        kernel,
        (1, 1, 1),
        "VALID",
        dimension_numbers=("NCDHW", "DHWIO", "NCDHW"),
        preferred_element_type=jnp.float32,
    )
    return result[0]


def to_patches(fine_field):
    channels = fine_field.shape[0]
    shaped = fine_field.reshape(
        channels, PATCH, fine_field.shape[2] // PATCH, PATCH, fine_field.shape[3] // PATCH, PATCH
    )
    return shaped.transpose(2, 4, 1, 3, 5, 0).reshape(-1, PATCH**3 * channels)


def send_patches(fine_field):
    return lax.all_to_all(to_patches(fine_field), "wide", split_axis=1, concat_axis=0, tiled=True)


def return_patches(patch_rows, fine_height, fine_depth, channels):
    returned = lax.all_to_all(patch_rows, "wide", split_axis=0, concat_axis=1, tiled=True)
    shaped = returned.reshape(
        fine_height // PATCH, fine_depth // PATCH, PATCH, PATCH, PATCH, channels
    )
    return shaped.transpose(5, 2, 0, 3, 1, 4).reshape(channels, PATCH, fine_height, fine_depth)


def coarse_faces(coarse_block):
    return extended(coarse_block, (("narrow", 2),), 1)


def wide_input_conv(coarse_block, weight_mat, out_count, transposed):
    grown = coarse_faces(coarse_block)
    products = jnp.einsum("xyzd,dk->xyzk", grown, weight_mat, preferred_element_type=jnp.float32)
    padded = jnp.pad(products, ((1, 1), (1, 1), (0, 0), (0, 0)))
    extent = coarse_block.shape[:3]
    summed = jnp.zeros(extent + (out_count,), jnp.float32)
    for tap_index, (a, b, c) in enumerate(shifts(transposed)):
        summed = (
            summed
            + padded[
                a : a + extent[0],
                b : b + extent[1],
                c : c + extent[2],
                tap_index * out_count : (tap_index + 1) * out_count,
            ]
        )
    return summed


def narrow_input_conv(coarse_block, weight_mat, transposed):
    grown = coarse_faces(coarse_block)
    padded = jnp.pad(grown, ((1, 1), (1, 1), (0, 0), (0, 0)))
    extent = coarse_block.shape[:3]
    columns = jnp.concatenate(
        [
            padded[a : a + extent[0], b : b + extent[1], c : c + extent[2]]
            for a, b, c in shifts(transposed)
        ],
        axis=3,
    )
    return jnp.einsum("xyzk,kd->xyzd", columns, weight_mat, preferred_element_type=jnp.float32)


BF = jnp.bfloat16
F32 = jnp.float32
LIMIT = 10 * 1024 * 1024
BESIDE = 32 * 1024 * 1024
VMEM = pl.BlockSpec(memory_space=pltpu.VMEM)
SMEM = pl.BlockSpec(memory_space=pltpu.SMEM)


def nn_dot(lhs, rhs):
    return jnp.dot(lhs, rhs, preferred_element_type=F32)


def nt_dot(lhs, rhs):
    return lax.dot_general(lhs, rhs, (((1,), (1,)), ((), ())), preferred_element_type=F32)


def shape_of(dims, dtype):
    return jax.ShapeDtypeStruct(dims, dtype)


def kernel_call(kernel, places, arrays, outs, scratch=(), cost=None, rest=()):
    return pl.pallas_call(
        kernel,
        in_specs=[SMEM] * len(places) + [VMEM] * len(arrays) + [pl.BlockSpec(memory_space=pl.ANY)] * len(rest),
        out_specs=[VMEM] * len(outs),
        out_shape=outs,
        scratch_shapes=list(scratch),
        cost_estimate=cost and pl.CostEstimate(flops=0, bytes_accessed=cost, transcendentals=0),
        compiler_params=pltpu.CompilerParams(vmem_limit_bytes=LIMIT),
    )(*places, *arrays, *[pltpu.with_memory_space_constraint(a, pltpu.HBM) for a in rest])


def band_kernel(weight_ref, out_ref, *, back):
    row = lax.broadcasted_iota(jnp.int32, (32, 256), 0)
    lane = lax.broadcasted_iota(jnp.int32, (32, 256), 1)
    places = [(lane == row + 32 * (2 - k)).astype(BF) for k in range(3)]
    same = (
        lax.broadcasted_iota(jnp.int32, (32, 32), 0) == lax.broadcasted_iota(jnp.int32, (32, 32), 1)
    ).astype(BF)
    for i in range(3):
        for j in range(3):
            taps = None
            for k in range(3):
                t = 9 * i + 3 * j + k
                tap = nt_dot(same, weight_ref[26 - t]).astype(BF) if back else weight_ref[t]
                part = nn_dot(tap, places[k])
                taps = part if taps is None else taps + part
            columns = slice(256 * j, 256 * j + 256)

            def placed(start):
                moved = pltpu.roll(taps, start % 256, 1)
                return jnp.where((lane >= start) & (lane < start + 96), moved, 0.0).astype(BF)

            for d in range(8):
                out_ref[256 * i + 32 * d : 256 * i + 32 * d + 32, columns] = placed(32 * (d - 1))
            out_ref[768 + 64 * i : 800 + 64 * i, columns] = placed(-64)
            out_ref[800 + 64 * i : 832 + 64 * i, columns] = placed(224)
    out_ref[960:1024, :] = jnp.zeros((64, 768), BF)


def band_and_bias_kernel(step_ref, weight_ref, table_ref, out_ref, bias_ref, rows_ref, sem):
    step = step_ref[0]
    group = pl.ds(pl.multiple_of(step // 8 * 8, 8), 8)
    fetch = pltpu.make_async_copy(table_ref.at[group], rows_ref, sem)
    fetch.start()
    band_kernel(weight_ref, out_ref, back=False)
    fetch.wait()
    rows = rows_ref[...]
    chosen = lax.broadcasted_iota(jnp.int32, rows.shape, 0) == step % 8
    bias_ref[...] = jnp.sum(jnp.where(chosen, rows, jnp.zeros_like(rows)), axis=0, keepdims=True)


def banded(weight, back):
    (out,) = kernel_call(
        functools.partial(band_kernel, back=back), (), (weight,), [shape_of((1024, 768), BF)], cost=BESIDE
    )
    return out


def lane_place(d):
    row = lax.broadcasted_iota(jnp.int32, (32, 256), 0)
    lane = lax.broadcasted_iota(jnp.int32, (32, 256), 1)
    return (lane == row + 32 * d).astype(BF)


def to_rows(field_ref, cells_ref):
    cells_ref[...] = field_ref[...].astype(F32).reshape(2048, 32)
    rows = None
    for d in range(8):
        part = nn_dot(cells_ref[pl.ds(d, 256, stride=8), :].astype(BF), lane_place(d))
        rows = part if rows is None else rows + part
    return rows.astype(BF)


def pack_kernel(n_ref, w_ref, step_ref, field_ref, cot_ref, out_ref, cells_ref, other_ref):
    del n_ref, w_ref, step_ref
    field = to_rows(field_ref, cells_ref)
    cot = to_rows(cot_ref, other_ref)
    for a in range(8):
        before, after = (a + 7) % 8, (a + 1) % 8
        out_ref[a, 0:32] = field[32 * before : 32 * before + 32]
        out_ref[a, 32:64] = field[32 * a : 32 * a + 32]
        out_ref[a, 64:96] = field[32 * after : 32 * after + 32]
        out_ref[a, 96:128] = cot[32 * a : 32 * a + 32]


def arrived_planes(w, arrived_ref):
    none = jnp.zeros((32, 256), BF)
    before, own, after = [
        arrived_ref[:, 32 * s : 32 * s + 32, :].reshape(256, 256) for s in range(3)
    ]
    before = jnp.where(w == 0, jnp.concatenate([none, before[:224]], axis=0), before)
    after = jnp.where(w == 7, jnp.concatenate([after[32:], none], axis=0), after)
    return before, own, after


def returned_planes(w, returned_ref):
    rows = [returned_ref[7, 32:64]] + [returned_ref[a, 0:32] for a in range(8)] + [returned_ref[0, 32:64]]
    grown = jnp.concatenate(rows, axis=0)
    return grown[0:256], grown[32:288], grown[64:320]


def side_kernel(w_ref, planes_ref, band_ref, *refs, planes_of):
    del band_ref
    own_ref, send_ref = refs[-2:]
    planes = planes_of(w_ref[0], planes_ref)
    source = lax.broadcasted_iota(jnp.int32, (256, 256), 0)
    target = lax.broadcasted_iota(jnp.int32, (256, 256), 1)
    sides = None
    for i, plane in enumerate(planes):
        high = (source >= 224) & (target == source - 224 + 64 * i)
        low = (source < 32) & (target == source + 64 * i + 32)
        part = nn_dot(plane, (high | low).astype(BF))
        sides = part if sides is None else sides + part
    even = (source & 1) == 0
    sides = jnp.where(even, pltpu.roll(sides, 255, 0), pltpu.roll(sides, 1, 0))
    low_side = (target & 32) != 0
    own = even == low_side
    zero = jnp.zeros_like(sides)
    own_ref[...] = jnp.where(own, sides, zero).astype(BF)
    send_ref[...] = jnp.where(own, zero, sides).astype(BF)


def side_call(w, planes, band, planes_of, rest=()):
    shape = shape_of((256, 256), BF)
    return kernel_call(
        functools.partial(side_kernel, planes_of=planes_of), (w,), (planes, band), [shape, shape], rest=rest
    )


def fine_sum(n, planes, own_ref, got_ref, band_ref):
    lane = lax.broadcasted_iota(jnp.int32, (256, 256), 1)
    keep = ((lane & 32) != 0) == (n == 0)
    got = jnp.where(keep, got_ref[...].astype(F32), jnp.zeros((256, 256), F32))
    sides = (own_ref[...].astype(F32) + got).astype(BF)
    lhs = jnp.concatenate([*planes, sides], axis=1)
    total = nn_dot(lhs, band_ref[:, 256:512])
    y = (lax.broadcasted_iota(jnp.int32, (256, 1), 0) >> 1) & 15
    zero = jnp.zeros_like(total)
    below = pltpu.roll(nn_dot(lhs, band_ref[:, 0:256]), 2, 0)
    above = pltpu.roll(nn_dot(lhs, band_ref[:, 512:768]), 254, 0)
    return total + jnp.where(y > 0, below, zero) + jnp.where(y < 15, above, zero)


def cell_rows(ref, b):
    return jnp.concatenate([ref[pl.ds(2 * b + z, 16, stride=16), :] for z in range(2)], axis=0)


def merge_kernel(
    n_ref, w_ref, planes_ref, own_ref, got_ref, band_ref, merge_ref, pre_ref, act_ref, sum_ref, sum_b_ref, rows_ref
):
    n = n_ref[0]
    planes = arrived_planes(w_ref[0], planes_ref)
    wide_rows = fine_sum(n, planes, own_ref, got_ref, band_ref)
    rows_ref[0] = wide_rows[:, :128]
    rows_ref[1] = wide_rows[:, 128:]
    total = None
    for b in range(8):
        pre = jnp.concatenate([cell_rows(rows_ref.at[h], b) for h in range(2)], axis=1)
        pre_ref[b] = pre
        act = (pre * jax.nn.sigmoid(pre)).astype(BF)
        act_ref[b] = act
        part = nn_dot(act, merge_ref[256 * b : 256 * b + 256])
        total = part if total is None else total + part
    sum_ref[...] = total
    sum_b_ref[...] = total.astype(BF)


def cot_kernel(planes_ref, cot_ref, rows_ref):
    rows = planes_ref[:, 96:128, :].reshape(256, 256).astype(F32)
    rows_ref[0] = rows[:, :128]
    rows_ref[1] = rows[:, 128:]
    for b in range(8):
        cot_ref[b] = jnp.concatenate([cell_rows(rows_ref.at[h], b) for h in range(2)], axis=1).astype(BF)


def final_kernel(n_ref, w_ref, planes_ref, own_ref, got_ref, band_ref, out_ref, cells_ref):
    planes = returned_planes(w_ref[0], planes_ref)
    rows = fine_sum(n_ref[0], planes, own_ref, got_ref, band_ref).astype(BF)
    for d in range(8):
        cells_ref[pl.ds(d, 256, stride=8), :] = nt_dot(rows, lane_place(d))
    out_ref[...] = cells_ref[...].astype(BF).reshape(8, 16, 16, 32)


def put_columns(cols_ref, cells):
    row = lax.broadcasted_iota(jnp.int32, (64, 1), 0)
    along_y, along_x = row & 1, (row >> 1) & 7
    zero = jnp.zeros_like(cells)
    none = jnp.zeros((16, cells.shape[1]), BF)
    below = jnp.where(along_y == 1, pltpu.roll(cells, 1, 0), zero)
    above = jnp.where(along_y == 0, pltpu.roll(cells, 63, 0), zero)
    for j, moved_y in enumerate((below, cells, above)):
        before = jnp.where(along_x > 0, pltpu.roll(moved_y, 2, 0), zero)
        after = jnp.where(along_x < 7, pltpu.roll(moved_y, 62, 0), zero)
        for i, moved in enumerate((before, moved_y, after)):
            rows = moved.astype(BF)
            cols_ref[9 * i + 3 * j] = jnp.concatenate([none, rows[:48]], axis=0)
            cols_ref[9 * i + 3 * j + 1] = rows
            cols_ref[9 * i + 3 * j + 2] = jnp.concatenate([rows[16:], none], axis=0)


def both_halves(n, mine, got, axis):
    first = n == 0
    return jnp.concatenate([jnp.where(first, mine, got), jnp.where(first, got, mine)], axis=axis)


def conv_sum(cols_ref, weight_of, flipped, dot):
    total = None
    for t in range(27):
        part = dot(cols_ref[26 - t if flipped else t], weight_of(t))
        total = part if total is None else total + part
    return total


def feature_rows(n, ref):
    half = ref.shape[1] // 2
    return lambda t: ref[t, pl.ds(pl.multiple_of(n * half, half), half), :]


def feature_columns(n, ref):
    half = ref.shape[2] // 2
    return lambda t: ref[t, :, pl.ds(pl.multiple_of(n * half, half), half)]


def outer_kernel(n_ref, mine_ref, got_ref, weight_ref, sum_ref, cols_ref, *, flipped, dot, part_of):
    n = n_ref[0]
    put_columns(cols_ref, both_halves(n, mine_ref[...].astype(F32), got_ref[...].astype(F32), 0))
    sum_ref[...] = conv_sum(cols_ref, part_of(n, weight_ref), flipped, dot)


def inner_forward_kernel(
    n_ref, mine_ref, got_ref, bias_ref, weight_ref, gate_ref, sum_ref, sum_b_ref, cols_ref
):
    gate = mine_ref[...] + got_ref[...] + bias_ref[...]
    gate_ref[...] = gate
    put_columns(cols_ref, gate * jax.nn.sigmoid(gate))
    total = conv_sum(cols_ref, feature_columns(n_ref[0], weight_ref), False, nn_dot)
    sum_ref[...] = total
    sum_b_ref[...] = total.astype(BF)


def inner_backward_kernel(
    n_ref, mine_ref, got_ref, gate_ref, weight_ref, sum_ref, sum_b_ref, cols_ref
):
    put_columns(cols_ref, (mine_ref[...] + got_ref[...]) * silu_slope(gate_ref[...]))
    total = conv_sum(cols_ref, feature_rows(n_ref[0], weight_ref), True, nt_dot)
    sum_ref[...] = total
    sum_b_ref[...] = total.astype(BF)


def expand_kernel(
    n_ref, merged_ref, mine_ref, got_ref, act_ref, cot_ref, expand_ref, grad_ref, sum_ref, sum_b_ref
):
    branch = both_halves(n_ref[0], mine_ref[...].astype(F32), got_ref[...].astype(F32), 1)
    residual = (merged_ref[...] + branch).astype(BF)
    total = None
    for b in range(8):
        part = expand_ref[:, 256 * b : 256 * b + 256]
        expanded = nn_dot(residual, part).astype(BF)
        combined = act_ref[b].astype(F32) + expanded.astype(F32)
        grad = (cot_ref[b].astype(F32) * silu_slope(combined)).astype(BF)
        grad_ref[b] = grad
        more = nt_dot(grad, part)
        total = more if total is None else total + more
    sum_ref[...] = total
    sum_b_ref[...] = total.astype(BF)


def grad_kernel(
    n_ref, w_ref, res_ref, mine_ref, got_ref, comb_ref, pre_ref, merge_ref, out_ref, rows_ref
):
    w = w_ref[0]
    conv = both_halves(n_ref[0], mine_ref[...].astype(F32), got_ref[...].astype(F32), 1)
    merged_grad = (res_ref[...] + conv).astype(BF)
    for b in range(8):
        cells = nt_dot(merged_grad, merge_ref[256 * b : 256 * b + 256]).astype(BF)
        grad = cells.astype(F32) + comb_ref[b].astype(F32)
        grad = grad * silu_slope(pre_ref[b])
        for z in range(2):
            for h in range(2):
                rows_ref[h, pl.ds(2 * b + z, 16, stride=16), :] = grad[
                    16 * z : 16 * z + 16, 128 * h : 128 * h + 128
                ]
    rows = jnp.concatenate([rows_ref[0], rows_ref[1]], axis=1).astype(BF)
    none = jnp.zeros((32, 256), BF)
    for x in range(8):
        ahead = rows[32 * x + 32 : 32 * x + 64] if x < 7 else none
        behind = rows[32 * x - 32 : 32 * x] if x > 0 else none
        out_ref[x, 0:32] = rows[32 * x : 32 * x + 32]
        out_ref[x, 32:64] = jnp.where(w == 0, ahead, behind)


def swap_narrow(value):
    return lax.ppermute(value, "narrow", [(0, 1), (1, 0)])


def pair_kernel(part_ref, got_ref, *refs):
    pair_ref, pair_b_ref = refs[-2:]
    pair = part_ref[...] + got_ref[...].astype(F32)
    pair_ref[...] = pair
    pair_b_ref[...] = pair.astype(BF)


def features_kernel(n_ref, pair_ref, one_ref, two_ref, three_ref, *refs):
    sum_ref, mine_ref, send_ref = refs[-3:]
    total = pair_ref[...] + one_ref[...].astype(F32) + two_ref[...].astype(F32) + three_ref[...].astype(F32)
    sum_ref[...] = total
    half = total.shape[1] // 2
    low, high = total[:, :half], total[:, half:]
    first = n_ref[0] == 0
    mine_ref[...] = jnp.where(first, low, high).astype(BF)
    send_ref[...] = jnp.where(first, high, low).astype(BF)


def cells_kernel(n_ref, pair_ref, one_ref, two_ref, three_ref, mine_ref, send_ref):
    total = pair_ref[...] + one_ref[...].astype(F32) + two_ref[...].astype(F32) + three_ref[...].astype(F32)
    half = total.shape[0] // 2
    low, high = total[:half], total[half:]
    first = n_ref[0] == 0
    mine_ref[...] = jnp.where(first, low, high)
    send_ref[...] = jnp.where(first, high, low).astype(BF)


def wide_terms(part, part_b, rest=()):
    def partner(value, mask):
        return lax.ppermute(value, "wide", [(i, i ^ mask) for i in range(8)])

    shape = part.shape
    pair, pair_b = kernel_call(
        pair_kernel, (), (part, partner(part_b, 1)), [shape_of(shape, F32), shape_of(shape, BF)], rest=rest
    )
    return (pair, *[partner(pair_b, mask) for mask in (2, 4, 6)])


def to_feature_halves(n, part, part_b, rest=()):
    terms = wide_terms(part, part_b, rest)
    cells, features = part.shape
    half_shape = shape_of((cells, features // 2), BF)
    total, mine, send = kernel_call(
        features_kernel, (n,), terms, [shape_of(part.shape, F32), half_shape, half_shape]
    )
    return total, mine, swap_narrow(send)


def to_cell_halves(n, part, part_b):
    terms = wide_terms(part, part_b)
    cells, features = part.shape
    half = (cells // 2, features)
    mine, send = kernel_call(cells_kernel, (n,), terms, [shape_of(half, F32), shape_of(half, BF)])
    return mine, swap_narrow(send)


def across_wide(value):
    return lax.all_to_all(value, "wide", split_axis=0, concat_axis=0, tiled=True)


def eight_shards(
    volume,
    cotangent,
    fine_weight,
    merge_weight,
    hidden_weight,
    step_table,
    output_weight,
    expand_weight,
    timestep,
):
    features = merge_weight.shape[1]
    hidden = hidden_weight.shape[2]
    half = features // 2
    w = lax.axis_index("wide").astype(jnp.int32).reshape(1)
    n = lax.axis_index("narrow").astype(jnp.int32).reshape(1)

    fine_cells = pltpu.VMEM((2048, 32), F32)
    (outgoing,) = kernel_call(
        pack_kernel, (n, w, timestep), (volume.transpose(1, 2, 3, 0), cotangent.transpose(1, 2, 3, 0)),
        [shape_of((8, 128, 256), BF)], [fine_cells, fine_cells],
    )
    arrived = across_wide(outgoing)
    band, bias = kernel_call(
        band_and_bias_kernel, (timestep,), (fine_weight,),
        [shape_of((1024, 768), BF), shape_of((1, hidden), F32)],
        [pltpu.VMEM((8, hidden), F32), pltpu.SemaphoreType.DMA], cost=BESIDE, rest=(step_table,),
    )
    sides, sent = side_call(w, arrived, band, arrived_planes, (merge_weight,))
    fine_rows = pltpu.VMEM((2, 256, 128), F32)
    sum_shapes = [shape_of((32, features), F32), shape_of((32, features), BF)]
    pre_act, act, merged_part, merged_part_b = kernel_call(
        merge_kernel,
        (n, w),
        (arrived, sides, swap_narrow(sent), band, merge_weight),
        [shape_of((8, 32, 256), F32), shape_of((8, 32, 256), BF)] + sum_shapes,
        [fine_rows],
    )
    (cot,) = kernel_call(cot_kernel, (), (arrived,), [shape_of((8, 32, 256), BF)], [fine_rows])
    merged, mine, got = to_feature_halves(n, merged_part, merged_part_b, (hidden_weight, output_weight))

    gate_shape = shape_of((64, hidden), F32)
    half_shapes = [shape_of((64, half), F32), shape_of((64, half), BF)]
    outer_columns = [pltpu.VMEM((27, 64, half), BF)]
    inner_columns = [pltpu.VMEM((27, 64, hidden), BF)]

    (gate_part,) = kernel_call(
        functools.partial(outer_kernel, flipped=False, dot=nn_dot, part_of=feature_rows),
        (n,), (mine, got, hidden_weight), [gate_shape], outer_columns,
    )
    gate_pre, branch_part, branch_part_b = kernel_call(
        inner_forward_kernel,
        (n,), (gate_part, swap_narrow(gate_part), bias, output_weight), [gate_shape] + half_shapes, inner_columns,
    )
    mine, got = to_cell_halves(n, branch_part, branch_part_b)
    grad_comb, res_part, res_part_b = kernel_call(
        expand_kernel,
        (n,), (merged, mine, got, act, cot, expand_weight),
        [shape_of((8, 32, 256), BF)] + sum_shapes,
    )
    grad_res, mine, got = to_feature_halves(n, res_part, res_part_b)
    (hidden_part,) = kernel_call(
        functools.partial(outer_kernel, flipped=True, dot=nt_dot, part_of=feature_columns),
        (n,), (mine, got, output_weight), [gate_shape], outer_columns,
    )
    conv_part, conv_part_b = kernel_call(
        inner_backward_kernel,
        (n,), (hidden_part, swap_narrow(hidden_part), gate_pre, hidden_weight),
        half_shapes, inner_columns,
    )
    mine, got = to_cell_halves(n, conv_part, conv_part_b)
    (leaving,) = kernel_call(
        grad_kernel,
        (n, w), (grad_res, mine, got, grad_comb, pre_act, merge_weight),
        [shape_of((8, 64, 256), BF)], [fine_rows],
    )
    returned = across_wide(leaving)
    band = banded(fine_weight, True)
    sides, sent = side_call(w, returned, band, returned_planes)
    (result,) = kernel_call(
        final_kernel,
        (n, w), (returned, sides, swap_narrow(sent), band),
        [shape_of((8, 16, 16, 32), BF)], [fine_cells],
    )
    return result.transpose(3, 0, 1, 2)


def shards(
    volume,
    cotangent,
    fine_weight,
    merge_weight,
    hidden_weight,
    step_table,
    output_weight,
    expand_weight,
    timestep,
):
    channels = volume.shape[0]
    fine_height = volume.shape[2]
    fine_depth = volume.shape[3]
    wide_count = lax.axis_size("wide")
    features = merge_weight.shape[1]
    hidden_local = hidden_weight.shape[2]
    coarse_grid = (wide_count, fine_height // PATCH, fine_depth // PATCH)
    hidden_mat = hidden_weight.transpose(1, 0, 2).reshape(features, 27 * hidden_local)
    output_mat = output_weight.reshape(27 * hidden_local, features)
    output_back = output_weight.transpose(2, 0, 1).reshape(features, 27 * hidden_local)
    hidden_back = hidden_weight.transpose(0, 2, 1).reshape(27 * hidden_local, features)

    def total_rows(partial_value):
        return lax.psum(partial_value, "wide")

    pre_act = fine_conv(volume, fine_weight, False)
    activated = jax.nn.silu(pre_act).astype(jnp.bfloat16)
    received = send_patches(activated)
    merged = total_rows(jnp.dot(received, merge_weight, preferred_element_type=jnp.float32))
    coarse_in = merged.astype(jnp.bfloat16).reshape(coarse_grid + (features,))
    bias_row = step_table[timestep[0]]
    gate_pre = wide_input_conv(coarse_in, hidden_mat, hidden_local, False) + bias_row
    hidden_act = jax.nn.silu(gate_pre).astype(jnp.bfloat16)
    branch = total_rows(narrow_input_conv(hidden_act, output_mat, False).reshape(-1, features))
    residual_sum = (merged + branch).astype(jnp.bfloat16)
    expanded = jnp.dot(residual_sum, expand_weight, preferred_element_type=jnp.float32).astype(
        jnp.bfloat16
    )
    expanded_field = return_patches(expanded, fine_height, fine_depth, channels)
    combined = activated.astype(jnp.float32) + expanded_field.astype(jnp.float32)
    grad_comb = (cotangent.astype(jnp.float32) * silu_slope(combined)).astype(jnp.bfloat16)
    grad_res = total_rows(
        jnp.einsum(
            "nk,dk->nd", send_patches(grad_comb), expand_weight, preferred_element_type=jnp.float32
        )
    )
    grad_res_b = grad_res.astype(jnp.bfloat16).reshape(coarse_grid + (features,))
    grad_hidden = wide_input_conv(grad_res_b, output_back, hidden_local, True)
    grad_gate = (grad_hidden * silu_slope(gate_pre)).astype(jnp.bfloat16)
    grad_conv = total_rows(narrow_input_conv(grad_gate, hidden_back, True).reshape(-1, features))
    grad_merged = (grad_res + grad_conv).astype(jnp.bfloat16)
    grad_cells = jnp.einsum(
        "nd,kd->nk", grad_merged, merge_weight, preferred_element_type=jnp.float32
    ).astype(jnp.bfloat16)
    grad_act = return_patches(grad_cells, fine_height, fine_depth, channels).astype(
        jnp.float32
    ) + grad_comb.astype(jnp.float32)
    grad_pre = (grad_act * silu_slope(pre_act)).astype(jnp.bfloat16)
    return fine_conv(grad_pre, fine_weight.transpose(0, 2, 1), True).astype(jnp.bfloat16)


def solution(mesh):
    in_specs = (
        P(None, ("groups", "wide"), None, "narrow"),
        P(None, ("groups", "wide"), None, "narrow"),
        P(),
        P("wide", None),
        P(None, None, "wide"),
        P(None, "wide"),
        P(None, "wide", None),
        P(None, "wide"),
        P("groups"),
    )
    out_specs = P(None, ("groups", "wide"), None, "narrow")
    sizes = dict(mesh.shape)
    fits = sizes["wide"] == PATCH and sizes["narrow"] == 2
    body = eight_shards if fits else shards
    return jax.shard_map(body, mesh=mesh, in_specs=in_specs, out_specs=out_specs, check_vma=False)
```

```python
import functools

import jax
import jax.numpy as jnp
from jax import lax
from jax.experimental import pallas as pl
from jax.experimental.pallas import tpu as pltpu
from jax.sharding import PartitionSpec as P

PATCH = 8


def extended(cells, sides, width):
    for axis, dim in sides:
        count = lax.axis_size(axis)
        ends = count - 1
        head = lax.slice_in_dim(cells, 0, width, axis=dim)
        tail = lax.slice_in_dim(cells, cells.shape[dim] - width, cells.shape[dim], axis=dim)
        cells = jnp.concatenate(
            [
                lax.ppermute(tail, axis, [(i, (i + 1) % count) for i in range(ends)]),
                cells,
                lax.ppermute(head, axis, [((i + 1) % count, i) for i in range(ends)]),
            ],
            axis=dim,
        )
    return cells


def shifts(transposed):
    return [
        (2 - i, 2 - j, 2 - k) if transposed else (i, j, k)
        for i in range(3)
        for j in range(3)
        for k in range(3)
    ]


def silu_slope(values):
    logistic = jax.nn.sigmoid(values)
    return logistic * (1.0 + values * (1.0 - logistic))


def fine_conv(fine_field, weight, transposed):
    grown = extended(fine_field, (("wide", 1), ("narrow", 3)), 1)
    padded = jnp.pad(grown, ((0, 0), (0, 0), (1, 1), (0, 0)))
    kernel = weight.reshape(3, 3, 3, weight.shape[1], weight.shape[2])
    if transposed:
        kernel = kernel[::-1, ::-1, ::-1]
    result = lax.conv_general_dilated(
        padded[None],
        kernel,
        (1, 1, 1),
        "VALID",
        dimension_numbers=("NCDHW", "DHWIO", "NCDHW"),
        preferred_element_type=jnp.float32,
    )
    return result[0]


def to_patches(fine_field):
    channels = fine_field.shape[0]
    shaped = fine_field.reshape(
        channels, PATCH, fine_field.shape[2] // PATCH, PATCH, fine_field.shape[3] // PATCH, PATCH
    )
    return shaped.transpose(2, 4, 1, 3, 5, 0).reshape(-1, PATCH**3 * channels)


def send_patches(fine_field):
    return lax.all_to_all(to_patches(fine_field), "wide", split_axis=1, concat_axis=0, tiled=True)


def return_patches(patch_rows, fine_height, fine_depth, channels):
    returned = lax.all_to_all(patch_rows, "wide", split_axis=0, concat_axis=1, tiled=True)
    shaped = returned.reshape(
        fine_height // PATCH, fine_depth // PATCH, PATCH, PATCH, PATCH, channels
    )
    return shaped.transpose(5, 2, 0, 3, 1, 4).reshape(channels, PATCH, fine_height, fine_depth)


def coarse_faces(coarse_block):
    return extended(coarse_block, (("narrow", 2),), 1)


def wide_input_conv(coarse_block, weight_mat, out_count, transposed):
    grown = coarse_faces(coarse_block)
    products = jnp.einsum("xyzd,dk->xyzk", grown, weight_mat, preferred_element_type=jnp.float32)
    padded = jnp.pad(products, ((1, 1), (1, 1), (0, 0), (0, 0)))
    extent = coarse_block.shape[:3]
    summed = jnp.zeros(extent + (out_count,), jnp.float32)
    for tap_index, (a, b, c) in enumerate(shifts(transposed)):
        summed = (
            summed
            + padded[
                a : a + extent[0],
                b : b + extent[1],
                c : c + extent[2],
                tap_index * out_count : (tap_index + 1) * out_count,
            ]
        )
    return summed


def narrow_input_conv(coarse_block, weight_mat, transposed):
    grown = coarse_faces(coarse_block)
    padded = jnp.pad(grown, ((1, 1), (1, 1), (0, 0), (0, 0)))
    extent = coarse_block.shape[:3]
    columns = jnp.concatenate(
        [
            padded[a : a + extent[0], b : b + extent[1], c : c + extent[2]]
            for a, b, c in shifts(transposed)
        ],
        axis=3,
    )
    return jnp.einsum("xyzk,kd->xyzd", columns, weight_mat, preferred_element_type=jnp.float32)


BF = jnp.bfloat16
F32 = jnp.float32
LIMIT = 10 * 1024 * 1024
BESIDE = 32 * 1024 * 1024
VMEM = pl.BlockSpec(memory_space=pltpu.VMEM)
SMEM = pl.BlockSpec(memory_space=pltpu.SMEM)


def nn_dot(lhs, rhs):
    return jnp.dot(lhs, rhs, preferred_element_type=F32)


def nt_dot(lhs, rhs):
    return lax.dot_general(lhs, rhs, (((1,), (1,)), ((), ())), preferred_element_type=F32)


def shape_of(dims, dtype):
    return jax.ShapeDtypeStruct(dims, dtype)


def kernel_call(kernel, places, arrays, outs, scratch=(), cost=None, rest=()):
    return pl.pallas_call(
        kernel,
        in_specs=[SMEM] * len(places) + [VMEM] * len(arrays) + [pl.BlockSpec(memory_space=pl.ANY)] * len(rest),
        out_specs=[VMEM] * len(outs),
        out_shape=outs,
        scratch_shapes=list(scratch),
        cost_estimate=cost and pl.CostEstimate(flops=0, bytes_accessed=cost, transcendentals=0),
        compiler_params=pltpu.CompilerParams(vmem_limit_bytes=LIMIT),
    )(*places, *arrays, *[pltpu.with_memory_space_constraint(a, pltpu.HBM) for a in rest])


def band_kernel(weight_ref, out_ref, *, back):
    row = lax.broadcasted_iota(jnp.int32, (32, 256), 0)
    lane = lax.broadcasted_iota(jnp.int32, (32, 256), 1)
    places = [(lane == row + 32 * (2 - k)).astype(BF) for k in range(3)]
    same = (
        lax.broadcasted_iota(jnp.int32, (32, 32), 0) == lax.broadcasted_iota(jnp.int32, (32, 32), 1)
    ).astype(BF)
    for i in range(3):
        for j in range(3):
            taps = None
            for k in range(3):
                t = 9 * i + 3 * j + k
                tap = nt_dot(same, weight_ref[26 - t]).astype(BF) if back else weight_ref[t]
                part = nn_dot(tap, places[k])
                taps = part if taps is None else taps + part
            columns = slice(256 * j, 256 * j + 256)

            def placed(start):
                moved = pltpu.roll(taps, start % 256, 1)
                return jnp.where((lane >= start) & (lane < start + 96), moved, 0.0).astype(BF)

            for d in range(8):
                out_ref[256 * i + 32 * d : 256 * i + 32 * d + 32, columns] = placed(32 * (d - 1))
            out_ref[768 + 64 * i : 800 + 64 * i, columns] = placed(-64)
            out_ref[800 + 64 * i : 832 + 64 * i, columns] = placed(224)
    out_ref[960:1024, :] = jnp.zeros((64, 768), BF)


def band_and_bias_kernel(step_ref, weight_ref, table_ref, out_ref, bias_ref, rows_ref, sem):
    step = step_ref[0]
    group = pl.ds(pl.multiple_of(step // 8 * 8, 8), 8)
    fetch = pltpu.make_async_copy(table_ref.at[group], rows_ref, sem)
    fetch.start()
    band_kernel(weight_ref, out_ref, back=False)
    fetch.wait()
    rows = rows_ref[...]
    chosen = lax.broadcasted_iota(jnp.int32, rows.shape, 0) == step % 8
    bias_ref[...] = jnp.sum(jnp.where(chosen, rows, jnp.zeros_like(rows)), axis=0, keepdims=True)


def banded(weight, back):
    (out,) = kernel_call(
        functools.partial(band_kernel, back=back), (), (weight,), [shape_of((1024, 768), BF)], cost=BESIDE
    )
    return out


def lane_place(d):
    row = lax.broadcasted_iota(jnp.int32, (32, 256), 0)
    lane = lax.broadcasted_iota(jnp.int32, (32, 256), 1)
    return (lane == row + 32 * d).astype(BF)


def to_rows(field_ref, cells_ref):
    cells_ref[...] = field_ref[...].astype(F32).reshape(2048, 32)
    rows = None
    for d in range(8):
        part = nn_dot(cells_ref[pl.ds(d, 256, stride=8), :].astype(BF), lane_place(d))
        rows = part if rows is None else rows + part
    return rows.astype(BF).reshape(8, 32, 256)


def pack_kernel(n_ref, w_ref, step_ref, volume_ref, cotangent_ref, *refs):
    del n_ref, step_ref
    out_refs = refs[:8]
    volume_copy_ref, cotangent_copy_ref, cells_ref, other_ref, field_ref, cot_ref, sems = refs[8:]
    first = pltpu.make_async_copy(volume_ref, volume_copy_ref, sems.at[0])
    second = pltpu.make_async_copy(cotangent_ref, cotangent_copy_ref, sems.at[1])
    first.start()
    second.start()
    first.wait()
    field_ref[...] = to_rows(volume_copy_ref, cells_ref)
    second.wait()
    cot_ref[...] = to_rows(cotangent_copy_ref, other_ref)
    for mask, out_ref in enumerate(out_refs):
        a = w_ref[0] ^ mask
        out_ref[0:32] = field_ref[(a + 7) & 7]
        out_ref[32:64] = field_ref[a]
        out_ref[64:96] = field_ref[(a + 1) & 7]
        out_ref[96:128] = cot_ref[a]


def arrived_planes(w, arrived_ref):
    none = jnp.zeros((32, 256), BF)
    before, own, after = [
        arrived_ref[:, 32 * s : 32 * s + 32, :].reshape(256, 256) for s in range(3)
    ]
    before = jnp.where(w == 0, jnp.concatenate([none, before[:224]], axis=0), before)
    after = jnp.where(w == 7, jnp.concatenate([after[32:], none], axis=0), after)
    return before, own, after


def returned_planes(w, returned_ref):
    rows = [returned_ref[7, 32:64]] + [returned_ref[a, 0:32] for a in range(8)] + [returned_ref[0, 32:64]]
    grown = jnp.concatenate(rows, axis=0)
    return grown[0:256], grown[32:288], grown[64:320]


def arrived_kernel(w_ref, *refs):
    planes_ref, own_ref, send_ref = refs[-3:]
    for mask in range(8):
        planes_ref[w_ref[0] ^ mask] = refs[mask][...]
    put_sides(arrived_planes(w_ref[0], planes_ref), own_ref, send_ref)


def returned_kernel(w_ref, planes_ref, band_ref, own_ref, send_ref):
    del band_ref
    put_sides(returned_planes(w_ref[0], planes_ref), own_ref, send_ref)


def put_sides(planes, own_ref, send_ref):
    source = lax.broadcasted_iota(jnp.int32, (256, 256), 0)
    target = lax.broadcasted_iota(jnp.int32, (256, 256), 1)
    sides = None
    for i, plane in enumerate(planes):
        high = (source >= 224) & (target == source - 224 + 64 * i)
        low = (source < 32) & (target == source + 64 * i + 32)
        part = nn_dot(plane, (high | low).astype(BF))
        sides = part if sides is None else sides + part
    even = (source & 1) == 0
    sides = jnp.where(even, pltpu.roll(sides, 255, 0), pltpu.roll(sides, 1, 0))
    low_side = (target & 32) != 0
    own = even == low_side
    zero = jnp.zeros_like(sides)
    own_ref[...] = jnp.where(own, sides, zero).astype(BF)
    send_ref[...] = jnp.where(own, zero, sides).astype(BF)


def main_kernel(w_ref, planes_ref, band_ref, out_ref, *, planes_of):
    lhs = jnp.concatenate(planes_of(w_ref[0], planes_ref), axis=1)
    out_ref[...] = nn_dot(lhs, band_ref[0:768])


def main_call(w, planes, band, planes_of):
    (out,) = kernel_call(
        functools.partial(main_kernel, planes_of=planes_of), (w,), (planes, band), [shape_of((256, 768), F32)]
    )
    return out


def fine_sum(n, main_ref, own_ref, got_ref, band_ref):
    lane = lax.broadcasted_iota(jnp.int32, (256, 256), 1)
    keep = ((lane & 32) != 0) == (n == 0)
    got = jnp.where(keep, got_ref[...].astype(F32), jnp.zeros((256, 256), F32))
    sides = (own_ref[...].astype(F32) + got).astype(BF)
    shifts_y = main_ref[...] + nn_dot(sides, band_ref[768:1024])
    y = (lax.broadcasted_iota(jnp.int32, (256, 1), 0) >> 1) & 15
    total = shifts_y[:, 256:512]
    zero = jnp.zeros_like(total)
    below = pltpu.roll(shifts_y[:, 0:256], 2, 0)
    above = pltpu.roll(shifts_y[:, 512:768], 254, 0)
    return total + jnp.where(y > 0, below, zero) + jnp.where(y < 15, above, zero)


def cell_rows(ref, b):
    return jnp.concatenate([ref[pl.ds(2 * b + z, 16, stride=16), :] for z in range(2)], axis=0)


def merge_kernel(
    n_ref, main_ref, own_ref, got_ref, band_ref, merge_ref, pre_ref, act_ref, sum_ref, sum_b_ref, rows_ref
):
    wide_rows = fine_sum(n_ref[0], main_ref, own_ref, got_ref, band_ref)
    rows_ref[0] = wide_rows[:, :128]
    rows_ref[1] = wide_rows[:, 128:]
    total = None
    for b in range(8):
        pre = jnp.concatenate([cell_rows(rows_ref.at[h], b) for h in range(2)], axis=1)
        pre_ref[b] = pre
        act = (pre * jax.nn.sigmoid(pre)).astype(BF)
        act_ref[b] = act
        part = nn_dot(act, merge_ref[256 * b : 256 * b + 256])
        total = part if total is None else total + part
    sum_ref[...] = total
    sum_b_ref[...] = total.astype(BF)


def cot_kernel(planes_ref, cot_ref, rows_ref):
    rows = planes_ref[:, 96:128, :].reshape(256, 256).astype(F32)
    rows_ref[0] = rows[:, :128]
    rows_ref[1] = rows[:, 128:]
    for b in range(8):
        cot_ref[b] = jnp.concatenate([cell_rows(rows_ref.at[h], b) for h in range(2)], axis=1).astype(BF)


def final_kernel(n_ref, main_ref, own_ref, got_ref, band_ref, out_ref, cells_ref):
    rows = fine_sum(n_ref[0], main_ref, own_ref, got_ref, band_ref).astype(BF)
    for d in range(8):
        cells_ref[pl.ds(d, 256, stride=8), :] = nt_dot(rows, lane_place(d))
    out_ref[...] = cells_ref[...].astype(BF).reshape(8, 16, 16, 32)


def put_columns(cols_ref, cells):
    row = lax.broadcasted_iota(jnp.int32, (64, 1), 0)
    along_y, along_x = row & 1, (row >> 1) & 7
    zero = jnp.zeros_like(cells)
    none = jnp.zeros((16, cells.shape[1]), BF)
    below = jnp.where(along_y == 1, pltpu.roll(cells, 1, 0), zero)
    above = jnp.where(along_y == 0, pltpu.roll(cells, 63, 0), zero)
    for j, moved_y in enumerate((below, cells, above)):
        before = jnp.where(along_x > 0, pltpu.roll(moved_y, 2, 0), zero)
        after = jnp.where(along_x < 7, pltpu.roll(moved_y, 62, 0), zero)
        for i, moved in enumerate((before, moved_y, after)):
            rows = moved.astype(BF)
            cols_ref[9 * i + 3 * j] = jnp.concatenate([none, rows[:48]], axis=0)
            cols_ref[9 * i + 3 * j + 1] = rows
            cols_ref[9 * i + 3 * j + 2] = jnp.concatenate([rows[16:], none], axis=0)


def both_halves(n, mine, got, axis):
    first = n == 0
    return jnp.concatenate([jnp.where(first, mine, got), jnp.where(first, got, mine)], axis=axis)


def conv_sum(cols_ref, weight_of, flipped, dot):
    total = None
    for t in range(27):
        part = dot(cols_ref[26 - t if flipped else t], weight_of(t))
        total = part if total is None else total + part
    return total


def feature_rows(n, ref):
    half = ref.shape[1] // 2
    return lambda t: ref[t, pl.ds(pl.multiple_of(n * half, half), half), :]


def feature_columns(n, ref):
    half = ref.shape[2] // 2
    return lambda t: ref[t, :, pl.ds(pl.multiple_of(n * half, half), half)]


def outer_kernel(n_ref, mine_ref, got_ref, weight_ref, sum_ref, cols_ref, *, flipped, dot, part_of):
    n = n_ref[0]
    put_columns(cols_ref, both_halves(n, mine_ref[...].astype(F32), got_ref[...].astype(F32), 0))
    sum_ref[...] = conv_sum(cols_ref, part_of(n, weight_ref), flipped, dot)


def inner_forward_kernel(
    n_ref, mine_ref, got_ref, bias_ref, weight_ref, gate_ref, sum_ref, sum_b_ref, cols_ref
):
    gate = mine_ref[...] + got_ref[...] + bias_ref[...]
    gate_ref[...] = gate
    put_columns(cols_ref, gate * jax.nn.sigmoid(gate))
    total = conv_sum(cols_ref, feature_columns(n_ref[0], weight_ref), False, nn_dot)
    sum_ref[...] = total
    sum_b_ref[...] = total.astype(BF)


def inner_backward_kernel(
    n_ref, mine_ref, got_ref, gate_ref, weight_ref, sum_ref, sum_b_ref, cols_ref
):
    put_columns(cols_ref, (mine_ref[...] + got_ref[...]) * silu_slope(gate_ref[...]))
    total = conv_sum(cols_ref, feature_rows(n_ref[0], weight_ref), True, nt_dot)
    sum_ref[...] = total
    sum_b_ref[...] = total.astype(BF)


def expand_kernel(
    n_ref, merged_ref, mine_ref, got_ref, act_ref, cot_ref, expand_ref, grad_ref, sum_ref, sum_b_ref
):
    branch = both_halves(n_ref[0], mine_ref[...].astype(F32), got_ref[...].astype(F32), 1)
    residual = (merged_ref[...] + branch).astype(BF)
    total = None
    for b in range(8):
        part = expand_ref[:, 256 * b : 256 * b + 256]
        expanded = nn_dot(residual, part).astype(BF)
        combined = act_ref[b].astype(F32) + expanded.astype(F32)
        grad = (cot_ref[b].astype(F32) * silu_slope(combined)).astype(BF)
        grad_ref[b] = grad
        more = nt_dot(grad, part)
        total = more if total is None else total + more
    sum_ref[...] = total
    sum_b_ref[...] = total.astype(BF)


def grad_kernel(
    n_ref, w_ref, res_ref, mine_ref, got_ref, comb_ref, pre_ref, merge_ref, out_ref, rows_ref
):
    w = w_ref[0]
    conv = both_halves(n_ref[0], mine_ref[...].astype(F32), got_ref[...].astype(F32), 1)
    merged_grad = (res_ref[...] + conv).astype(BF)
    for b in range(8):
        cells = nt_dot(merged_grad, merge_ref[256 * b : 256 * b + 256]).astype(BF)
        grad = cells.astype(F32) + comb_ref[b].astype(F32)
        grad = grad * silu_slope(pre_ref[b])
        for z in range(2):
            for h in range(2):
                rows_ref[h, pl.ds(2 * b + z, 16, stride=16), :] = grad[
                    16 * z : 16 * z + 16, 128 * h : 128 * h + 128
                ]
    rows = jnp.concatenate([rows_ref[0], rows_ref[1]], axis=1).astype(BF)
    none = jnp.zeros((32, 256), BF)
    for x in range(8):
        ahead = rows[32 * x + 32 : 32 * x + 64] if x < 7 else none
        behind = rows[32 * x - 32 : 32 * x] if x > 0 else none
        out_ref[x, 0:32] = rows[32 * x : 32 * x + 32]
        out_ref[x, 32:64] = jnp.where(w == 0, ahead, behind)


def swap_narrow(value):
    return lax.ppermute(value, "narrow", [(0, 1), (1, 0)])


def pair_kernel(part_ref, got_ref, *refs):
    pair_ref, pair_b_ref = refs[-2:]
    pair = part_ref[...] + got_ref[...].astype(F32)
    pair_ref[...] = pair
    pair_b_ref[...] = pair.astype(BF)


def features_kernel(n_ref, pair_ref, one_ref, two_ref, three_ref, *refs):
    sum_ref, mine_ref, send_ref = refs[-3:]
    total = pair_ref[...] + one_ref[...].astype(F32) + two_ref[...].astype(F32) + three_ref[...].astype(F32)
    sum_ref[...] = total
    half = total.shape[1] // 2
    low, high = total[:, :half], total[:, half:]
    first = n_ref[0] == 0
    mine_ref[...] = jnp.where(first, low, high).astype(BF)
    send_ref[...] = jnp.where(first, high, low).astype(BF)


def cells_kernel(n_ref, pair_ref, one_ref, two_ref, three_ref, mine_ref, send_ref):
    total = pair_ref[...] + one_ref[...].astype(F32) + two_ref[...].astype(F32) + three_ref[...].astype(F32)
    half = total.shape[0] // 2
    low, high = total[:half], total[half:]
    first = n_ref[0] == 0
    mine_ref[...] = jnp.where(first, low, high)
    send_ref[...] = jnp.where(first, high, low).astype(BF)


def wide_terms(part, part_b, rest=()):
    def partner(value, mask):
        return lax.ppermute(value, "wide", [(i, i ^ mask) for i in range(8)])

    shape = part.shape
    pair, pair_b = kernel_call(
        pair_kernel, (), (part, partner(part_b, 1)), [shape_of(shape, F32), shape_of(shape, BF)], rest=rest
    )
    return (pair, *[partner(pair_b, mask) for mask in (2, 4, 6)])


def to_feature_halves(n, part, part_b, rest=()):
    terms = wide_terms(part, part_b, rest)
    cells, features = part.shape
    half_shape = shape_of((cells, features // 2), BF)
    total, mine, send = kernel_call(
        features_kernel, (n,), terms, [shape_of(part.shape, F32), half_shape, half_shape]
    )
    return total, mine, swap_narrow(send)


def to_cell_halves(n, part, part_b):
    terms = wide_terms(part, part_b)
    cells, features = part.shape
    half = (cells // 2, features)
    mine, send = kernel_call(cells_kernel, (n,), terms, [shape_of(half, F32), shape_of(half, BF)])
    return mine, swap_narrow(send)


def across_wide(messages):
    return [messages[0]] + [
        lax.ppermute(messages[mask], "wide", [(i, i ^ mask) for i in range(8)]) for mask in range(1, 8)
    ]


def eight_shards(
    volume,
    cotangent,
    fine_weight,
    merge_weight,
    hidden_weight,
    step_table,
    output_weight,
    expand_weight,
    timestep,
):
    features = merge_weight.shape[1]
    hidden = hidden_weight.shape[2]
    half = features // 2
    w = lax.axis_index("wide").astype(jnp.int32).reshape(1)
    n = lax.axis_index("narrow").astype(jnp.int32).reshape(1)

    fine_cells = pltpu.VMEM((2048, 32), F32)
    fine_field = pltpu.VMEM((8, 16, 16, 32), BF)
    fine_blocks = pltpu.VMEM((8, 32, 256), BF)
    outgoing = kernel_call(
        pack_kernel, (n, w, timestep), (), [shape_of((128, 256), BF)] * 8,
        [fine_field, fine_field, fine_cells, fine_cells, fine_blocks, fine_blocks, pltpu.SemaphoreType.DMA((2,))],
        rest=(volume.transpose(1, 2, 3, 0), cotangent.transpose(1, 2, 3, 0)),
    )
    messages = across_wide(outgoing)
    band, bias = kernel_call(
        band_and_bias_kernel, (timestep,), (fine_weight,),
        [shape_of((1024, 768), BF), shape_of((1, hidden), F32)],
        [pltpu.VMEM((8, hidden), F32), pltpu.SemaphoreType.DMA], cost=BESIDE, rest=(step_table,),
    )
    side_shape = shape_of((256, 256), BF)
    arrived, sides, sent = kernel_call(
        arrived_kernel, (w,), (*messages, band), [shape_of((8, 128, 256), BF), side_shape, side_shape],
        rest=(merge_weight,),
    )
    fine_rows = pltpu.VMEM((2, 256, 128), F32)
    sum_shapes = [shape_of((32, features), F32), shape_of((32, features), BF)]
    pre_act, act, merged_part, merged_part_b = kernel_call(
        merge_kernel,
        (n,),
        (main_call(w, arrived, band, arrived_planes), sides, swap_narrow(sent), band, merge_weight),
        [shape_of((8, 32, 256), F32), shape_of((8, 32, 256), BF)] + sum_shapes,
        [fine_rows],
    )
    (cot,) = kernel_call(cot_kernel, (), (arrived,), [shape_of((8, 32, 256), BF)], [fine_rows])
    merged, mine, got = to_feature_halves(n, merged_part, merged_part_b, (hidden_weight, output_weight))

    gate_shape = shape_of((64, hidden), F32)
    half_shapes = [shape_of((64, half), F32), shape_of((64, half), BF)]
    outer_columns = [pltpu.VMEM((27, 64, half), BF)]
    inner_columns = [pltpu.VMEM((27, 64, hidden), BF)]

    (gate_part,) = kernel_call(
        functools.partial(outer_kernel, flipped=False, dot=nn_dot, part_of=feature_rows),
        (n,), (mine, got, hidden_weight), [gate_shape], outer_columns,
    )
    gate_pre, branch_part, branch_part_b = kernel_call(
        inner_forward_kernel,
        (n,), (gate_part, swap_narrow(gate_part), bias, output_weight), [gate_shape] + half_shapes, inner_columns,
    )
    mine, got = to_cell_halves(n, branch_part, branch_part_b)
    grad_comb, res_part, res_part_b = kernel_call(
        expand_kernel,
        (n,), (merged, mine, got, act, cot, expand_weight),
        [shape_of((8, 32, 256), BF)] + sum_shapes,
    )
    grad_res, mine, got = to_feature_halves(n, res_part, res_part_b)
    (hidden_part,) = kernel_call(
        functools.partial(outer_kernel, flipped=True, dot=nt_dot, part_of=feature_columns),
        (n,), (mine, got, output_weight), [gate_shape], outer_columns,
    )
    conv_part, conv_part_b = kernel_call(
        inner_backward_kernel,
        (n,), (hidden_part, swap_narrow(hidden_part), gate_pre, hidden_weight),
        half_shapes, inner_columns,
    )
    mine, got = to_cell_halves(n, conv_part, conv_part_b)
    (leaving,) = kernel_call(
        grad_kernel,
        (n, w), (grad_res, mine, got, grad_comb, pre_act, merge_weight),
        [shape_of((8, 64, 256), BF)], [fine_rows],
    )
    returned = lax.all_to_all(leaving, "wide", split_axis=0, concat_axis=0, tiled=True)
    band = banded(fine_weight, True)
    sides, sent = kernel_call(returned_kernel, (w,), (returned, band), [side_shape, side_shape])
    (result,) = kernel_call(
        final_kernel,
        (n,), (main_call(w, returned, band, returned_planes), sides, swap_narrow(sent), band),
        [shape_of((8, 16, 16, 32), BF)], [fine_cells],
    )
    return result.transpose(3, 0, 1, 2)


def shards(
    volume,
    cotangent,
    fine_weight,
    merge_weight,
    hidden_weight,
    step_table,
    output_weight,
    expand_weight,
    timestep,
):
    channels = volume.shape[0]
    fine_height = volume.shape[2]
    fine_depth = volume.shape[3]
    wide_count = lax.axis_size("wide")
    features = merge_weight.shape[1]
    hidden_local = hidden_weight.shape[2]
    coarse_grid = (wide_count, fine_height // PATCH, fine_depth // PATCH)
    hidden_mat = hidden_weight.transpose(1, 0, 2).reshape(features, 27 * hidden_local)
    output_mat = output_weight.reshape(27 * hidden_local, features)
    output_back = output_weight.transpose(2, 0, 1).reshape(features, 27 * hidden_local)
    hidden_back = hidden_weight.transpose(0, 2, 1).reshape(27 * hidden_local, features)

    def total_rows(partial_value):
        return lax.psum(partial_value, "wide")

    pre_act = fine_conv(volume, fine_weight, False)
    activated = jax.nn.silu(pre_act).astype(jnp.bfloat16)
    received = send_patches(activated)
    merged = total_rows(jnp.dot(received, merge_weight, preferred_element_type=jnp.float32))
    coarse_in = merged.astype(jnp.bfloat16).reshape(coarse_grid + (features,))
    bias_row = step_table[timestep[0]]
    gate_pre = wide_input_conv(coarse_in, hidden_mat, hidden_local, False) + bias_row
    hidden_act = jax.nn.silu(gate_pre).astype(jnp.bfloat16)
    branch = total_rows(narrow_input_conv(hidden_act, output_mat, False).reshape(-1, features))
    residual_sum = (merged + branch).astype(jnp.bfloat16)
    expanded = jnp.dot(residual_sum, expand_weight, preferred_element_type=jnp.float32).astype(
        jnp.bfloat16
    )
    expanded_field = return_patches(expanded, fine_height, fine_depth, channels)
    combined = activated.astype(jnp.float32) + expanded_field.astype(jnp.float32)
    grad_comb = (cotangent.astype(jnp.float32) * silu_slope(combined)).astype(jnp.bfloat16)
    grad_res = total_rows(
        jnp.einsum(
            "nk,dk->nd", send_patches(grad_comb), expand_weight, preferred_element_type=jnp.float32
        )
    )
    grad_res_b = grad_res.astype(jnp.bfloat16).reshape(coarse_grid + (features,))
    grad_hidden = wide_input_conv(grad_res_b, output_back, hidden_local, True)
    grad_gate = (grad_hidden * silu_slope(gate_pre)).astype(jnp.bfloat16)
    grad_conv = total_rows(narrow_input_conv(grad_gate, hidden_back, True).reshape(-1, features))
    grad_merged = (grad_res + grad_conv).astype(jnp.bfloat16)
    grad_cells = jnp.einsum(
        "nd,kd->nk", grad_merged, merge_weight, preferred_element_type=jnp.float32
    ).astype(jnp.bfloat16)
    grad_act = return_patches(grad_cells, fine_height, fine_depth, channels).astype(
        jnp.float32
    ) + grad_comb.astype(jnp.float32)
    grad_pre = (grad_act * silu_slope(pre_act)).astype(jnp.bfloat16)
    return fine_conv(grad_pre, fine_weight.transpose(0, 2, 1), True).astype(jnp.bfloat16)


def solution(mesh):
    in_specs = (
        P(None, ("groups", "wide"), None, "narrow"),
        P(None, ("groups", "wide"), None, "narrow"),
        P(),
        P("wide", None),
        P(None, None, "wide"),
        P(None, "wide"),
        P(None, "wide", None),
        P(None, "wide"),
        P("groups"),
    )
    out_specs = P(None, ("groups", "wide"), None, "narrow")
    sizes = dict(mesh.shape)
    fits = sizes["wide"] == PATCH and sizes["narrow"] == 2
    body = eight_shards if fits else shards
    return jax.shard_map(body, mesh=mesh, in_specs=in_specs, out_specs=out_specs, check_vma=False)
```

```python
import functools

import jax
import jax.numpy as jnp
from jax import lax
from jax.experimental import pallas as pl
from jax.experimental.pallas import tpu as pltpu
from jax.sharding import PartitionSpec as P

PATCH = 8


def extended(cells, sides, width):
    for axis, dim in sides:
        count = lax.axis_size(axis)
        ends = count - 1
        head = lax.slice_in_dim(cells, 0, width, axis=dim)
        tail = lax.slice_in_dim(cells, cells.shape[dim] - width, cells.shape[dim], axis=dim)
        cells = jnp.concatenate(
            [
                lax.ppermute(tail, axis, [(i, (i + 1) % count) for i in range(ends)]),
                cells,
                lax.ppermute(head, axis, [((i + 1) % count, i) for i in range(ends)]),
            ],
            axis=dim,
        )
    return cells


def shifts(transposed):
    return [
        (2 - i, 2 - j, 2 - k) if transposed else (i, j, k)
        for i in range(3)
        for j in range(3)
        for k in range(3)
    ]


def silu_slope(values):
    logistic = jax.nn.sigmoid(values)
    return logistic * (1.0 + values * (1.0 - logistic))


def fine_conv(fine_field, weight, transposed):
    grown = extended(fine_field, (("wide", 1), ("narrow", 3)), 1)
    padded = jnp.pad(grown, ((0, 0), (0, 0), (1, 1), (0, 0)))
    kernel = weight.reshape(3, 3, 3, weight.shape[1], weight.shape[2])
    if transposed:
        kernel = kernel[::-1, ::-1, ::-1]
    result = lax.conv_general_dilated(
        padded[None],
        kernel,
        (1, 1, 1),
        "VALID",
        dimension_numbers=("NCDHW", "DHWIO", "NCDHW"),
        preferred_element_type=jnp.float32,
    )
    return result[0]


def to_patches(fine_field):
    channels = fine_field.shape[0]
    shaped = fine_field.reshape(
        channels, PATCH, fine_field.shape[2] // PATCH, PATCH, fine_field.shape[3] // PATCH, PATCH
    )
    return shaped.transpose(2, 4, 1, 3, 5, 0).reshape(-1, PATCH**3 * channels)


def send_patches(fine_field):
    return lax.all_to_all(to_patches(fine_field), "wide", split_axis=1, concat_axis=0, tiled=True)


def return_patches(patch_rows, fine_height, fine_depth, channels):
    returned = lax.all_to_all(patch_rows, "wide", split_axis=0, concat_axis=1, tiled=True)
    shaped = returned.reshape(
        fine_height // PATCH, fine_depth // PATCH, PATCH, PATCH, PATCH, channels
    )
    return shaped.transpose(5, 2, 0, 3, 1, 4).reshape(channels, PATCH, fine_height, fine_depth)


def coarse_faces(coarse_block):
    return extended(coarse_block, (("narrow", 2),), 1)


def wide_input_conv(coarse_block, weight_mat, out_count, transposed):
    grown = coarse_faces(coarse_block)
    products = jnp.einsum("xyzd,dk->xyzk", grown, weight_mat, preferred_element_type=jnp.float32)
    padded = jnp.pad(products, ((1, 1), (1, 1), (0, 0), (0, 0)))
    extent = coarse_block.shape[:3]
    summed = jnp.zeros(extent + (out_count,), jnp.float32)
    for tap_index, (a, b, c) in enumerate(shifts(transposed)):
        summed = (
            summed
            + padded[
                a : a + extent[0],
                b : b + extent[1],
                c : c + extent[2],
                tap_index * out_count : (tap_index + 1) * out_count,
            ]
        )
    return summed


def narrow_input_conv(coarse_block, weight_mat, transposed):
    grown = coarse_faces(coarse_block)
    padded = jnp.pad(grown, ((1, 1), (1, 1), (0, 0), (0, 0)))
    extent = coarse_block.shape[:3]
    columns = jnp.concatenate(
        [
            padded[a : a + extent[0], b : b + extent[1], c : c + extent[2]]
            for a, b, c in shifts(transposed)
        ],
        axis=3,
    )
    return jnp.einsum("xyzk,kd->xyzd", columns, weight_mat, preferred_element_type=jnp.float32)


BF = jnp.bfloat16
F32 = jnp.float32
LIMIT = 10 * 1024 * 1024
BESIDE = 32 * 1024 * 1024
NEAR, FAR = (1,), (6, 2, 4)
VMEM = pl.BlockSpec(memory_space=pltpu.VMEM)
SMEM = pl.BlockSpec(memory_space=pltpu.SMEM)


def nn_dot(lhs, rhs):
    return jnp.dot(lhs, rhs, preferred_element_type=F32)


def nt_dot(lhs, rhs):
    return lax.dot_general(lhs, rhs, (((1,), (1,)), ((), ())), preferred_element_type=F32)


def shape_of(dims, dtype):
    return jax.ShapeDtypeStruct(dims, dtype)


def kernel_call(kernel, places, arrays, outs, scratch=(), cost=None, rest=()):
    return pl.pallas_call(
        kernel,
        in_specs=[SMEM] * len(places) + [VMEM] * len(arrays) + [pl.BlockSpec(memory_space=pl.ANY)] * len(rest),
        out_specs=[VMEM] * len(outs),
        out_shape=outs,
        scratch_shapes=list(scratch),
        cost_estimate=cost and pl.CostEstimate(flops=0, bytes_accessed=cost, transcendentals=0),
        compiler_params=pltpu.CompilerParams(vmem_limit_bytes=LIMIT),
    )(*places, *arrays, *[pltpu.with_memory_space_constraint(a, pltpu.HBM) for a in rest])


def band_kernel(weight_ref, out_ref, *, back):
    row = lax.broadcasted_iota(jnp.int32, (32, 256), 0)
    lane = lax.broadcasted_iota(jnp.int32, (32, 256), 1)
    places = [(lane == row + 32 * (2 - k)).astype(BF) for k in range(3)]
    same = (
        lax.broadcasted_iota(jnp.int32, (32, 32), 0) == lax.broadcasted_iota(jnp.int32, (32, 32), 1)
    ).astype(BF)
    for i in range(3):
        for j in range(3):
            taps = None
            for k in range(3):
                t = 9 * i + 3 * j + k
                tap = nt_dot(same, weight_ref[26 - t]).astype(BF) if back else weight_ref[t]
                part = nn_dot(tap, places[k])
                taps = part if taps is None else taps + part
            columns = slice(256 * j, 256 * j + 256)

            def placed(start):
                moved = pltpu.roll(taps, start % 256, 1)
                return jnp.where((lane >= start) & (lane < start + 96), moved, 0.0).astype(BF)

            for d in range(8):
                out_ref[256 * i + 32 * d : 256 * i + 32 * d + 32, columns] = placed(32 * (d - 1))
            out_ref[768 + 64 * i : 800 + 64 * i, columns] = placed(-64)
            out_ref[800 + 64 * i : 832 + 64 * i, columns] = placed(224)
    out_ref[960:1024, :] = jnp.zeros((64, 768), BF)


def band_and_bias_kernel(step_ref, weight_ref, table_ref, out_ref, bias_ref, rows_ref, sem):
    step = step_ref[0]
    group = pl.ds(pl.multiple_of(step // 8 * 8, 8), 8)
    fetch = pltpu.make_async_copy(table_ref.at[group], rows_ref, sem)
    fetch.start()
    band_kernel(weight_ref, out_ref, back=False)
    fetch.wait()
    rows = rows_ref[...]
    chosen = lax.broadcasted_iota(jnp.int32, rows.shape, 0) == step % 8
    bias_ref[...] = jnp.sum(jnp.where(chosen, rows, jnp.zeros_like(rows)), axis=0, keepdims=True)


def banded(weight, back):
    (out,) = kernel_call(
        functools.partial(band_kernel, back=back), (), (weight,), [shape_of((1024, 768), BF)], cost=BESIDE
    )
    return out


def lane_place(d):
    row = lax.broadcasted_iota(jnp.int32, (32, 256), 0)
    lane = lax.broadcasted_iota(jnp.int32, (32, 256), 1)
    return (lane == row + 32 * d).astype(BF)


def to_rows(field_ref, cells_ref):
    cells_ref[...] = field_ref[...].astype(F32).reshape(2048, 32)
    rows = None
    for d in range(8):
        part = nn_dot(cells_ref[pl.ds(d, 256, stride=8), :].astype(BF), lane_place(d))
        rows = part if rows is None else rows + part
    return rows.astype(BF).reshape(8, 32, 256)


def pack_kernel(n_ref, w_ref, step_ref, volume_ref, cotangent_ref, *refs):
    del n_ref, step_ref
    out_refs = refs[:8]
    volume_copy_ref, cotangent_copy_ref, cells_ref, other_ref, field_ref, cot_ref, sems = refs[8:]
    first = pltpu.make_async_copy(volume_ref, volume_copy_ref, sems.at[0])
    second = pltpu.make_async_copy(cotangent_ref, cotangent_copy_ref, sems.at[1])
    first.start()
    second.start()
    first.wait()
    field_ref[...] = to_rows(volume_copy_ref, cells_ref)
    second.wait()
    cot_ref[...] = to_rows(cotangent_copy_ref, other_ref)
    for mask, out_ref in enumerate(out_refs):
        a = w_ref[0] ^ mask
        out_ref[0:32] = field_ref[(a + 7) & 7]
        out_ref[32:64] = field_ref[a]
        out_ref[64:96] = field_ref[(a + 1) & 7]
        out_ref[96:128] = cot_ref[a]


def arrived_planes(w, arrived_ref):
    none = jnp.zeros((32, 256), BF)
    before, own, after = [
        arrived_ref[:, 32 * s : 32 * s + 32, :].reshape(256, 256) for s in range(3)
    ]
    before = jnp.where(w == 0, jnp.concatenate([none, before[:224]], axis=0), before)
    after = jnp.where(w == 7, jnp.concatenate([after[32:], none], axis=0), after)
    return before, own, after


def returned_planes(w, returned_ref):
    rows = [returned_ref[7, 32:64]] + [returned_ref[a, 0:32] for a in range(8)] + [returned_ref[0, 32:64]]
    grown = jnp.concatenate(rows, axis=0)
    return grown[0:256], grown[32:288], grown[64:320]


def arrived_kernel(w_ref, *refs):
    planes_ref, own_ref, send_ref = refs[-3:]
    for mask in range(8):
        planes_ref[w_ref[0] ^ mask] = refs[mask][...]
    put_sides(arrived_planes(w_ref[0], planes_ref), own_ref, send_ref)


def returned_kernel(w_ref, planes_ref, band_ref, own_ref, send_ref):
    del band_ref
    put_sides(returned_planes(w_ref[0], planes_ref), own_ref, send_ref)


def put_sides(planes, own_ref, send_ref):
    source = lax.broadcasted_iota(jnp.int32, (256, 256), 0)
    target = lax.broadcasted_iota(jnp.int32, (256, 256), 1)
    sides = None
    for i, plane in enumerate(planes):
        high = (source >= 224) & (target == source - 224 + 64 * i)
        low = (source < 32) & (target == source + 64 * i + 32)
        part = nn_dot(plane, (high | low).astype(BF))
        sides = part if sides is None else sides + part
    even = (source & 1) == 0
    sides = jnp.where(even, pltpu.roll(sides, 255, 0), pltpu.roll(sides, 1, 0))
    low_side = (target & 32) != 0
    own = even == low_side
    zero = jnp.zeros_like(sides)
    own_ref[...] = jnp.where(own, sides, zero).astype(BF)
    send_ref[...] = jnp.where(own, zero, sides).astype(BF)


def main_kernel(w_ref, planes_ref, band_ref, out_ref, *, planes_of):
    lhs = jnp.concatenate(planes_of(w_ref[0], planes_ref), axis=1)
    out_ref[...] = nn_dot(lhs, band_ref[0:768])


def main_call(w, planes, band, planes_of):
    (out,) = kernel_call(
        functools.partial(main_kernel, planes_of=planes_of), (w,), (planes, band), [shape_of((256, 768), F32)]
    )
    return out


def fine_sum(n, main_ref, own_ref, got_ref, band_ref):
    lane = lax.broadcasted_iota(jnp.int32, (256, 256), 1)
    keep = ((lane & 32) != 0) == (n == 0)
    got = jnp.where(keep, got_ref[...].astype(F32), jnp.zeros((256, 256), F32))
    sides = (own_ref[...].astype(F32) + got).astype(BF)
    shifts_y = main_ref[...] + nn_dot(sides, band_ref[768:1024])
    y = (lax.broadcasted_iota(jnp.int32, (256, 1), 0) >> 1) & 15
    total = shifts_y[:, 256:512]
    zero = jnp.zeros_like(total)
    below = pltpu.roll(shifts_y[:, 0:256], 2, 0)
    above = pltpu.roll(shifts_y[:, 512:768], 254, 0)
    return total + jnp.where(y > 0, below, zero) + jnp.where(y < 15, above, zero)


def cell_rows(ref, b):
    return jnp.concatenate([ref[pl.ds(2 * b + z, 16, stride=16), :] for z in range(2)], axis=0)


def merge_kernel(
    n_ref, main_ref, own_ref, got_ref, band_ref, merge_ref, pre_ref, act_ref, sum_ref, sum_b_ref, rows_ref
):
    wide_rows = fine_sum(n_ref[0], main_ref, own_ref, got_ref, band_ref)
    rows_ref[0] = wide_rows[:, :128]
    rows_ref[1] = wide_rows[:, 128:]
    total = None
    for b in range(8):
        pre = jnp.concatenate([cell_rows(rows_ref.at[h], b) for h in range(2)], axis=1)
        pre_ref[b] = pre
        act = (pre * jax.nn.sigmoid(pre)).astype(BF)
        act_ref[b] = act
        part = nn_dot(act, merge_ref[256 * b : 256 * b + 256])
        total = part if total is None else total + part
    sum_ref[...] = total
    sum_b_ref[...] = total.astype(BF)


def cot_kernel(planes_ref, cot_ref, rows_ref):
    rows = planes_ref[:, 96:128, :].reshape(256, 256).astype(F32)
    rows_ref[0] = rows[:, :128]
    rows_ref[1] = rows[:, 128:]
    for b in range(8):
        cot_ref[b] = jnp.concatenate([cell_rows(rows_ref.at[h], b) for h in range(2)], axis=1).astype(BF)


def final_kernel(n_ref, main_ref, own_ref, got_ref, band_ref, out_ref, cells_ref):
    rows = fine_sum(n_ref[0], main_ref, own_ref, got_ref, band_ref).astype(BF)
    for d in range(8):
        cells_ref[pl.ds(d, 256, stride=8), :] = nt_dot(rows, lane_place(d))
    out_ref[...] = cells_ref[...].astype(BF).reshape(8, 16, 16, 32)


def put_columns(cols_ref, cells):
    row = lax.broadcasted_iota(jnp.int32, (64, 1), 0)
    along_y, along_x = row & 1, (row >> 1) & 7
    zero = jnp.zeros_like(cells)
    none = jnp.zeros((16, cells.shape[1]), BF)
    below = jnp.where(along_y == 1, pltpu.roll(cells, 1, 0), zero)
    above = jnp.where(along_y == 0, pltpu.roll(cells, 63, 0), zero)
    for j, moved_y in enumerate((below, cells, above)):
        before = jnp.where(along_x > 0, pltpu.roll(moved_y, 2, 0), zero)
        after = jnp.where(along_x < 7, pltpu.roll(moved_y, 62, 0), zero)
        for i, moved in enumerate((before, moved_y, after)):
            rows = moved.astype(BF)
            cols_ref[9 * i + 3 * j] = jnp.concatenate([none, rows[:48]], axis=0)
            cols_ref[9 * i + 3 * j + 1] = rows
            cols_ref[9 * i + 3 * j + 2] = jnp.concatenate([rows[16:], none], axis=0)


def both_halves(n, mine, got, axis):
    first = n == 0
    return jnp.concatenate([jnp.where(first, mine, got), jnp.where(first, got, mine)], axis=axis)


def conv_sum(cols_ref, weight_of, flipped, dot):
    total = None
    for t in range(27):
        part = dot(cols_ref[26 - t if flipped else t], weight_of(t))
        total = part if total is None else total + part
    return total


def feature_rows(n, ref):
    half = ref.shape[1] // 2
    return lambda t: ref[t, pl.ds(pl.multiple_of(n * half, half), half), :]


def feature_columns(n, ref):
    half = ref.shape[2] // 2
    return lambda t: ref[t, :, pl.ds(pl.multiple_of(n * half, half), half)]


def outer_kernel(n_ref, mine_ref, got_ref, weight_ref, sum_ref, cols_ref, *, flipped, dot, part_of):
    n = n_ref[0]
    put_columns(cols_ref, both_halves(n, mine_ref[...].astype(F32), got_ref[...].astype(F32), 0))
    sum_ref[...] = conv_sum(cols_ref, part_of(n, weight_ref), flipped, dot)


def inner_forward_kernel(
    n_ref, mine_ref, got_ref, bias_ref, weight_ref, gate_ref, sum_ref, sum_b_ref, cols_ref
):
    gate = mine_ref[...] + got_ref[...] + bias_ref[...]
    gate_ref[...] = gate
    put_columns(cols_ref, gate * jax.nn.sigmoid(gate))
    total = conv_sum(cols_ref, feature_columns(n_ref[0], weight_ref), False, nn_dot)
    sum_ref[...] = total
    sum_b_ref[...] = total.astype(BF)


def inner_backward_kernel(
    n_ref, mine_ref, got_ref, gate_ref, weight_ref, sum_ref, sum_b_ref, cols_ref
):
    put_columns(cols_ref, (mine_ref[...] + got_ref[...]) * silu_slope(gate_ref[...]))
    total = conv_sum(cols_ref, feature_rows(n_ref[0], weight_ref), True, nt_dot)
    sum_ref[...] = total
    sum_b_ref[...] = total.astype(BF)


def expand_kernel(
    n_ref, merged_ref, mine_ref, got_ref, act_ref, cot_ref, expand_ref, grad_ref, sum_ref, sum_b_ref
):
    branch = both_halves(n_ref[0], mine_ref[...].astype(F32), got_ref[...].astype(F32), 1)
    residual = (merged_ref[...] + branch).astype(BF)
    total = None
    for b in range(8):
        part = expand_ref[:, 256 * b : 256 * b + 256]
        expanded = nn_dot(residual, part).astype(BF)
        combined = act_ref[b].astype(F32) + expanded.astype(F32)
        grad = (cot_ref[b].astype(F32) * silu_slope(combined)).astype(BF)
        grad_ref[b] = grad
        more = nt_dot(grad, part)
        total = more if total is None else total + more
    sum_ref[...] = total
    sum_b_ref[...] = total.astype(BF)


def grad_kernel(
    n_ref, w_ref, res_ref, mine_ref, got_ref, comb_ref, pre_ref, merge_ref, out_ref, rows_ref
):
    w = w_ref[0]
    conv = both_halves(n_ref[0], mine_ref[...].astype(F32), got_ref[...].astype(F32), 1)
    merged_grad = (res_ref[...] + conv).astype(BF)
    for b in range(8):
        cells = nt_dot(merged_grad, merge_ref[256 * b : 256 * b + 256]).astype(BF)
        grad = cells.astype(F32) + comb_ref[b].astype(F32)
        grad = grad * silu_slope(pre_ref[b])
        for z in range(2):
            for h in range(2):
                rows_ref[h, pl.ds(2 * b + z, 16, stride=16), :] = grad[
                    16 * z : 16 * z + 16, 128 * h : 128 * h + 128
                ]
    rows = jnp.concatenate([rows_ref[0], rows_ref[1]], axis=1).astype(BF)
    none = jnp.zeros((32, 256), BF)
    for x in range(8):
        ahead = rows[32 * x + 32 : 32 * x + 64] if x < 7 else none
        behind = rows[32 * x - 32 : 32 * x] if x > 0 else none
        out_ref[x, 0:32] = rows[32 * x : 32 * x + 32]
        out_ref[x, 32:64] = jnp.where(w == 0, ahead, behind)


def swap_narrow(value):
    return lax.ppermute(value, "narrow", [(0, 1), (1, 0)])


def near_kernel(part_ref, *refs, count):
    pair_ref, pair_b_ref = refs[-2:]
    pair = part_ref[...]
    for got_ref in refs[:count]:
        pair += got_ref[...].astype(F32)
    pair_ref[...] = pair
    pair_b_ref[...] = pair.astype(BF)


def features_kernel(n_ref, pair_ref, one_ref, two_ref, three_ref, *refs):
    sum_ref, mine_ref, send_ref = refs[-3:]
    total = pair_ref[...] + one_ref[...].astype(F32) + two_ref[...].astype(F32) + three_ref[...].astype(F32)
    sum_ref[...] = total
    half = total.shape[1] // 2
    low, high = total[:, :half], total[:, half:]
    first = n_ref[0] == 0
    mine_ref[...] = jnp.where(first, low, high).astype(BF)
    send_ref[...] = jnp.where(first, high, low).astype(BF)


def cells_kernel(n_ref, pair_ref, one_ref, two_ref, three_ref, mine_ref, send_ref):
    total = pair_ref[...] + one_ref[...].astype(F32) + two_ref[...].astype(F32) + three_ref[...].astype(F32)
    half = total.shape[0] // 2
    low, high = total[:half], total[half:]
    first = n_ref[0] == 0
    mine_ref[...] = jnp.where(first, low, high)
    send_ref[...] = jnp.where(first, high, low).astype(BF)


def wide_terms(part, part_b, rest=()):
    def partner(value, mask):
        return lax.ppermute(value, "wide", [(i, i ^ mask) for i in range(8)])

    shape = part.shape
    pair, pair_b = kernel_call(
        functools.partial(near_kernel, count=len(NEAR)), (), (part, *[partner(part_b, mask) for mask in NEAR]),
        [shape_of(shape, F32), shape_of(shape, BF)], rest=rest,
    )
    return (pair, *[partner(pair_b, mask) for mask in FAR])


def to_feature_halves(n, part, part_b, rest=()):
    terms = wide_terms(part, part_b, rest)
    cells, features = part.shape
    half_shape = shape_of((cells, features // 2), BF)
    total, mine, send = kernel_call(
        features_kernel, (n,), terms, [shape_of(part.shape, F32), half_shape, half_shape]
    )
    return total, mine, swap_narrow(send)


def to_cell_halves(n, part, part_b):
    terms = wide_terms(part, part_b)
    cells, features = part.shape
    half = (cells // 2, features)
    mine, send = kernel_call(cells_kernel, (n,), terms, [shape_of(half, F32), shape_of(half, BF)])
    return mine, swap_narrow(send)


def across_wide(messages):
    return [messages[0]] + [
        lax.ppermute(messages[mask], "wide", [(i, i ^ mask) for i in range(8)]) for mask in range(1, 8)
    ]


def eight_shards(
    volume,
    cotangent,
    fine_weight,
    merge_weight,
    hidden_weight,
    step_table,
    output_weight,
    expand_weight,
    timestep,
):
    features = merge_weight.shape[1]
    hidden = hidden_weight.shape[2]
    half = features // 2
    w = lax.axis_index("wide").astype(jnp.int32).reshape(1)
    n = lax.axis_index("narrow").astype(jnp.int32).reshape(1)

    fine_cells = pltpu.VMEM((2048, 32), F32)
    fine_field = pltpu.VMEM((8, 16, 16, 32), BF)
    fine_blocks = pltpu.VMEM((8, 32, 256), BF)
    outgoing = kernel_call(
        pack_kernel, (n, w, timestep), (), [shape_of((128, 256), BF)] * 8,
        [fine_field, fine_field, fine_cells, fine_cells, fine_blocks, fine_blocks, pltpu.SemaphoreType.DMA((2,))],
        rest=(volume.transpose(1, 2, 3, 0), cotangent.transpose(1, 2, 3, 0)),
    )
    messages = across_wide(outgoing)
    band, bias = kernel_call(
        band_and_bias_kernel, (timestep,), (fine_weight,),
        [shape_of((1024, 768), BF), shape_of((1, hidden), F32)],
        [pltpu.VMEM((8, hidden), F32), pltpu.SemaphoreType.DMA], cost=BESIDE, rest=(step_table,),
    )
    side_shape = shape_of((256, 256), BF)
    arrived, sides, sent = kernel_call(
        arrived_kernel, (w,), (*messages, band), [shape_of((8, 128, 256), BF), side_shape, side_shape],
        rest=(merge_weight,),
    )
    fine_rows = pltpu.VMEM((2, 256, 128), F32)
    sum_shapes = [shape_of((32, features), F32), shape_of((32, features), BF)]
    pre_act, act, merged_part, merged_part_b = kernel_call(
        merge_kernel,
        (n,),
        (main_call(w, arrived, band, arrived_planes), sides, swap_narrow(sent), band, merge_weight),
        [shape_of((8, 32, 256), F32), shape_of((8, 32, 256), BF)] + sum_shapes,
        [fine_rows],
    )
    (cot,) = kernel_call(cot_kernel, (), (arrived,), [shape_of((8, 32, 256), BF)], [fine_rows])
    merged, mine, got = to_feature_halves(n, merged_part, merged_part_b, (hidden_weight, output_weight))

    gate_shape = shape_of((64, hidden), F32)
    half_shapes = [shape_of((64, half), F32), shape_of((64, half), BF)]
    outer_columns = [pltpu.VMEM((27, 64, half), BF)]
    inner_columns = [pltpu.VMEM((27, 64, hidden), BF)]

    (gate_part,) = kernel_call(
        functools.partial(outer_kernel, flipped=False, dot=nn_dot, part_of=feature_rows),
        (n,), (mine, got, hidden_weight), [gate_shape], outer_columns,
    )
    gate_pre, branch_part, branch_part_b = kernel_call(
        inner_forward_kernel,
        (n,), (gate_part, swap_narrow(gate_part), bias, output_weight), [gate_shape] + half_shapes, inner_columns,
    )
    mine, got = to_cell_halves(n, branch_part, branch_part_b)
    grad_comb, res_part, res_part_b = kernel_call(
        expand_kernel,
        (n,), (merged, mine, got, act, cot, expand_weight),
        [shape_of((8, 32, 256), BF)] + sum_shapes,
    )
    grad_res, mine, got = to_feature_halves(n, res_part, res_part_b)
    (hidden_part,) = kernel_call(
        functools.partial(outer_kernel, flipped=True, dot=nt_dot, part_of=feature_columns),
        (n,), (mine, got, output_weight), [gate_shape], outer_columns,
    )
    conv_part, conv_part_b = kernel_call(
        inner_backward_kernel,
        (n,), (hidden_part, swap_narrow(hidden_part), gate_pre, hidden_weight),
        half_shapes, inner_columns,
    )
    mine, got = to_cell_halves(n, conv_part, conv_part_b)
    (leaving,) = kernel_call(
        grad_kernel,
        (n, w), (grad_res, mine, got, grad_comb, pre_act, merge_weight),
        [shape_of((8, 64, 256), BF)], [fine_rows],
    )
    returned = lax.all_to_all(leaving, "wide", split_axis=0, concat_axis=0, tiled=True)
    band = banded(fine_weight, True)
    sides, sent = kernel_call(returned_kernel, (w,), (returned, band), [side_shape, side_shape])
    (result,) = kernel_call(
        final_kernel,
        (n,), (main_call(w, returned, band, returned_planes), sides, swap_narrow(sent), band),
        [shape_of((8, 16, 16, 32), BF)], [fine_cells],
    )
    return result.transpose(3, 0, 1, 2)


def shards(
    volume,
    cotangent,
    fine_weight,
    merge_weight,
    hidden_weight,
    step_table,
    output_weight,
    expand_weight,
    timestep,
):
    channels = volume.shape[0]
    fine_height = volume.shape[2]
    fine_depth = volume.shape[3]
    wide_count = lax.axis_size("wide")
    features = merge_weight.shape[1]
    hidden_local = hidden_weight.shape[2]
    coarse_grid = (wide_count, fine_height // PATCH, fine_depth // PATCH)
    hidden_mat = hidden_weight.transpose(1, 0, 2).reshape(features, 27 * hidden_local)
    output_mat = output_weight.reshape(27 * hidden_local, features)
    output_back = output_weight.transpose(2, 0, 1).reshape(features, 27 * hidden_local)
    hidden_back = hidden_weight.transpose(0, 2, 1).reshape(27 * hidden_local, features)

    def total_rows(partial_value):
        return lax.psum(partial_value, "wide")

    pre_act = fine_conv(volume, fine_weight, False)
    activated = jax.nn.silu(pre_act).astype(jnp.bfloat16)
    received = send_patches(activated)
    merged = total_rows(jnp.dot(received, merge_weight, preferred_element_type=jnp.float32))
    coarse_in = merged.astype(jnp.bfloat16).reshape(coarse_grid + (features,))
    bias_row = step_table[timestep[0]]
    gate_pre = wide_input_conv(coarse_in, hidden_mat, hidden_local, False) + bias_row
    hidden_act = jax.nn.silu(gate_pre).astype(jnp.bfloat16)
    branch = total_rows(narrow_input_conv(hidden_act, output_mat, False).reshape(-1, features))
    residual_sum = (merged + branch).astype(jnp.bfloat16)
    expanded = jnp.dot(residual_sum, expand_weight, preferred_element_type=jnp.float32).astype(
        jnp.bfloat16
    )
    expanded_field = return_patches(expanded, fine_height, fine_depth, channels)
    combined = activated.astype(jnp.float32) + expanded_field.astype(jnp.float32)
    grad_comb = (cotangent.astype(jnp.float32) * silu_slope(combined)).astype(jnp.bfloat16)
    grad_res = total_rows(
        jnp.einsum(
            "nk,dk->nd", send_patches(grad_comb), expand_weight, preferred_element_type=jnp.float32
        )
    )
    grad_res_b = grad_res.astype(jnp.bfloat16).reshape(coarse_grid + (features,))
    grad_hidden = wide_input_conv(grad_res_b, output_back, hidden_local, True)
    grad_gate = (grad_hidden * silu_slope(gate_pre)).astype(jnp.bfloat16)
    grad_conv = total_rows(narrow_input_conv(grad_gate, hidden_back, True).reshape(-1, features))
    grad_merged = (grad_res + grad_conv).astype(jnp.bfloat16)
    grad_cells = jnp.einsum(
        "nd,kd->nk", grad_merged, merge_weight, preferred_element_type=jnp.float32
    ).astype(jnp.bfloat16)
    grad_act = return_patches(grad_cells, fine_height, fine_depth, channels).astype(
        jnp.float32
    ) + grad_comb.astype(jnp.float32)
    grad_pre = (grad_act * silu_slope(pre_act)).astype(jnp.bfloat16)
    return fine_conv(grad_pre, fine_weight.transpose(0, 2, 1), True).astype(jnp.bfloat16)


def solution(mesh):
    in_specs = (
        P(None, ("groups", "wide"), None, "narrow"),
        P(None, ("groups", "wide"), None, "narrow"),
        P(),
        P("wide", None),
        P(None, None, "wide"),
        P(None, "wide"),
        P(None, "wide", None),
        P(None, "wide"),
        P("groups"),
    )
    out_specs = P(None, ("groups", "wide"), None, "narrow")
    sizes = dict(mesh.shape)
    fits = sizes["wide"] == PATCH and sizes["narrow"] == 2
    body = eight_shards if fits else shards
    return jax.shard_map(body, mesh=mesh, in_specs=in_specs, out_specs=out_specs, check_vma=False)
```

```python
import functools

import jax
import jax.numpy as jnp
from jax import lax
from jax.experimental import pallas as pl
from jax.experimental.pallas import tpu as pltpu
from jax.sharding import PartitionSpec as P

PATCH = 8


def extended(cells, sides, width):
    for axis, dim in sides:
        count = lax.axis_size(axis)
        ends = count - 1
        head = lax.slice_in_dim(cells, 0, width, axis=dim)
        tail = lax.slice_in_dim(cells, cells.shape[dim] - width, cells.shape[dim], axis=dim)
        cells = jnp.concatenate(
            [
                lax.ppermute(tail, axis, [(i, (i + 1) % count) for i in range(ends)]),
                cells,
                lax.ppermute(head, axis, [((i + 1) % count, i) for i in range(ends)]),
            ],
            axis=dim,
        )
    return cells


def shifts(transposed):
    return [
        (2 - i, 2 - j, 2 - k) if transposed else (i, j, k)
        for i in range(3)
        for j in range(3)
        for k in range(3)
    ]


def silu_slope(values):
    logistic = jax.nn.sigmoid(values)
    return logistic * (1.0 + values * (1.0 - logistic))


def fine_conv(fine_field, weight, transposed):
    grown = extended(fine_field, (("wide", 1), ("narrow", 3)), 1)
    padded = jnp.pad(grown, ((0, 0), (0, 0), (1, 1), (0, 0)))
    kernel = weight.reshape(3, 3, 3, weight.shape[1], weight.shape[2])
    if transposed:
        kernel = kernel[::-1, ::-1, ::-1]
    result = lax.conv_general_dilated(
        padded[None],
        kernel,
        (1, 1, 1),
        "VALID",
        dimension_numbers=("NCDHW", "DHWIO", "NCDHW"),
        preferred_element_type=jnp.float32,
    )
    return result[0]


def to_patches(fine_field):
    channels = fine_field.shape[0]
    shaped = fine_field.reshape(
        channels, PATCH, fine_field.shape[2] // PATCH, PATCH, fine_field.shape[3] // PATCH, PATCH
    )
    return shaped.transpose(2, 4, 1, 3, 5, 0).reshape(-1, PATCH**3 * channels)


def send_patches(fine_field):
    return lax.all_to_all(to_patches(fine_field), "wide", split_axis=1, concat_axis=0, tiled=True)


def return_patches(patch_rows, fine_height, fine_depth, channels):
    returned = lax.all_to_all(patch_rows, "wide", split_axis=0, concat_axis=1, tiled=True)
    shaped = returned.reshape(
        fine_height // PATCH, fine_depth // PATCH, PATCH, PATCH, PATCH, channels
    )
    return shaped.transpose(5, 2, 0, 3, 1, 4).reshape(channels, PATCH, fine_height, fine_depth)


def coarse_faces(coarse_block):
    return extended(coarse_block, (("narrow", 2),), 1)


def wide_input_conv(coarse_block, weight_mat, out_count, transposed):
    grown = coarse_faces(coarse_block)
    products = jnp.einsum("xyzd,dk->xyzk", grown, weight_mat, preferred_element_type=jnp.float32)
    padded = jnp.pad(products, ((1, 1), (1, 1), (0, 0), (0, 0)))
    extent = coarse_block.shape[:3]
    summed = jnp.zeros(extent + (out_count,), jnp.float32)
    for tap_index, (a, b, c) in enumerate(shifts(transposed)):
        summed = (
            summed
            + padded[
                a : a + extent[0],
                b : b + extent[1],
                c : c + extent[2],
                tap_index * out_count : (tap_index + 1) * out_count,
            ]
        )
    return summed


def narrow_input_conv(coarse_block, weight_mat, transposed):
    grown = coarse_faces(coarse_block)
    padded = jnp.pad(grown, ((1, 1), (1, 1), (0, 0), (0, 0)))
    extent = coarse_block.shape[:3]
    columns = jnp.concatenate(
        [
            padded[a : a + extent[0], b : b + extent[1], c : c + extent[2]]
            for a, b, c in shifts(transposed)
        ],
        axis=3,
    )
    return jnp.einsum("xyzk,kd->xyzd", columns, weight_mat, preferred_element_type=jnp.float32)


BF = jnp.bfloat16
F32 = jnp.float32
LIMIT = 10 * 1024 * 1024
BESIDE = 32 * 1024 * 1024
NEAR, FAR = (1,), (6, 2, 4)
VMEM = pl.BlockSpec(memory_space=pltpu.VMEM)
SMEM = pl.BlockSpec(memory_space=pltpu.SMEM)


def nn_dot(lhs, rhs):
    return jnp.dot(lhs, rhs, preferred_element_type=F32)


def nt_dot(lhs, rhs):
    return lax.dot_general(lhs, rhs, (((1,), (1,)), ((), ())), preferred_element_type=F32)


def shape_of(dims, dtype):
    return jax.ShapeDtypeStruct(dims, dtype)


def kernel_call(kernel, places, arrays, outs, scratch=(), cost=None, rest=()):
    return pl.pallas_call(
        kernel,
        in_specs=[SMEM] * len(places) + [VMEM] * len(arrays) + [pl.BlockSpec(memory_space=pl.ANY)] * len(rest),
        out_specs=[VMEM] * len(outs),
        out_shape=outs,
        scratch_shapes=list(scratch),
        cost_estimate=cost and pl.CostEstimate(flops=0, bytes_accessed=cost, transcendentals=0),
        compiler_params=pltpu.CompilerParams(vmem_limit_bytes=LIMIT),
    )(*places, *arrays, *[pltpu.with_memory_space_constraint(a, pltpu.HBM) for a in rest])


def band_kernel(weight_ref, out_ref, *, back):
    row = lax.broadcasted_iota(jnp.int32, (32, 256), 0)
    lane = lax.broadcasted_iota(jnp.int32, (32, 256), 1)
    places = [(lane == row + 32 * (2 - k)).astype(BF) for k in range(3)]
    same = (
        lax.broadcasted_iota(jnp.int32, (32, 32), 0) == lax.broadcasted_iota(jnp.int32, (32, 32), 1)
    ).astype(BF)
    for i in range(3):
        for j in range(3):
            taps = None
            for k in range(3):
                t = 9 * i + 3 * j + k
                tap = nt_dot(same, weight_ref[26 - t]).astype(BF) if back else weight_ref[t]
                part = nn_dot(tap, places[k])
                taps = part if taps is None else taps + part
            columns = slice(256 * j, 256 * j + 256)

            def placed(start):
                moved = pltpu.roll(taps, start % 256, 1)
                return jnp.where((lane >= start) & (lane < start + 96), moved, 0.0).astype(BF)

            for d in range(8):
                out_ref[256 * i + 32 * d : 256 * i + 32 * d + 32, columns] = placed(32 * (d - 1))
            out_ref[768 + 64 * i : 800 + 64 * i, columns] = placed(-64)
            out_ref[800 + 64 * i : 832 + 64 * i, columns] = placed(224)
    out_ref[960:1024, :] = jnp.zeros((64, 768), BF)


def band_and_bias_kernel(step_ref, weight_ref, table_ref, out_ref, bias_ref, rows_ref, sem):
    step = step_ref[0]
    group = pl.ds(pl.multiple_of(step // 8 * 8, 8), 8)
    fetch = pltpu.make_async_copy(table_ref.at[group], rows_ref, sem)
    fetch.start()
    band_kernel(weight_ref, out_ref, back=False)
    fetch.wait()
    rows = rows_ref[...]
    chosen = lax.broadcasted_iota(jnp.int32, rows.shape, 0) == step % 8
    bias_ref[...] = jnp.sum(jnp.where(chosen, rows, jnp.zeros_like(rows)), axis=0, keepdims=True)


def banded(weight, back):
    (out,) = kernel_call(
        functools.partial(band_kernel, back=back), (), (weight,), [shape_of((1024, 768), BF)], cost=BESIDE
    )
    return out


def lane_place(d):
    row = lax.broadcasted_iota(jnp.int32, (32, 256), 0)
    lane = lax.broadcasted_iota(jnp.int32, (32, 256), 1)
    return (lane == row + 32 * d).astype(BF)


def to_rows(field_ref, cells_ref):
    cells_ref[...] = field_ref[...].astype(F32).reshape(2048, 32)
    rows = None
    for d in range(8):
        part = nn_dot(cells_ref[pl.ds(d, 256, stride=8), :].astype(BF), lane_place(d))
        rows = part if rows is None else rows + part
    return rows.astype(BF).reshape(8, 32, 256)


def pack_kernel(n_ref, w_ref, step_ref, volume_ref, cotangent_ref, *refs):
    del n_ref, step_ref
    out_refs = refs[:8]
    volume_copy_ref, cotangent_copy_ref, cells_ref, other_ref, field_ref, cot_ref, sems = refs[8:]
    first = pltpu.make_async_copy(volume_ref, volume_copy_ref, sems.at[0])
    second = pltpu.make_async_copy(cotangent_ref, cotangent_copy_ref, sems.at[1])
    first.start()
    second.start()
    first.wait()
    field_ref[...] = to_rows(volume_copy_ref, cells_ref)
    second.wait()
    cot_ref[...] = to_rows(cotangent_copy_ref, other_ref)
    for mask, out_ref in enumerate(out_refs):
        a = w_ref[0] ^ mask
        out_ref[0:32] = field_ref[(a + 7) & 7]
        out_ref[32:64] = field_ref[a]
        out_ref[64:96] = field_ref[(a + 1) & 7]
        out_ref[96:128] = cot_ref[a]


def arrived_planes(w, arrived_ref):
    none = jnp.zeros((32, 256), BF)
    before, own, after = [
        arrived_ref[:, 32 * s : 32 * s + 32, :].reshape(256, 256) for s in range(3)
    ]
    before = jnp.where(w == 0, jnp.concatenate([none, before[:224]], axis=0), before)
    after = jnp.where(w == 7, jnp.concatenate([after[32:], none], axis=0), after)
    return before, own, after


def returned_planes(w, returned_ref):
    rows = [returned_ref[7, 32:64]] + [returned_ref[a, 0:32] for a in range(8)] + [returned_ref[0, 32:64]]
    grown = jnp.concatenate(rows, axis=0)
    return grown[0:256], grown[32:288], grown[64:320]


def arrived_kernel(w_ref, *refs):
    planes_ref, own_ref, send_ref = refs[-3:]
    for mask in range(8):
        planes_ref[w_ref[0] ^ mask] = refs[mask][...]
    put_sides(arrived_planes(w_ref[0], planes_ref), own_ref, send_ref)


def returned_kernel(w_ref, planes_ref, band_ref, own_ref, send_ref):
    del band_ref
    put_sides(returned_planes(w_ref[0], planes_ref), own_ref, send_ref)


def put_sides(planes, own_ref, send_ref):
    source = lax.broadcasted_iota(jnp.int32, (256, 256), 0)
    target = lax.broadcasted_iota(jnp.int32, (256, 256), 1)
    sides = None
    for i, plane in enumerate(planes):
        high = (source >= 224) & (target == source - 224 + 64 * i)
        low = (source < 32) & (target == source + 64 * i + 32)
        part = nn_dot(plane, (high | low).astype(BF))
        sides = part if sides is None else sides + part
    even = (source & 1) == 0
    sides = jnp.where(even, pltpu.roll(sides, 255, 0), pltpu.roll(sides, 1, 0))
    low_side = (target & 32) != 0
    own = even == low_side
    zero = jnp.zeros_like(sides)
    own_ref[...] = jnp.where(own, sides, zero).astype(BF)
    send_ref[...] = jnp.where(own, zero, sides).astype(BF)


def main_kernel(w_ref, planes_ref, band_ref, out_ref, *, planes_of):
    lhs = jnp.concatenate(planes_of(w_ref[0], planes_ref), axis=1)
    out_ref[...] = nn_dot(lhs, band_ref[0:768])


def main_call(w, planes, band, planes_of):
    (out,) = kernel_call(
        functools.partial(main_kernel, planes_of=planes_of), (w,), (planes, band), [shape_of((256, 768), F32)]
    )
    return out


def fine_sum(n, main_ref, own_ref, got_ref, band_ref):
    lane = lax.broadcasted_iota(jnp.int32, (256, 256), 1)
    keep = ((lane & 32) != 0) == (n == 0)
    got = jnp.where(keep, got_ref[...].astype(F32), jnp.zeros((256, 256), F32))
    sides = (own_ref[...].astype(F32) + got).astype(BF)
    shifts_y = main_ref[...] + nn_dot(sides, band_ref[768:1024])
    y = (lax.broadcasted_iota(jnp.int32, (256, 1), 0) >> 1) & 15
    total = shifts_y[:, 256:512]
    zero = jnp.zeros_like(total)
    below = pltpu.roll(shifts_y[:, 0:256], 2, 0)
    above = pltpu.roll(shifts_y[:, 512:768], 254, 0)
    return total + jnp.where(y > 0, below, zero) + jnp.where(y < 15, above, zero)


def cell_rows(ref, b):
    return jnp.concatenate([ref[pl.ds(2 * b + z, 16, stride=16), :] for z in range(2)], axis=0)


def merge_kernel(
    n_ref, main_ref, own_ref, got_ref, band_ref, merge_ref, pre_ref, act_ref, sum_ref, sum_b_ref, rows_ref
):
    wide_rows = fine_sum(n_ref[0], main_ref, own_ref, got_ref, band_ref)
    rows_ref[0] = wide_rows[:, :128]
    rows_ref[1] = wide_rows[:, 128:]
    total = None
    for b in range(8):
        pre = jnp.concatenate([cell_rows(rows_ref.at[h], b) for h in range(2)], axis=1)
        pre_ref[b] = pre
        act = (pre * jax.nn.sigmoid(pre)).astype(BF)
        act_ref[b] = act
        part = nn_dot(act, merge_ref[256 * b : 256 * b + 256])
        total = part if total is None else total + part
    sum_ref[...] = total
    sum_b_ref[...] = total.astype(BF)


def cot_kernel(planes_ref, cot_ref, rows_ref):
    rows = planes_ref[:, 96:128, :].reshape(256, 256).astype(F32)
    rows_ref[0] = rows[:, :128]
    rows_ref[1] = rows[:, 128:]
    for b in range(8):
        cot_ref[b] = jnp.concatenate([cell_rows(rows_ref.at[h], b) for h in range(2)], axis=1).astype(BF)


def final_kernel(n_ref, main_ref, own_ref, got_ref, band_ref, out_ref, cells_ref):
    rows = fine_sum(n_ref[0], main_ref, own_ref, got_ref, band_ref).astype(BF)
    for d in range(8):
        cells_ref[pl.ds(d, 256, stride=8), :] = nt_dot(rows, lane_place(d))
    out_ref[...] = cells_ref[...].astype(BF).reshape(8, 16, 16, 32)


def put_columns(cols_ref, cells):
    row = lax.broadcasted_iota(jnp.int32, (64, 1), 0)
    along_y, along_x = row & 1, (row >> 1) & 7
    zero = jnp.zeros_like(cells)
    none = jnp.zeros((16, cells.shape[1]), BF)
    below = jnp.where(along_y == 1, pltpu.roll(cells, 1, 0), zero)
    above = jnp.where(along_y == 0, pltpu.roll(cells, 63, 0), zero)
    for j, moved_y in enumerate((below, cells, above)):
        before = jnp.where(along_x > 0, pltpu.roll(moved_y, 2, 0), zero)
        after = jnp.where(along_x < 7, pltpu.roll(moved_y, 62, 0), zero)
        for i, moved in enumerate((before, moved_y, after)):
            rows = moved.astype(BF)
            cols_ref[9 * i + 3 * j] = jnp.concatenate([none, rows[:48]], axis=0)
            cols_ref[9 * i + 3 * j + 1] = rows
            cols_ref[9 * i + 3 * j + 2] = jnp.concatenate([rows[16:], none], axis=0)


def both_halves(n, mine, got, axis):
    first = n == 0
    return jnp.concatenate([jnp.where(first, mine, got), jnp.where(first, got, mine)], axis=axis)


def conv_sum(cols_ref, weight_of, back):
    total = None
    for t in range(27):
        cells = cols_ref[26 - t if back else t]
        part = nt_dot(weight_of(t), cells) if back else nn_dot(cells, weight_of(t))
        total = part if total is None else total + part
    return total.T if back else total


def feature_rows(n, ref):
    half = ref.shape[1] // 2
    return lambda t: ref[t, pl.ds(pl.multiple_of(n * half, half), half), :]


def feature_columns(n, ref):
    half = ref.shape[2] // 2
    return lambda t: ref[t, :, pl.ds(pl.multiple_of(n * half, half), half)]


def outer_kernel(n_ref, mine_ref, got_ref, weight_ref, sum_ref, cols_ref, *, back, part_of):
    n = n_ref[0]
    put_columns(cols_ref, both_halves(n, mine_ref[...].astype(F32), got_ref[...].astype(F32), 0))
    sum_ref[...] = conv_sum(cols_ref, part_of(n, weight_ref), back)


def inner_forward_kernel(
    n_ref, mine_ref, got_ref, bias_ref, weight_ref, gate_ref, sum_ref, sum_b_ref, cols_ref
):
    gate = mine_ref[...] + got_ref[...] + bias_ref[...]
    gate_ref[...] = gate
    put_columns(cols_ref, gate * jax.nn.sigmoid(gate))
    total = conv_sum(cols_ref, feature_columns(n_ref[0], weight_ref), False)
    sum_ref[...] = total
    sum_b_ref[...] = total.astype(BF)


def inner_backward_kernel(
    n_ref, mine_ref, got_ref, gate_ref, weight_ref, sum_ref, sum_b_ref, cols_ref
):
    put_columns(cols_ref, (mine_ref[...] + got_ref[...]) * silu_slope(gate_ref[...]))
    total = conv_sum(cols_ref, feature_rows(n_ref[0], weight_ref), True)
    sum_ref[...] = total
    sum_b_ref[...] = total.astype(BF)


def expand_kernel(
    n_ref, merged_ref, mine_ref, got_ref, act_ref, cot_ref, expand_ref, grad_ref, sum_ref, sum_b_ref
):
    branch = both_halves(n_ref[0], mine_ref[...].astype(F32), got_ref[...].astype(F32), 1)
    residual = (merged_ref[...] + branch).astype(BF)
    total = None
    for b in range(8):
        part = expand_ref[:, 256 * b : 256 * b + 256]
        expanded = nn_dot(residual, part).astype(BF)
        combined = act_ref[b].astype(F32) + expanded.astype(F32)
        grad = (cot_ref[b].astype(F32) * silu_slope(combined)).astype(BF)
        grad_ref[b] = grad
        more = nt_dot(grad, part)
        total = more if total is None else total + more
    sum_ref[...] = total
    sum_b_ref[...] = total.astype(BF)


def grad_kernel(
    n_ref, w_ref, res_ref, mine_ref, got_ref, comb_ref, pre_ref, merge_ref, out_ref, rows_ref
):
    w = w_ref[0]
    conv = both_halves(n_ref[0], mine_ref[...].astype(F32), got_ref[...].astype(F32), 1)
    merged_grad = (res_ref[...] + conv).astype(BF)
    for b in range(8):
        cells = nt_dot(merged_grad, merge_ref[256 * b : 256 * b + 256]).astype(BF)
        grad = cells.astype(F32) + comb_ref[b].astype(F32)
        grad = grad * silu_slope(pre_ref[b])
        for z in range(2):
            for h in range(2):
                rows_ref[h, pl.ds(2 * b + z, 16, stride=16), :] = grad[
                    16 * z : 16 * z + 16, 128 * h : 128 * h + 128
                ]
    rows = jnp.concatenate([rows_ref[0], rows_ref[1]], axis=1).astype(BF)
    none = jnp.zeros((32, 256), BF)
    for x in range(8):
        ahead = rows[32 * x + 32 : 32 * x + 64] if x < 7 else none
        behind = rows[32 * x - 32 : 32 * x] if x > 0 else none
        out_ref[x, 0:32] = rows[32 * x : 32 * x + 32]
        out_ref[x, 32:64] = jnp.where(w == 0, ahead, behind)


def swap_narrow(value):
    return lax.ppermute(value, "narrow", [(0, 1), (1, 0)])


def near_kernel(part_ref, *refs, count):
    pair_ref, pair_b_ref = refs[-2:]
    pair = part_ref[...]
    for got_ref in refs[:count]:
        pair += got_ref[...].astype(F32)
    pair_ref[...] = pair
    pair_b_ref[...] = pair.astype(BF)


def features_kernel(n_ref, pair_ref, one_ref, two_ref, three_ref, *refs):
    sum_ref, mine_ref, send_ref = refs[-3:]
    total = pair_ref[...] + one_ref[...].astype(F32) + two_ref[...].astype(F32) + three_ref[...].astype(F32)
    sum_ref[...] = total
    half = total.shape[1] // 2
    low, high = total[:, :half], total[:, half:]
    first = n_ref[0] == 0
    mine_ref[...] = jnp.where(first, low, high).astype(BF)
    send_ref[...] = jnp.where(first, high, low).astype(BF)


def cells_kernel(n_ref, pair_ref, one_ref, two_ref, three_ref, mine_ref, send_ref):
    total = pair_ref[...] + one_ref[...].astype(F32) + two_ref[...].astype(F32) + three_ref[...].astype(F32)
    half = total.shape[0] // 2
    low, high = total[:half], total[half:]
    first = n_ref[0] == 0
    mine_ref[...] = jnp.where(first, low, high)
    send_ref[...] = jnp.where(first, high, low).astype(BF)


def wide_terms(part, part_b, rest=()):
    def partner(value, mask):
        return lax.ppermute(value, "wide", [(i, i ^ mask) for i in range(8)])

    shape = part.shape
    pair, pair_b = kernel_call(
        functools.partial(near_kernel, count=len(NEAR)), (), (part, *[partner(part_b, mask) for mask in NEAR]),
        [shape_of(shape, F32), shape_of(shape, BF)], rest=rest,
    )
    return (pair, *[partner(pair_b, mask) for mask in FAR])


def to_feature_halves(n, part, part_b, rest=()):
    terms = wide_terms(part, part_b, rest)
    cells, features = part.shape
    half_shape = shape_of((cells, features // 2), BF)
    total, mine, send = kernel_call(
        features_kernel, (n,), terms, [shape_of(part.shape, F32), half_shape, half_shape]
    )
    return total, mine, swap_narrow(send)


def to_cell_halves(n, part, part_b):
    terms = wide_terms(part, part_b)
    cells, features = part.shape
    half = (cells // 2, features)
    mine, send = kernel_call(cells_kernel, (n,), terms, [shape_of(half, F32), shape_of(half, BF)])
    return mine, swap_narrow(send)


def across_wide(messages):
    return [messages[0]] + [
        lax.ppermute(messages[mask], "wide", [(i, i ^ mask) for i in range(8)]) for mask in range(1, 8)
    ]


def eight_shards(
    volume,
    cotangent,
    fine_weight,
    merge_weight,
    hidden_weight,
    step_table,
    output_weight,
    expand_weight,
    timestep,
):
    features = merge_weight.shape[1]
    hidden = hidden_weight.shape[2]
    half = features // 2
    w = lax.axis_index("wide").astype(jnp.int32).reshape(1)
    n = lax.axis_index("narrow").astype(jnp.int32).reshape(1)

    fine_cells = pltpu.VMEM((2048, 32), F32)
    fine_field = pltpu.VMEM((8, 16, 16, 32), BF)
    fine_blocks = pltpu.VMEM((8, 32, 256), BF)
    outgoing = kernel_call(
        pack_kernel, (n, w, timestep), (), [shape_of((128, 256), BF)] * 8,
        [fine_field, fine_field, fine_cells, fine_cells, fine_blocks, fine_blocks, pltpu.SemaphoreType.DMA((2,))],
        rest=(volume.transpose(1, 2, 3, 0), cotangent.transpose(1, 2, 3, 0)),
    )
    messages = across_wide(outgoing)
    band, bias = kernel_call(
        band_and_bias_kernel, (timestep,), (fine_weight,),
        [shape_of((1024, 768), BF), shape_of((1, hidden), F32)],
        [pltpu.VMEM((8, hidden), F32), pltpu.SemaphoreType.DMA], cost=BESIDE, rest=(step_table,),
    )
    side_shape = shape_of((256, 256), BF)
    arrived, sides, sent = kernel_call(
        arrived_kernel, (w,), (*messages, band), [shape_of((8, 128, 256), BF), side_shape, side_shape],
        rest=(merge_weight,),
    )
    fine_rows = pltpu.VMEM((2, 256, 128), F32)
    sum_shapes = [shape_of((32, features), F32), shape_of((32, features), BF)]
    pre_act, act, merged_part, merged_part_b = kernel_call(
        merge_kernel,
        (n,),
        (main_call(w, arrived, band, arrived_planes), sides, swap_narrow(sent), band, merge_weight),
        [shape_of((8, 32, 256), F32), shape_of((8, 32, 256), BF)] + sum_shapes,
        [fine_rows],
    )
    (cot,) = kernel_call(cot_kernel, (), (arrived,), [shape_of((8, 32, 256), BF)], [fine_rows])
    merged, mine, got = to_feature_halves(n, merged_part, merged_part_b, (hidden_weight, output_weight))

    gate_shape = shape_of((64, hidden), F32)
    half_shapes = [shape_of((64, half), F32), shape_of((64, half), BF)]
    outer_columns = [pltpu.VMEM((27, 64, half), BF)]
    inner_columns = [pltpu.VMEM((27, 64, hidden), BF)]

    (gate_part,) = kernel_call(
        functools.partial(outer_kernel, back=False, part_of=feature_rows),
        (n,), (mine, got, hidden_weight), [gate_shape], outer_columns,
    )
    gate_pre, branch_part, branch_part_b = kernel_call(
        inner_forward_kernel,
        (n,), (gate_part, swap_narrow(gate_part), bias, output_weight), [gate_shape] + half_shapes, inner_columns,
    )
    mine, got = to_cell_halves(n, branch_part, branch_part_b)
    grad_comb, res_part, res_part_b = kernel_call(
        expand_kernel,
        (n,), (merged, mine, got, act, cot, expand_weight),
        [shape_of((8, 32, 256), BF)] + sum_shapes,
    )
    grad_res, mine, got = to_feature_halves(n, res_part, res_part_b)
    (hidden_part,) = kernel_call(
        functools.partial(outer_kernel, back=True, part_of=feature_columns),
        (n,), (mine, got, output_weight), [gate_shape], outer_columns,
    )
    conv_part, conv_part_b = kernel_call(
        inner_backward_kernel,
        (n,), (hidden_part, swap_narrow(hidden_part), gate_pre, hidden_weight),
        half_shapes, inner_columns,
    )
    mine, got = to_cell_halves(n, conv_part, conv_part_b)
    (leaving,) = kernel_call(
        grad_kernel,
        (n, w), (grad_res, mine, got, grad_comb, pre_act, merge_weight),
        [shape_of((8, 64, 256), BF)], [fine_rows],
    )
    returned = lax.all_to_all(leaving, "wide", split_axis=0, concat_axis=0, tiled=True)
    band = banded(fine_weight, True)
    sides, sent = kernel_call(returned_kernel, (w,), (returned, band), [side_shape, side_shape])
    (result,) = kernel_call(
        final_kernel,
        (n,), (main_call(w, returned, band, returned_planes), sides, swap_narrow(sent), band),
        [shape_of((8, 16, 16, 32), BF)], [fine_cells],
    )
    return result.transpose(3, 0, 1, 2)


def shards(
    volume,
    cotangent,
    fine_weight,
    merge_weight,
    hidden_weight,
    step_table,
    output_weight,
    expand_weight,
    timestep,
):
    channels = volume.shape[0]
    fine_height = volume.shape[2]
    fine_depth = volume.shape[3]
    wide_count = lax.axis_size("wide")
    features = merge_weight.shape[1]
    hidden_local = hidden_weight.shape[2]
    coarse_grid = (wide_count, fine_height // PATCH, fine_depth // PATCH)
    hidden_mat = hidden_weight.transpose(1, 0, 2).reshape(features, 27 * hidden_local)
    output_mat = output_weight.reshape(27 * hidden_local, features)
    output_back = output_weight.transpose(2, 0, 1).reshape(features, 27 * hidden_local)
    hidden_back = hidden_weight.transpose(0, 2, 1).reshape(27 * hidden_local, features)

    def total_rows(partial_value):
        return lax.psum(partial_value, "wide")

    pre_act = fine_conv(volume, fine_weight, False)
    activated = jax.nn.silu(pre_act).astype(jnp.bfloat16)
    received = send_patches(activated)
    merged = total_rows(jnp.dot(received, merge_weight, preferred_element_type=jnp.float32))
    coarse_in = merged.astype(jnp.bfloat16).reshape(coarse_grid + (features,))
    bias_row = step_table[timestep[0]]
    gate_pre = wide_input_conv(coarse_in, hidden_mat, hidden_local, False) + bias_row
    hidden_act = jax.nn.silu(gate_pre).astype(jnp.bfloat16)
    branch = total_rows(narrow_input_conv(hidden_act, output_mat, False).reshape(-1, features))
    residual_sum = (merged + branch).astype(jnp.bfloat16)
    expanded = jnp.dot(residual_sum, expand_weight, preferred_element_type=jnp.float32).astype(
        jnp.bfloat16
    )
    expanded_field = return_patches(expanded, fine_height, fine_depth, channels)
    combined = activated.astype(jnp.float32) + expanded_field.astype(jnp.float32)
    grad_comb = (cotangent.astype(jnp.float32) * silu_slope(combined)).astype(jnp.bfloat16)
    grad_res = total_rows(
        jnp.einsum(
            "nk,dk->nd", send_patches(grad_comb), expand_weight, preferred_element_type=jnp.float32
        )
    )
    grad_res_b = grad_res.astype(jnp.bfloat16).reshape(coarse_grid + (features,))
    grad_hidden = wide_input_conv(grad_res_b, output_back, hidden_local, True)
    grad_gate = (grad_hidden * silu_slope(gate_pre)).astype(jnp.bfloat16)
    grad_conv = total_rows(narrow_input_conv(grad_gate, hidden_back, True).reshape(-1, features))
    grad_merged = (grad_res + grad_conv).astype(jnp.bfloat16)
    grad_cells = jnp.einsum(
        "nd,kd->nk", grad_merged, merge_weight, preferred_element_type=jnp.float32
    ).astype(jnp.bfloat16)
    grad_act = return_patches(grad_cells, fine_height, fine_depth, channels).astype(
        jnp.float32
    ) + grad_comb.astype(jnp.float32)
    grad_pre = (grad_act * silu_slope(pre_act)).astype(jnp.bfloat16)
    return fine_conv(grad_pre, fine_weight.transpose(0, 2, 1), True).astype(jnp.bfloat16)


def solution(mesh):
    in_specs = (
        P(None, ("groups", "wide"), None, "narrow"),
        P(None, ("groups", "wide"), None, "narrow"),
        P(),
        P("wide", None),
        P(None, None, "wide"),
        P(None, "wide"),
        P(None, "wide", None),
        P(None, "wide"),
        P("groups"),
    )
    out_specs = P(None, ("groups", "wide"), None, "narrow")
    sizes = dict(mesh.shape)
    fits = sizes["wide"] == PATCH and sizes["narrow"] == 2
    body = eight_shards if fits else shards
    return jax.shard_map(body, mesh=mesh, in_specs=in_specs, out_specs=out_specs, check_vma=False)
```

```python
import functools

import jax
import jax.numpy as jnp
from jax import lax
from jax.experimental import pallas as pl
from jax.experimental.pallas import tpu as pltpu
from jax.sharding import PartitionSpec as P

PATCH = 8


def extended(cells, sides, width):
    for axis, dim in sides:
        count = lax.axis_size(axis)
        ends = count - 1
        head = lax.slice_in_dim(cells, 0, width, axis=dim)
        tail = lax.slice_in_dim(cells, cells.shape[dim] - width, cells.shape[dim], axis=dim)
        cells = jnp.concatenate(
            [
                lax.ppermute(tail, axis, [(i, (i + 1) % count) for i in range(ends)]),
                cells,
                lax.ppermute(head, axis, [((i + 1) % count, i) for i in range(ends)]),
            ],
            axis=dim,
        )
    return cells


def shifts(transposed):
    return [
        (2 - i, 2 - j, 2 - k) if transposed else (i, j, k)
        for i in range(3)
        for j in range(3)
        for k in range(3)
    ]


def silu_slope(values):
    logistic = jax.nn.sigmoid(values)
    return logistic * (1.0 + values * (1.0 - logistic))


def fine_conv(fine_field, weight, transposed):
    grown = extended(fine_field, (("wide", 1), ("narrow", 3)), 1)
    padded = jnp.pad(grown, ((0, 0), (0, 0), (1, 1), (0, 0)))
    kernel = weight.reshape(3, 3, 3, weight.shape[1], weight.shape[2])
    if transposed:
        kernel = kernel[::-1, ::-1, ::-1]
    result = lax.conv_general_dilated(
        padded[None],
        kernel,
        (1, 1, 1),
        "VALID",
        dimension_numbers=("NCDHW", "DHWIO", "NCDHW"),
        preferred_element_type=jnp.float32,
    )
    return result[0]


def to_patches(fine_field):
    channels = fine_field.shape[0]
    shaped = fine_field.reshape(
        channels, PATCH, fine_field.shape[2] // PATCH, PATCH, fine_field.shape[3] // PATCH, PATCH
    )
    return shaped.transpose(2, 4, 1, 3, 5, 0).reshape(-1, PATCH**3 * channels)


def send_patches(fine_field):
    return lax.all_to_all(to_patches(fine_field), "wide", split_axis=1, concat_axis=0, tiled=True)


def return_patches(patch_rows, fine_height, fine_depth, channels):
    returned = lax.all_to_all(patch_rows, "wide", split_axis=0, concat_axis=1, tiled=True)
    shaped = returned.reshape(
        fine_height // PATCH, fine_depth // PATCH, PATCH, PATCH, PATCH, channels
    )
    return shaped.transpose(5, 2, 0, 3, 1, 4).reshape(channels, PATCH, fine_height, fine_depth)


def coarse_faces(coarse_block):
    return extended(coarse_block, (("narrow", 2),), 1)


def wide_input_conv(coarse_block, weight_mat, out_count, transposed):
    grown = coarse_faces(coarse_block)
    products = jnp.einsum("xyzd,dk->xyzk", grown, weight_mat, preferred_element_type=jnp.float32)
    padded = jnp.pad(products, ((1, 1), (1, 1), (0, 0), (0, 0)))
    extent = coarse_block.shape[:3]
    summed = jnp.zeros(extent + (out_count,), jnp.float32)
    for tap_index, (a, b, c) in enumerate(shifts(transposed)):
        summed = (
            summed
            + padded[
                a : a + extent[0],
                b : b + extent[1],
                c : c + extent[2],
                tap_index * out_count : (tap_index + 1) * out_count,
            ]
        )
    return summed


def narrow_input_conv(coarse_block, weight_mat, transposed):
    grown = coarse_faces(coarse_block)
    padded = jnp.pad(grown, ((1, 1), (1, 1), (0, 0), (0, 0)))
    extent = coarse_block.shape[:3]
    columns = jnp.concatenate(
        [
            padded[a : a + extent[0], b : b + extent[1], c : c + extent[2]]
            for a, b, c in shifts(transposed)
        ],
        axis=3,
    )
    return jnp.einsum("xyzk,kd->xyzd", columns, weight_mat, preferred_element_type=jnp.float32)


BF = jnp.bfloat16
F32 = jnp.float32
LIMIT = 10 * 1024 * 1024
BESIDE = 32 * 1024 * 1024
NEAR, FAR = (1,), (6, 2, 4)
VMEM = pl.BlockSpec(memory_space=pltpu.VMEM)
SMEM = pl.BlockSpec(memory_space=pltpu.SMEM)


def nn_dot(lhs, rhs):
    return jnp.dot(lhs, rhs, preferred_element_type=F32)


def nt_dot(lhs, rhs):
    return lax.dot_general(lhs, rhs, (((1,), (1,)), ((), ())), preferred_element_type=F32)


def shape_of(dims, dtype):
    return jax.ShapeDtypeStruct(dims, dtype)


def kernel_call(kernel, places, arrays, outs, scratch=(), cost=None, rest=()):
    return pl.pallas_call(
        kernel,
        in_specs=[SMEM] * len(places) + [VMEM] * len(arrays) + [pl.BlockSpec(memory_space=pl.ANY)] * len(rest),
        out_specs=[VMEM] * len(outs),
        out_shape=outs,
        scratch_shapes=list(scratch),
        cost_estimate=cost and pl.CostEstimate(flops=0, bytes_accessed=cost, transcendentals=0),
        compiler_params=pltpu.CompilerParams(vmem_limit_bytes=LIMIT),
    )(*places, *arrays, *[pltpu.with_memory_space_constraint(a, pltpu.HBM) for a in rest])


def band_kernel(weight_ref, out_ref, *, back):
    row = lax.broadcasted_iota(jnp.int32, (32, 256), 0)
    lane = lax.broadcasted_iota(jnp.int32, (32, 256), 1)
    places = [(lane == row + 32 * (2 - k)).astype(BF) for k in range(3)]
    same = (
        lax.broadcasted_iota(jnp.int32, (32, 32), 0) == lax.broadcasted_iota(jnp.int32, (32, 32), 1)
    ).astype(BF)
    for i in range(3):
        for j in range(3):
            taps = None
            for k in range(3):
                t = 9 * i + 3 * j + k
                tap = nt_dot(same, weight_ref[26 - t]).astype(BF) if back else weight_ref[t]
                part = nn_dot(tap, places[k])
                taps = part if taps is None else taps + part
            columns = slice(256 * j, 256 * j + 256)

            def placed(start):
                moved = pltpu.roll(taps, start % 256, 1)
                return jnp.where((lane >= start) & (lane < start + 96), moved, 0.0).astype(BF)

            for d in range(8):
                out_ref[256 * i + 32 * d : 256 * i + 32 * d + 32, columns] = placed(32 * (d - 1))
            out_ref[768 + 64 * i : 800 + 64 * i, columns] = placed(-64)
            out_ref[800 + 64 * i : 832 + 64 * i, columns] = placed(224)
    out_ref[960:1024, :] = jnp.zeros((64, 768), BF)


def band_and_bias_kernel(step_ref, weight_ref, table_ref, out_ref, bias_ref, rows_ref, sem):
    step = step_ref[0]
    group = pl.ds(pl.multiple_of(step // 8 * 8, 8), 8)
    fetch = pltpu.make_async_copy(table_ref.at[group], rows_ref, sem)
    fetch.start()
    band_kernel(weight_ref, out_ref, back=False)
    fetch.wait()
    rows = rows_ref[...]
    chosen = lax.broadcasted_iota(jnp.int32, rows.shape, 0) == step % 8
    bias_ref[...] = jnp.sum(jnp.where(chosen, rows, jnp.zeros_like(rows)), axis=0, keepdims=True)


def banded(weight, back):
    (out,) = kernel_call(
        functools.partial(band_kernel, back=back), (), (weight,), [shape_of((1024, 768), BF)], cost=BESIDE
    )
    return out


def lane_place(d):
    row = lax.broadcasted_iota(jnp.int32, (32, 256), 0)
    lane = lax.broadcasted_iota(jnp.int32, (32, 256), 1)
    return (lane == row + 32 * d).astype(BF)


def to_rows(field_ref, cells_ref):
    cells_ref[...] = field_ref[...].astype(F32).reshape(2048, 32)
    rows = None
    for d in range(8):
        part = nn_dot(cells_ref[pl.ds(d, 256, stride=8), :].astype(BF), lane_place(d))
        rows = part if rows is None else rows + part
    return rows.astype(BF).reshape(8, 32, 256)


def pack_kernel(n_ref, w_ref, step_ref, volume_ref, cotangent_ref, *refs):
    del n_ref, step_ref
    out_refs = refs[:8]
    volume_copy_ref, cotangent_copy_ref, cells_ref, other_ref, field_ref, cot_ref, sems = refs[8:]
    first = pltpu.make_async_copy(volume_ref, volume_copy_ref, sems.at[0])
    second = pltpu.make_async_copy(cotangent_ref, cotangent_copy_ref, sems.at[1])
    first.start()
    second.start()
    first.wait()
    field_ref[...] = to_rows(volume_copy_ref, cells_ref)
    second.wait()
    cot_ref[...] = to_rows(cotangent_copy_ref, other_ref)
    for mask, out_ref in enumerate(out_refs):
        a = w_ref[0] ^ mask
        out_ref[0:32] = field_ref[(a + 7) & 7]
        out_ref[32:64] = field_ref[a]
        out_ref[64:96] = field_ref[(a + 1) & 7]
        out_ref[96:128] = cot_ref[a]


def arrived_planes(w, arrived_ref):
    none = jnp.zeros((32, 256), BF)
    before, own, after = [
        arrived_ref[:, 32 * s : 32 * s + 32, :].reshape(256, 256) for s in range(3)
    ]
    before = jnp.where(w == 0, jnp.concatenate([none, before[:224]], axis=0), before)
    after = jnp.where(w == 7, jnp.concatenate([after[32:], none], axis=0), after)
    return before, own, after


def returned_planes(w, returned_ref):
    rows = [returned_ref[7, 32:64]] + [returned_ref[a, 0:32] for a in range(8)] + [returned_ref[0, 32:64]]
    grown = jnp.concatenate(rows, axis=0)
    return grown[0:256], grown[32:288], grown[64:320]


def arrived_kernel(w_ref, *refs):
    planes_ref, own_ref, send_ref = refs[-3:]
    for mask in range(8):
        planes_ref[w_ref[0] ^ mask] = refs[mask][...]
    put_sides(arrived_planes(w_ref[0], planes_ref), own_ref, send_ref)


def returned_kernel(w_ref, planes_ref, band_ref, own_ref, send_ref):
    del band_ref
    put_sides(returned_planes(w_ref[0], planes_ref), own_ref, send_ref)


def put_sides(planes, own_ref, send_ref):
    source = lax.broadcasted_iota(jnp.int32, (256, 256), 0)
    target = lax.broadcasted_iota(jnp.int32, (256, 256), 1)
    sides = None
    for i, plane in enumerate(planes):
        high = (source >= 224) & (target == source - 224 + 64 * i)
        low = (source < 32) & (target == source + 64 * i + 32)
        part = nn_dot(plane, (high | low).astype(BF))
        sides = part if sides is None else sides + part
    even = (source & 1) == 0
    sides = jnp.where(even, pltpu.roll(sides, 255, 0), pltpu.roll(sides, 1, 0))
    low_side = (target & 32) != 0
    own = even == low_side
    zero = jnp.zeros_like(sides)
    own_ref[...] = jnp.where(own, sides, zero).astype(BF)
    send_ref[...] = jnp.where(own, zero, sides).astype(BF)


def main_kernel(w_ref, planes_ref, band_ref, out_ref, *, planes_of):
    lhs = jnp.concatenate(planes_of(w_ref[0], planes_ref), axis=1)
    out_ref[...] = nn_dot(lhs, band_ref[0:768])


def main_call(w, planes, band, planes_of):
    (out,) = kernel_call(
        functools.partial(main_kernel, planes_of=planes_of), (w,), (planes, band), [shape_of((256, 768), F32)]
    )
    return out


def fine_sum(n, main_ref, own_ref, got_ref, band_ref):
    lane = lax.broadcasted_iota(jnp.int32, (256, 256), 1)
    keep = ((lane & 32) != 0) == (n == 0)
    got = jnp.where(keep, got_ref[...].astype(F32), jnp.zeros((256, 256), F32))
    sides = (own_ref[...].astype(F32) + got).astype(BF)
    shifts_y = main_ref[...] + nn_dot(sides, band_ref[768:1024])
    y = (lax.broadcasted_iota(jnp.int32, (256, 1), 0) >> 1) & 15
    total = shifts_y[:, 256:512]
    zero = jnp.zeros_like(total)
    below = pltpu.roll(shifts_y[:, 0:256], 2, 0)
    above = pltpu.roll(shifts_y[:, 512:768], 254, 0)
    return total + jnp.where(y > 0, below, zero) + jnp.where(y < 15, above, zero)


def cell_rows(ref, b):
    return jnp.concatenate([ref[pl.ds(2 * b + z, 16, stride=16), :] for z in range(2)], axis=0)


def merge_kernel(
    n_ref, main_ref, own_ref, got_ref, band_ref, merge_ref, pre_ref, act_ref, sum_ref, sum_b_ref, rows_ref
):
    wide_rows = fine_sum(n_ref[0], main_ref, own_ref, got_ref, band_ref)
    rows_ref[0] = wide_rows[:, :128]
    rows_ref[1] = wide_rows[:, 128:]
    total = None
    for b in range(8):
        pre = jnp.concatenate([cell_rows(rows_ref.at[h], b) for h in range(2)], axis=1)
        pre_ref[b] = pre
        act = (pre * jax.nn.sigmoid(pre)).astype(BF)
        act_ref[b] = act
        part = nn_dot(act, merge_ref[256 * b : 256 * b + 256])
        total = part if total is None else total + part
    sum_ref[...] = total
    sum_b_ref[...] = total.astype(BF)


def cot_kernel(planes_ref, cot_ref, rows_ref):
    rows = planes_ref[:, 96:128, :].reshape(256, 256).astype(F32)
    rows_ref[0] = rows[:, :128]
    rows_ref[1] = rows[:, 128:]
    for b in range(8):
        cot_ref[b] = jnp.concatenate([cell_rows(rows_ref.at[h], b) for h in range(2)], axis=1).astype(BF)


def final_kernel(n_ref, main_ref, own_ref, got_ref, band_ref, out_ref, cells_ref):
    rows = fine_sum(n_ref[0], main_ref, own_ref, got_ref, band_ref).astype(BF)
    for d in range(8):
        cells_ref[pl.ds(d, 256, stride=8), :] = nt_dot(rows, lane_place(d))
    out_ref[...] = cells_ref[...].astype(BF).reshape(8, 16, 16, 32)


def put_columns(cols_ref, cells):
    row = lax.broadcasted_iota(jnp.int32, (64, 1), 0)
    along_y, along_x = row & 1, (row >> 1) & 7
    zero = jnp.zeros_like(cells)
    none = jnp.zeros((16, cells.shape[1]), BF)
    below = jnp.where(along_y == 1, pltpu.roll(cells, 1, 0), zero)
    above = jnp.where(along_y == 0, pltpu.roll(cells, 63, 0), zero)
    for j, moved_y in enumerate((below, cells, above)):
        before = jnp.where(along_x > 0, pltpu.roll(moved_y, 2, 0), zero)
        after = jnp.where(along_x < 7, pltpu.roll(moved_y, 62, 0), zero)
        for i, moved in enumerate((before, moved_y, after)):
            rows = moved.astype(BF)
            cols_ref[9 * i + 3 * j] = jnp.concatenate([none, rows[:48]], axis=0)
            cols_ref[9 * i + 3 * j + 1] = rows
            cols_ref[9 * i + 3 * j + 2] = jnp.concatenate([rows[16:], none], axis=0)


def both_halves(n, mine, got, axis):
    first = n == 0
    return jnp.concatenate([jnp.where(first, mine, got), jnp.where(first, got, mine)], axis=axis)


def conv_sum(cols_ref, weight_of, back):
    total = None
    for t in range(27):
        cells = cols_ref[26 - t if back else t]
        part = nt_dot(weight_of(t), cells) if back else nn_dot(cells, weight_of(t))
        total = part if total is None else total + part
    return total.T if back else total


def feature_rows(n, ref):
    half = ref.shape[1] // 2
    return lambda t: ref[t, pl.ds(pl.multiple_of(n * half, half), half), :]


def feature_columns(n, ref):
    half = ref.shape[2] // 2
    return lambda t: ref[t, :, pl.ds(pl.multiple_of(n * half, half), half)]


def outer_kernel(n_ref, mine_ref, got_ref, weight_ref, sum_ref, sum_b_ref, cols_ref, *, back, part_of):
    n = n_ref[0]
    put_columns(cols_ref, both_halves(n, mine_ref[...].astype(F32), got_ref[...].astype(F32), 0))
    total = conv_sum(cols_ref, part_of(n, weight_ref), back)
    sum_ref[...] = total
    sum_b_ref[...] = total.astype(BF)


def inner_forward_kernel(
    n_ref, mine_ref, got_ref, bias_ref, weight_ref, gate_ref, sum_ref, sum_b_ref, cols_ref
):
    gate = mine_ref[...] + got_ref[...].astype(F32) + bias_ref[...]
    gate_ref[...] = gate
    put_columns(cols_ref, gate * jax.nn.sigmoid(gate))
    total = conv_sum(cols_ref, feature_columns(n_ref[0], weight_ref), False)
    sum_ref[...] = total
    sum_b_ref[...] = total.astype(BF)


def inner_backward_kernel(
    n_ref, mine_ref, got_ref, gate_ref, weight_ref, sum_ref, sum_b_ref, cols_ref
):
    put_columns(cols_ref, (mine_ref[...] + got_ref[...].astype(F32)) * silu_slope(gate_ref[...]))
    total = conv_sum(cols_ref, feature_rows(n_ref[0], weight_ref), True)
    sum_ref[...] = total
    sum_b_ref[...] = total.astype(BF)


def expand_kernel(
    n_ref, merged_ref, mine_ref, got_ref, act_ref, cot_ref, expand_ref, grad_ref, sum_ref, sum_b_ref
):
    branch = both_halves(n_ref[0], mine_ref[...].astype(F32), got_ref[...].astype(F32), 1)
    residual = (merged_ref[...] + branch).astype(BF)
    total = None
    for b in range(8):
        part = expand_ref[:, 256 * b : 256 * b + 256]
        expanded = nn_dot(residual, part).astype(BF)
        combined = act_ref[b].astype(F32) + expanded.astype(F32)
        grad = (cot_ref[b].astype(F32) * silu_slope(combined)).astype(BF)
        grad_ref[b] = grad
        more = nt_dot(grad, part)
        total = more if total is None else total + more
    sum_ref[...] = total
    sum_b_ref[...] = total.astype(BF)


def grad_kernel(
    n_ref, w_ref, res_ref, mine_ref, got_ref, comb_ref, pre_ref, merge_ref, out_ref, rows_ref
):
    w = w_ref[0]
    conv = both_halves(n_ref[0], mine_ref[...].astype(F32), got_ref[...].astype(F32), 1)
    merged_grad = (res_ref[...] + conv).astype(BF)
    for b in range(8):
        cells = nt_dot(merged_grad, merge_ref[256 * b : 256 * b + 256]).astype(BF)
        grad = cells.astype(F32) + comb_ref[b].astype(F32)
        grad = grad * silu_slope(pre_ref[b])
        for z in range(2):
            for h in range(2):
                rows_ref[h, pl.ds(2 * b + z, 16, stride=16), :] = grad[
                    16 * z : 16 * z + 16, 128 * h : 128 * h + 128
                ]
    rows = jnp.concatenate([rows_ref[0], rows_ref[1]], axis=1).astype(BF)
    none = jnp.zeros((32, 256), BF)
    for x in range(8):
        ahead = rows[32 * x + 32 : 32 * x + 64] if x < 7 else none
        behind = rows[32 * x - 32 : 32 * x] if x > 0 else none
        out_ref[x, 0:32] = rows[32 * x : 32 * x + 32]
        out_ref[x, 32:64] = jnp.where(w == 0, ahead, behind)


def swap_narrow(value):
    return lax.ppermute(value, "narrow", [(0, 1), (1, 0)])


def near_kernel(part_ref, *refs, count):
    pair_ref, pair_b_ref = refs[-2:]
    pair = part_ref[...]
    for got_ref in refs[:count]:
        pair += got_ref[...].astype(F32)
    pair_ref[...] = pair
    pair_b_ref[...] = pair.astype(BF)


def features_kernel(n_ref, pair_ref, one_ref, two_ref, three_ref, *refs):
    sum_ref, mine_ref, send_ref = refs[-3:]
    total = pair_ref[...] + one_ref[...].astype(F32) + two_ref[...].astype(F32) + three_ref[...].astype(F32)
    sum_ref[...] = total
    half = total.shape[1] // 2
    low, high = total[:, :half], total[:, half:]
    first = n_ref[0] == 0
    mine_ref[...] = jnp.where(first, low, high).astype(BF)
    send_ref[...] = jnp.where(first, high, low).astype(BF)


def cells_kernel(n_ref, pair_ref, one_ref, two_ref, three_ref, mine_ref, send_ref):
    total = pair_ref[...] + one_ref[...].astype(F32) + two_ref[...].astype(F32) + three_ref[...].astype(F32)
    half = total.shape[0] // 2
    low, high = total[:half], total[half:]
    first = n_ref[0] == 0
    mine_ref[...] = jnp.where(first, low, high)
    send_ref[...] = jnp.where(first, high, low).astype(BF)


def wide_terms(part, part_b, rest=()):
    def partner(value, mask):
        return lax.ppermute(value, "wide", [(i, i ^ mask) for i in range(8)])

    shape = part.shape
    pair, pair_b = kernel_call(
        functools.partial(near_kernel, count=len(NEAR)), (), (part, *[partner(part_b, mask) for mask in NEAR]),
        [shape_of(shape, F32), shape_of(shape, BF)], rest=rest,
    )
    return (pair, *[partner(pair_b, mask) for mask in FAR])


def to_feature_halves(n, part, part_b, rest=()):
    terms = wide_terms(part, part_b, rest)
    cells, features = part.shape
    half_shape = shape_of((cells, features // 2), BF)
    total, mine, send = kernel_call(
        features_kernel, (n,), terms, [shape_of(part.shape, F32), half_shape, half_shape]
    )
    return total, mine, swap_narrow(send)


def to_cell_halves(n, part, part_b):
    terms = wide_terms(part, part_b)
    cells, features = part.shape
    half = (cells // 2, features)
    mine, send = kernel_call(cells_kernel, (n,), terms, [shape_of(half, F32), shape_of(half, BF)])
    return mine, swap_narrow(send)


def across_wide(messages):
    return [messages[0]] + [
        lax.ppermute(messages[mask], "wide", [(i, i ^ mask) for i in range(8)]) for mask in range(1, 8)
    ]


def eight_shards(
    volume,
    cotangent,
    fine_weight,
    merge_weight,
    hidden_weight,
    step_table,
    output_weight,
    expand_weight,
    timestep,
):
    features = merge_weight.shape[1]
    hidden = hidden_weight.shape[2]
    half = features // 2
    w = lax.axis_index("wide").astype(jnp.int32).reshape(1)
    n = lax.axis_index("narrow").astype(jnp.int32).reshape(1)

    fine_cells = pltpu.VMEM((2048, 32), F32)
    fine_field = pltpu.VMEM((8, 16, 16, 32), BF)
    fine_blocks = pltpu.VMEM((8, 32, 256), BF)
    outgoing = kernel_call(
        pack_kernel, (n, w, timestep), (), [shape_of((128, 256), BF)] * 8,
        [fine_field, fine_field, fine_cells, fine_cells, fine_blocks, fine_blocks, pltpu.SemaphoreType.DMA((2,))],
        rest=(volume.transpose(1, 2, 3, 0), cotangent.transpose(1, 2, 3, 0)),
    )
    messages = across_wide(outgoing)
    band, bias = kernel_call(
        band_and_bias_kernel, (timestep,), (fine_weight,),
        [shape_of((1024, 768), BF), shape_of((1, hidden), F32)],
        [pltpu.VMEM((8, hidden), F32), pltpu.SemaphoreType.DMA], cost=BESIDE, rest=(step_table,),
    )
    side_shape = shape_of((256, 256), BF)
    arrived, sides, sent = kernel_call(
        arrived_kernel, (w,), (*messages, band), [shape_of((8, 128, 256), BF), side_shape, side_shape],
        rest=(merge_weight, hidden_weight, output_weight),
    )
    fine_rows = pltpu.VMEM((2, 256, 128), F32)
    sum_shapes = [shape_of((32, features), F32), shape_of((32, features), BF)]
    pre_act, act, merged_part, merged_part_b = kernel_call(
        merge_kernel,
        (n,),
        (main_call(w, arrived, band, arrived_planes), sides, swap_narrow(sent), band, merge_weight),
        [shape_of((8, 32, 256), F32), shape_of((8, 32, 256), BF)] + sum_shapes,
        [fine_rows],
    )
    (cot,) = kernel_call(cot_kernel, (), (arrived,), [shape_of((8, 32, 256), BF)], [fine_rows])
    merged, mine, got = to_feature_halves(n, merged_part, merged_part_b, (hidden_weight, output_weight))

    gate_shape = shape_of((64, hidden), F32)
    half_shapes = [shape_of((64, half), F32), shape_of((64, half), BF)]
    outer_columns = [pltpu.VMEM((27, 64, half), BF)]
    inner_columns = [pltpu.VMEM((27, 64, hidden), BF)]

    gate_part, gate_part_b = kernel_call(
        functools.partial(outer_kernel, back=False, part_of=feature_rows),
        (n,), (mine, got, hidden_weight), [gate_shape, shape_of((64, hidden), BF)], outer_columns,
    )
    gate_pre, branch_part, branch_part_b = kernel_call(
        inner_forward_kernel,
        (n,), (gate_part, swap_narrow(gate_part_b), bias, output_weight), [gate_shape] + half_shapes, inner_columns,
    )
    mine, got = to_cell_halves(n, branch_part, branch_part_b)
    grad_comb, res_part, res_part_b = kernel_call(
        expand_kernel,
        (n,), (merged, mine, got, act, cot, expand_weight),
        [shape_of((8, 32, 256), BF)] + sum_shapes,
    )
    grad_res, mine, got = to_feature_halves(n, res_part, res_part_b)
    hidden_part, hidden_part_b = kernel_call(
        functools.partial(outer_kernel, back=True, part_of=feature_columns),
        (n,), (mine, got, output_weight), [gate_shape, shape_of((64, hidden), BF)], outer_columns,
    )
    conv_part, conv_part_b = kernel_call(
        inner_backward_kernel,
        (n,), (hidden_part, swap_narrow(hidden_part_b), gate_pre, hidden_weight),
        half_shapes, inner_columns,
    )
    mine, got = to_cell_halves(n, conv_part, conv_part_b)
    (leaving,) = kernel_call(
        grad_kernel,
        (n, w), (grad_res, mine, got, grad_comb, pre_act, merge_weight),
        [shape_of((8, 64, 256), BF)], [fine_rows],
    )
    returned = lax.all_to_all(leaving, "wide", split_axis=0, concat_axis=0, tiled=True)
    band = banded(fine_weight, True)
    sides, sent = kernel_call(returned_kernel, (w,), (returned, band), [side_shape, side_shape])
    (result,) = kernel_call(
        final_kernel,
        (n,), (main_call(w, returned, band, returned_planes), sides, swap_narrow(sent), band),
        [shape_of((8, 16, 16, 32), BF)], [fine_cells],
    )
    return result.transpose(3, 0, 1, 2)


def shards(
    volume,
    cotangent,
    fine_weight,
    merge_weight,
    hidden_weight,
    step_table,
    output_weight,
    expand_weight,
    timestep,
):
    channels = volume.shape[0]
    fine_height = volume.shape[2]
    fine_depth = volume.shape[3]
    wide_count = lax.axis_size("wide")
    features = merge_weight.shape[1]
    hidden_local = hidden_weight.shape[2]
    coarse_grid = (wide_count, fine_height // PATCH, fine_depth // PATCH)
    hidden_mat = hidden_weight.transpose(1, 0, 2).reshape(features, 27 * hidden_local)
    output_mat = output_weight.reshape(27 * hidden_local, features)
    output_back = output_weight.transpose(2, 0, 1).reshape(features, 27 * hidden_local)
    hidden_back = hidden_weight.transpose(0, 2, 1).reshape(27 * hidden_local, features)

    def total_rows(partial_value):
        return lax.psum(partial_value, "wide")

    pre_act = fine_conv(volume, fine_weight, False)
    activated = jax.nn.silu(pre_act).astype(jnp.bfloat16)
    received = send_patches(activated)
    merged = total_rows(jnp.dot(received, merge_weight, preferred_element_type=jnp.float32))
    coarse_in = merged.astype(jnp.bfloat16).reshape(coarse_grid + (features,))
    bias_row = step_table[timestep[0]]
    gate_pre = wide_input_conv(coarse_in, hidden_mat, hidden_local, False) + bias_row
    hidden_act = jax.nn.silu(gate_pre).astype(jnp.bfloat16)
    branch = total_rows(narrow_input_conv(hidden_act, output_mat, False).reshape(-1, features))
    residual_sum = (merged + branch).astype(jnp.bfloat16)
    expanded = jnp.dot(residual_sum, expand_weight, preferred_element_type=jnp.float32).astype(
        jnp.bfloat16
    )
    expanded_field = return_patches(expanded, fine_height, fine_depth, channels)
    combined = activated.astype(jnp.float32) + expanded_field.astype(jnp.float32)
    grad_comb = (cotangent.astype(jnp.float32) * silu_slope(combined)).astype(jnp.bfloat16)
    grad_res = total_rows(
        jnp.einsum(
            "nk,dk->nd", send_patches(grad_comb), expand_weight, preferred_element_type=jnp.float32
        )
    )
    grad_res_b = grad_res.astype(jnp.bfloat16).reshape(coarse_grid + (features,))
    grad_hidden = wide_input_conv(grad_res_b, output_back, hidden_local, True)
    grad_gate = (grad_hidden * silu_slope(gate_pre)).astype(jnp.bfloat16)
    grad_conv = total_rows(narrow_input_conv(grad_gate, hidden_back, True).reshape(-1, features))
    grad_merged = (grad_res + grad_conv).astype(jnp.bfloat16)
    grad_cells = jnp.einsum(
        "nd,kd->nk", grad_merged, merge_weight, preferred_element_type=jnp.float32
    ).astype(jnp.bfloat16)
    grad_act = return_patches(grad_cells, fine_height, fine_depth, channels).astype(
        jnp.float32
    ) + grad_comb.astype(jnp.float32)
    grad_pre = (grad_act * silu_slope(pre_act)).astype(jnp.bfloat16)
    return fine_conv(grad_pre, fine_weight.transpose(0, 2, 1), True).astype(jnp.bfloat16)


def solution(mesh):
    in_specs = (
        P(None, ("groups", "wide"), None, "narrow"),
        P(None, ("groups", "wide"), None, "narrow"),
        P(),
        P("wide", None),
        P(None, None, "wide"),
        P(None, "wide"),
        P(None, "wide", None),
        P(None, "wide"),
        P("groups"),
    )
    out_specs = P(None, ("groups", "wide"), None, "narrow")
    sizes = dict(mesh.shape)
    fits = sizes["wide"] == PATCH and sizes["narrow"] == 2
    body = eight_shards if fits else shards
    return jax.shard_map(body, mesh=mesh, in_specs=in_specs, out_specs=out_specs, check_vma=False)
```
